512 devices in a mesh: dom: 128 (over y, z, core), cell: 4 (over x).
Axes of the slice: x: 4, y: 4, z: 16, core: 2. Of those that a mesh axis runs over, the one named last changes fastest.
Arguments:
- potential: float32 [64, 131072], P(None, ('dom', 'cell')), may hold values from -6 to 6
- types: int32 [131072, 1], P(('dom', 'cell')), may hold values from 0 to 127; in each aligned block of 256 rows (0 to 255, 256 to 511, ...) at most 4 rows name the same one
- saturation: int32 [131072], P(('dom', 'cell')), may hold values from 0 to 3
- pattern: int32 [131072], P(('dom', 'cell')), may hold values from 0 to 127
- inverses: bfloat16 [128, 4, 64, 64], P('dom'), may hold values from -1 to 1, as said below
- coupling: bfloat16 [128, 64, 64], P('dom'), may hold values from -0.75 to 0.75
- skin: float32 [8], replicated, may hold values from 0.25 to 1.75
Outputs:
- new_potential: float32 [64, 131072], P(None, ('dom', 'cell'))
The draws below stay inside these ranges and needn't reach their ends.
Inputs may be any that keep to these rules, and one draw needn't show every extreme that they name: `types`: among the 256 points of one device no type is named more than 4 times. `inverses`: entries of the inverse blocks are bounded by 1.
All inputs are finite; a program needn't handle non-finite values.
Results may differ from the reference program's by a relative error of at most 0.0051.
Values may be sent and summed in bfloat16 or wider, within the bound.
A program may use at most 64 MiB of HBM per device.

```python
import math
import jax
import jax.numpy as jnp
import numpy as np
from jax import lax

D = 64
LAM = 8
NSAT = 4
ITERS = 3
P_DEV = 256
CAP = 4
TYPES = 128
ROWS = 131072


def draw_inverses(key, part):
    key = jax.random.fold_in(key, 7)
    key_diag, key_off = jax.random.split(key)
    diag = jnp.exp(jax.random.uniform(key_diag, (TYPES, NSAT, D), jnp.float32, jnp.log(0.25), jnp.log(0.6)))
    off = jax.random.normal(key_off, (TYPES, NSAT, D, D), jnp.float32) * (0.3 / D ** 0.5)
    eye = jnp.eye(D, dtype=jnp.float32)
    full = off * (1.0 - eye) + diag[..., None] * eye
    return jnp.clip(full, -1.0, 1.0).astype(jnp.bfloat16)


def with_ends(drawn, stream_key, low, top_value):
    dims = drawn.shape
    index_at = [jax.random.randint(jax.random.fold_in(stream_key, axis), (), 0, dims[axis]) for axis in range(len(dims))]
    drawn = drawn.at[tuple(index_at)].set(low)
    longest = dims.index(max(dims))
    index_at[longest] = (index_at[longest] + 1) % dims[longest]
    return drawn.at[tuple(index_at)].set(top_value)


def block_levels(own_key, dims, pieces, least, largest):
    gain = 1.0
    for axis_at, blocks in pieces:
        steps = jax.random.uniform(jax.random.fold_in(jax.random.fold_in(own_key, 6), axis_at), (blocks,), jnp.float32, least / len(pieces), largest / len(pieces))
        gain = gain * jnp.repeat(jnp.exp(steps), dims[axis_at] // blocks).reshape((-1,) + (1,) * (len(dims) - 1 - axis_at))
    return gain


def shared_out(rng, own, number, rows, number_of, top, most, skew):
    sequence = jax.random.permutation(rng, number_of)
    crowded, ordinary = shares(number_of, rows * top, most, skew, True), shares(number_of, rows * top, most, skew, False)
    places = jnp.arange(number_of)

    def named(sizes, offset_by):
        used = int((sizes > 0).sum())
        fixed = max(1, used // 4)
        passed = fixed + (places - fixed + offset_by * (used - fixed)) % max(1, number_of - fixed)
        return jnp.zeros((number_of,), jnp.int32).at[sequence[jnp.where(places < fixed, places, passed)]].set(jnp.asarray(sizes, jnp.int32))

    sizes = jnp.where(number % 4 == 0, named(crowded, number // 4), named(ordinary, number - number // 4 - 1))
    mixed = jax.random.permutation(jax.random.fold_in(own, 3), number_of)
    source_of, sink = mixed[0:number_of // 2 * 2:2], mixed[1:number_of // 2 * 2:2]
    slack = jnp.minimum(sizes[source_of] - 1, most - sizes[sink]) // 2
    slack = jnp.where((source_of == sequence[0]) | (sink == sequence[0]) | (sizes[sink] == 0), 0, jnp.maximum(slack, 0))
    passed = jax.random.randint(jax.random.fold_in(own, 4), (number_of // 2,), 0, 1 << 20) % (slack + 1)
    sizes = sizes.at[source_of].add(-passed).at[sink].add(passed)
    labels = jnp.searchsorted(jnp.cumsum(sizes), jnp.arange(rows * top), side="right").astype(jnp.int32)
    table = labels.reshape(top, rows).T
    table = table[jax.random.permutation(jax.random.fold_in(own, 1), rows)]
    offset_by = jax.random.randint(jax.random.fold_in(own, 2), (rows, 1), 0, top)
    return jnp.take_along_axis(table, (jnp.arange(top)[None, :] + offset_by) % top, axis=1)


def shares(number_of, total, reach, skew, full):
    loads = [(1 << 20) // math.isqrt(grade ** skew) + 1 for grade in range(1, number_of + 1)]
    largest = reach if full else min(reach, max(-(-total // number_of), total * loads[0] // sum(loads)))
    least = 1 if total - largest >= number_of - 1 else 0
    given, spare = [largest] + [least] * (number_of - 1), total - largest - least * (number_of - 1)
    while spare > 0:
        movable = [i for i in range(1, number_of) if given[i] < largest] or [i for i in range(1, number_of) if given[i] < reach]
        mass, left = sum([loads[i] for i in movable]), spare
        for i in movable:
            extra = min(reach - given[i], max(1, left * loads[i] // mass), spare)
            given[i] = given[i] + extra
            spare = spare - extra
    return np.array(given)


def centred(own_key, shape, scale, bound, pieces=(), kind=jnp.bfloat16):
    values = jax.random.normal(own_key, shape, jnp.float32) * scale
    if len(pieces) > 0:
        values = block_levels(own_key, shape, pieces, -0.22, 0.18) * values
    return jnp.clip(values, min=-bound, max=bound).astype(kind)


def setup_inputs(seed: int = 0) -> dict:
    splits = jax.random.split(jax.random.key(seed), 8)
    potential = centred(splits[0], (D, ROWS), 1.0, 6.0, ((1, 512),), jnp.float32)
    types_keys = jax.random.split(jax.random.fold_in(splits[1], 1), ROWS // P_DEV)
    types_turns = jax.random.permutation(jax.random.fold_in(splits[1], 3), ROWS // P_DEV)
    types = jax.vmap(lambda own, number: shared_out(jax.random.fold_in(splits[1], 2), own, number, P_DEV, TYPES, 1, CAP, 2))(types_keys, types_turns).reshape((ROWS, 1))
    saturation = with_ends(jax.random.randint(splits[2], (ROWS,), 0, NSAT), jax.random.fold_in(splits[2], 1), 0, NSAT - 1).astype(jnp.int32)
    pattern = with_ends(jax.random.randint(splits[3], (ROWS,), 0, 2 ** (LAM - 1)), jax.random.fold_in(splits[3], 1), 0, (2 ** (LAM - 1)) - 1).astype(jnp.int32)
    inverses = draw_inverses(jax.random.fold_in(splits[7], 71), 0)
    coupling = centred(splits[5], (TYPES, D, D), D ** -0.5, 0.75, ((0, 128),))
    skin = jnp.clip(1.0 + 0.15 * jax.random.normal(splits[6], (LAM,), jnp.float32), 0.25, 1.75)
    return dict(potential=potential, types=types, saturation=saturation, pattern=pattern, inverses=inverses, coupling=coupling, skin=skin)


def reference(potential, types, saturation, pattern, inverses, coupling, skin):
    padded = jnp.pad(potential, ((0, 0), (1, 1)))
    stencil = padded[:, :-2] - 2.0 * potential + padded[:, 2:]
    drive = potential.astype(jnp.bfloat16)
    nblocks = ROWS // P_DEV
    drive_blocks = drive.reshape(D, nblocks, P_DEV).transpose(1, 0, 2)
    type_blocks = types[:, 0].reshape(nblocks, P_DEV)
    sat_blocks = saturation.reshape(nblocks, P_DEV)
    pat_blocks = pattern.reshape(nblocks, P_DEV)
    shifts = jnp.arange(LAM - 1, dtype=jnp.int32)

    def one_block(packed):
        drive_b, type_b, sat_b, pat_b = packed
        dsel = inverses[type_b, sat_b].astype(jnp.float32)
        csel = coupling[type_b].astype(jnp.float32)
        bits = jnp.bitwise_and(jnp.right_shift(pat_b[None, :], shifts[:, None]), 1).astype(jnp.float32)
        bvec = skin[None, :, None] * drive_b.astype(jnp.float32)[:, None, :]
        state = jnp.zeros((D, LAM, P_DEV), jnp.float32)
        for sweep in range(ITERS):
            rounded = lax.optimization_barrier(state.astype(jnp.bfloat16)).astype(jnp.float32)
            upper = jnp.einsum('pij,jkp->ikp', csel, rounded)
            lower = jnp.einsum('pji,jkp->ikp', csel, rounded)
            resid = bvec
            resid = resid.at[:, :-1].add(-bits[None] * upper[:, 1:])
            resid = resid.at[:, 1:].add(-bits[None] * lower[:, :-1])
            rbound = lax.optimization_barrier(resid.astype(jnp.bfloat16)).astype(jnp.float32)
            state = jnp.einsum('pij,jkp->ikp', dsel, rbound)
        return (jnp.sum(state, axis=1) / LAM).astype(jnp.bfloat16)

    response = lax.map(one_block, (drive_blocks, type_blocks, sat_blocks, pat_blocks))
    response = response.transpose(1, 0, 2).reshape(D, ROWS)
    return potential + 0.25 * stencil - response.astype(jnp.float32)
```

```python
import functools

import jax
import jax.numpy as jnp
from jax import lax
from jax.experimental import pallas as pl
from jax.experimental.pallas import tpu as pltpu
from jax.sharding import PartitionSpec as P

MESH = pl.DeviceIdType.MESH
F32 = jnp.float32
BF16 = jnp.bfloat16
NY, NZ, NX = 4, 16, 4
NT = (((1,), (1,)), ((), ()))
TN = (((0,), (0,)), ((), ()))
NN = (((1,), (0,)), ((), ()))
OFFSETS = sorted(range(1, NZ), key=lambda d: min(d, NZ - d))


def mm(a, b, dims=NN):
    return lax.dot_general(a, b, dims, preferred_element_type=F32)


def iota(shape, axis):
    return lax.broadcasted_iota(jnp.int32, shape, axis)


def turn(x):
    return pltpu.roll(x, 64, 1)


def solve(points, codes, wbuf, skin):
    row, lane = iota((256, 128), 0), iota((256, 128), 1)
    half = lane // 64
    r2, c2 = iota((256, 256), 0), iota((256, 256), 1)
    order = ((r2 // 64) * 4 + ((r2 // 4) % 16) * 16 + r2 % 4 == c2).astype(BF16)
    x = mm(order, points)
    zsel = ((iota((256, 16), 0) // 4) % 16 == iota((256, 16), 1)).astype(BF16)
    spread = mm(zsel, codes.astype(BF16))
    spread = jnp.where(lane % 64 == (row // 64) * 4 + row % 4, spread, 0.0).astype(BF16)
    pick = (iota((128, 256), 0) // 64 == iota((128, 256), 1) // 128).astype(BF16)
    code2 = mm(spread, pick)
    xr = turn(x)
    total = skin[0]
    for k in range(1, 8):
        total = total + skin[k]
    sides = []
    for h in range(2):
        d2 = jnp.where(half == h, x, xr)
        code = code2[:, h * 128 : (h + 1) * 128]
        hi = (code < 0.0).astype(jnp.int32)
        bits = jnp.abs(code).astype(jnp.int32) - 1
        lo = jnp.bitwise_and(jnp.right_shift(bits, 7), 1)
        m = [jnp.bitwise_and(jnp.right_shift(bits, k), 1) == 1 for k in range(7)]
        both = [jnp.logical_and(m[k], m[k + 1]) for k in range(6)]
        alpha = sum(jnp.where(m[k], skin[k + 1], 0.0) for k in range(7))
        gamma = sum(jnp.where(m[k], skin[k], 0.0) for k in range(7))
        beta = sum(jnp.where(both[k], skin[k + 2], 0.0) for k in range(6))
        delta = sum(jnp.where(both[k], skin[k], 0.0) for k in range(6))
        sides.append((d2, hi == half, lo == half, alpha, beta, gamma, delta))

    def inverse(vs, h, rows):
        hi, lo = sides[h][1], sides[h][2]
        n = len(vs)
        masked = [jnp.where(hi, v, 0.0).astype(BF16) for v in vs]
        outs = [[] for _ in vs]
        for pair in range(4):
            part = slice(pair * 64, (pair + 1) * 64)
            stacked = masked[0][part] if n == 1 else jnp.concatenate([v[part] for v in masked], axis=0)
            got = mm(stacked, wbuf[h * 4 + pair, 0:128, :], NT)
            for i in range(n):
                outs[i].append(got[i * 64 : (i + 1) * 64])
        res = []
        for i in range(n):
            y = jnp.where(lo, jnp.concatenate(outs[i], axis=0), 0.0)
            res.append(y + turn(y))
        return res

    def couple(parts, h):
        n = len(parts)
        outs = [[] for _ in parts]
        for pair in range(4):
            part = slice(pair * 64, (pair + 1) * 64)
            c = wbuf[h * 4 + pair, 128:192, :]
            cc = jnp.concatenate([c, c], axis=0)
            stacked = parts[0][part] if n == 1 else jnp.concatenate([v[part] for v in parts], axis=0)
            got = mm(stacked, cc, NT)
            for i in range(n):
                outs[i].append(got[i * 64 : (i + 1) * 64])
        return [jnp.concatenate(o, axis=0) for o in outs]

    first = half == 0
    answers = []
    ys = [inverse([sides[h][0]], h, 64)[0] for h in range(2)]
    uvs = [
        couple([jnp.where(first, ys[h], 0.0).astype(BF16), jnp.where(first, 0.0, ys[h]).astype(BF16)], h)
        for h in range(2)
    ]
    pqs = [inverse(uvs[h], h, 128) for h in range(2)]
    for h in range(2):
        d2, _, _, alpha, beta, gamma, delta = sides[h]
        y, (p, q) = ys[h], pqs[h]
        up = alpha * y - beta * p - gamma * q
        down = gamma * y - alpha * p - delta * q
        z = total * d2 - couple([jnp.where(first, up, down).astype(BF16)], h)[0]
        high = z.astype(BF16).astype(F32)
        a, b = inverse([high, z - high], h, 128)
        answers.append((a + b) * 0.125)
    packed = jnp.where(first, answers[0], answers[1]).astype(BF16)
    return mm(order, packed, TN).astype(BF16)


def kernel(
    pot_hbm, types_hbm, sat_hbm, pat_hbm, inv_hbm, cpl_hbm, skin_hbm, out_ref,
    pot, typ, sat, pat, inv, cpl, skin, place, wbuf, send, recv, bsend, brecv, csend, crecv, hsend, hrecv,
    load_sem, ready, ps, pr, cs, cr, bs, br, ws, wr, hs, hr,
):
    dom, x = lax.axis_index("dom"), lax.axis_index("cell")
    c, z, y = lax.rem(dom, 2), lax.rem(dom // 2, NZ), dom // (2 * NZ)

    def at(yy, zz, cc):
        return ((yy * NZ + zz) * 2 + cc, x)

    zpeer = {d: at(y, lax.rem(z + d, NZ), c) for d in OFFSETS}
    zback = {d: at(y, lax.rem(z + NZ - d, NZ), c) for d in OFFSETS}
    wpeer = {h * 4 + u: at(lax.rem(y + NY - u, NY), z, c if h == 0 else 1 - c) for h in range(2) for u in range(NY)}
    wpeer.pop(0)
    index = dom * NX + x
    last = 2 * NY * NZ * NX - 1
    after = ((index + 1) // NX, lax.rem(index + 1, NX))
    before = ((index - 1 + NX) // NX - 1, lax.rem(index - 1 + NX, NX))
    has_after, has_before = index < last, index > 0

    barrier = pltpu.get_barrier_semaphore()
    for d in OFFSETS:
        @pl.when(z + d < NZ)
        def _(d=d):
            pl.semaphore_signal(barrier, inc=1, device_id=zpeer[d], device_id_type=MESH)
    for k in wpeer:
        pl.semaphore_signal(barrier, inc=1, device_id=wpeer[k], device_id_type=MESH)

    @pl.when(has_after)
    def _():
        pl.semaphore_signal(barrier, inc=1, device_id=after, device_id_type=MESH)

    @pl.when(has_before)
    def _():
        pl.semaphore_signal(barrier, inc=1, device_id=before, device_id_type=MESH)

    loads = [
        pltpu.make_async_copy(src, dst, load_sem.at[i])
        for i, (src, dst) in enumerate([
            (types_hbm, typ), (sat_hbm, sat), (pat_hbm, pat), (pot_hbm, pot), (inv_hbm, inv), (cpl_hbm, cpl),
            (skin_hbm, skin),
        ])
    ]
    for load in loads:
        load.start()
    pl.semaphore_wait(
        barrier, len(wpeer) + z + has_after.astype(jnp.int32) + has_before.astype(jnp.int32)
    )
    for d in OFFSETS:
        @pl.when(z - d >= 0)
        def _(d=d):
            pl.semaphore_signal(ready.at[d], inc=1, device_id=zback[d], device_id_type=MESH)
    for load in loads:
        load.wait()

    w = inv[...]
    wbuf[0, 0:128, :] = jnp.concatenate([w[0:128].astype(F32), w[128:256].astype(F32)], axis=1).astype(BF16)
    couple = cpl[...].astype(F32)
    wbuf[0, 128:192, :] = jnp.concatenate([couple, couple.T], axis=1).astype(BF16)
    sends = []
    for k in wpeer:
        copy = pltpu.make_async_remote_copy(
            wbuf.at[0], wbuf.at[k], ws.at[k], wr.at[k], device_id=wpeer[k], device_id_type=MESH
        )
        copy.start()
        sends.append(copy)
    weights = list(sends)

    field = pot[...]
    eye = iota((64, 128), 0) == iota((64, 128), 1)
    hsend[0] = jnp.sum(jnp.where(eye, field[:, 255:256], 0.0), axis=0, keepdims=True)
    hsend[1] = jnp.sum(jnp.where(eye, field[:, 0:1], 0.0), axis=0, keepdims=True)
    to_after = pltpu.make_async_remote_copy(
        hsend.at[0], hrecv.at[0], hs.at[0], hr.at[0], device_id=after, device_id_type=MESH
    )
    to_before = pltpu.make_async_remote_copy(
        hsend.at[1], hrecv.at[1], hs.at[1], hr.at[1], device_id=before, device_id_type=MESH
    )
    pl.when(has_after)(to_after.start)
    pl.when(has_before)(to_before.start)

    t = typ[...]
    onehot = (iota((128, 256), 0) == t).astype(BF16)
    earlier = (iota((256, 256), 0) < iota((256, 256), 1)).astype(BF16)
    rank = jnp.sum(onehot.astype(F32) * mm(onehot, earlier), axis=0, keepdims=True).astype(jnp.int32)
    t_y, t_z, t_c = t // (2 * NZ), (t // 2) % NZ, t % 2
    row = ((t_z - z + NZ) % NZ) * 16 + ((t_y - y + NY) % NY) * 4 + rank
    side = (t_c - c + 2) % 2
    both = jnp.concatenate([jnp.where(side == 0, row, -1), jnp.where(side == 1, row, -1)], axis=1)
    place[...] = (iota((256, 512), 0) == both).astype(BF16)
    level, bits = sat[...], pat[...]
    code = (1 + (level % 2) * 128 + bits) * jnp.where(level >= 2, -1, 1)
    code = jnp.broadcast_to(code.astype(F32), (64, 256)).astype(BF16)
    drive = field.astype(BF16)
    none = jnp.zeros((64, 256), BF16)
    table = jnp.concatenate(
        [jnp.concatenate([a, none], axis=1) if i == 0 else jnp.concatenate([none, a], axis=1)
         for a in (drive, code) for i in range(2)], axis=0
    )
    placed = mm(place[...], table, NT)
    points = placed[:, 0:128].astype(BF16).reshape(NZ, 16, 128)
    keep = iota((NZ, 16, 128), 2) % 64 == iota((NZ, 16, 128), 1)
    codes = jnp.sum(jnp.where(keep, placed[:, 128:256].reshape(NZ, 16, 128), 0.0), axis=1, keepdims=True)
    send[...] = points
    csend[...] = codes
    recv[0] = points[0]
    crecv[0] = codes[0]

    out, back = {}, {}
    for d in OFFSETS:
        out[d] = [
            pltpu.make_async_remote_copy(
                csend.at[d], crecv.at[d], cs.at[d], cr.at[d], device_id=zpeer[d], device_id_type=MESH
            ),
            pltpu.make_async_remote_copy(
                send.at[d], recv.at[d], ps.at[d], pr.at[d], device_id=zpeer[d], device_id_type=MESH
            ),
        ]
        back[d] = pltpu.make_async_remote_copy(
            bsend.at[d], brecv.at[d], bs.at[d], br.at[d], device_id=zback[d], device_id_type=MESH
        )

    for d in OFFSETS:
        @pl.when(z + d < NZ)
        def _(d=d):
            pl.semaphore_wait(ready.at[d], 1)
        for copy in out[d]:
            copy.start()

    pl.when(has_before)(to_after.wait_recv)
    pl.when(has_after)(to_before.wait_recv)
    lane = iota((64, 256), 1)
    wide = iota((64, 128), 0) == iota((64, 128), 1)
    left = jnp.sum(jnp.where(jnp.logical_and(wide, has_before), hrecv[0], 0.0), axis=1, keepdims=True)
    right = jnp.sum(jnp.where(jnp.logical_and(wide, has_after), hrecv[1], 0.0), axis=1, keepdims=True)
    left = jnp.where(lane == 0, left, pltpu.roll(field, 1, 1))
    right = jnp.where(lane == 255, right, pltpu.roll(field, 255, 1))
    pot[...] = field + 0.25 * (left - 2.0 * field + right)

    for copy in weights:
        copy.wait_recv()
    for d in OFFSETS:
        for copy in out[d]:
            copy.wait_recv()
    answer = solve(recv[...].reshape(256, 128), crecv[...].reshape(NZ, 128), wbuf, skin)
    bsend[...] = answer.reshape(NZ, 16, 128)
    for d in reversed(OFFSETS):
        back[d].start()
    brecv[0] = bsend[0]
    for d in OFFSETS:
        back[d].wait_recv()
    got = mm(brecv[...].reshape(256, 128), place[...], TN)
    out_ref[...] = pot[...] - (got[0:64, 0:256] + got[64:128, 256:512])

    for copy in sends:
        copy.wait_send()
    for d in OFFSETS:
        for copy in out[d]:
            copy.wait_send()
        back[d].wait_send()
    pl.when(has_after)(to_after.wait_send)
    pl.when(has_before)(to_before.wait_send)


def body(potential, types, saturation, pattern, inverses, coupling, skin):
    dma = pltpu.SemaphoreType.DMA
    return pl.pallas_call(
        kernel,
        out_shape=jax.ShapeDtypeStruct((64, 256), F32),
        in_specs=[pl.BlockSpec(memory_space=pl.ANY)] * 7,
        out_specs=pl.BlockSpec(memory_space=pltpu.VMEM),
        scratch_shapes=[
            pltpu.VMEM((64, 256), F32),
            pltpu.VMEM((1, 256), jnp.int32),
            pltpu.VMEM((1, 256), jnp.int32),
            pltpu.VMEM((1, 256), jnp.int32),
            pltpu.VMEM((256, 64), BF16),
            pltpu.VMEM((64, 64), BF16),
            pltpu.SMEM((8,), F32),
            pltpu.VMEM((256, 512), BF16),
            pltpu.VMEM((8, 192, 128), BF16),
            pltpu.VMEM((NZ, 16, 128), BF16),
            pltpu.VMEM((NZ, 16, 128), BF16),
            pltpu.VMEM((NZ, 16, 128), BF16),
            pltpu.VMEM((NZ, 16, 128), BF16),
            pltpu.VMEM((NZ, 1, 128), F32),
            pltpu.VMEM((NZ, 1, 128), F32),
            pltpu.VMEM((2, 1, 128), F32),
            pltpu.VMEM((2, 1, 128), F32),
            dma((7,)),
            pltpu.SemaphoreType.REGULAR((NZ,)),
            *[dma((NZ,)) for _ in range(6)],
            *[dma((8,)) for _ in range(2)],
            *[dma((2,)) for _ in range(2)],
        ],
        compiler_params=pltpu.CompilerParams(
            collective_id=0, has_side_effects=True, vmem_limit_bytes=32 * 1024 * 1024
        ),
        name="regroup_solve",
    )(
        potential,
        types.reshape(1, 256),
        saturation.reshape(1, 256),
        pattern.reshape(1, 256),
        inverses.reshape(256, 64),
        coupling.reshape(64, 64),
        skin,
    )


def solution(mesh):
    placed = (
        P(None, ("dom", "cell")),
        P(("dom", "cell"), None),
        P(("dom", "cell")),
        P(("dom", "cell")),
        P("dom", None, None, None),
        P("dom", None, None),
        P(),
    )
    return jax.shard_map(
        body, mesh=mesh, in_specs=placed, out_specs=P(None, ("dom", "cell")), check_vma=False
    )
```

```python
import functools

import jax
import jax.numpy as jnp
from jax import lax
from jax.experimental import pallas as pl
from jax.experimental.pallas import tpu as pltpu
from jax.sharding import PartitionSpec as P

MESH = pl.DeviceIdType.MESH
F32 = jnp.float32
BF16 = jnp.bfloat16
NY, NZ, NX = 4, 16, 4
NT = (((1,), (1,)), ((), ()))
TN = (((0,), (0,)), ((), ()))
NN = (((1,), (0,)), ((), ()))
OFFSETS = sorted(range(1, NZ), key=lambda d: min(d, NZ - d))


def mm(a, b, dims=NN):
    return lax.dot_general(a, b, dims, preferred_element_type=F32)


def iota(shape, axis):
    return lax.broadcasted_iota(jnp.int32, shape, axis)


def turn(x):
    return pltpu.roll(x, 64, 1)


def coefficients(skin):
    row, lane = iota((128, 128), 0), iota((128, 128), 1)
    place_in = row % 64
    bit, part, first = place_in % 13, place_in // 13, lane < 64

    def chosen(lower, upper):
        value = jnp.zeros((128, 128), F32)
        for i in range(13):
            a = skin[lower[i]] if i in lower else 0.0
            b = skin[upper[i]] if i in upper else 0.0
            value = jnp.where(bit == i, jnp.where(first, a, b), value)
        return value

    above, here = {i: i + 1 for i in range(7)}, {i: i for i in range(7)}
    above2, here2 = {7 + i: i + 2 for i in range(6)}, {7 + i: i for i in range(6)}
    value = jnp.concatenate([chosen(above, here), chosen(above2, above), chosen(here, here2)], axis=1)
    row, part = iota((128, 384), 0), (iota((128, 384), 0) % 64) // 13
    high = value.astype(BF16).astype(F32)
    rest = value - high
    middle = rest.astype(BF16).astype(F32)
    value = jnp.where(part == 0, high, jnp.where(part == 1, middle, jnp.where(part == 2, rest - middle, 0.0)))
    return jnp.concatenate([jnp.where(row // 64 == h, value, 0.0) for h in range(2)], axis=1).astype(BF16)


def solve(points, codes, wbuf, table, total):
    n = codes.shape[0]
    rows, each = 16 * n, 4 * n
    row, lane = iota((rows, 128), 0), iota((rows, 128), 1)
    first = lane < 64
    r2, c2 = iota((rows, rows), 0), iota((rows, rows), 1)
    order = ((r2 // each) * 4 + ((r2 // 4) % n) * 16 + r2 % 4 == c2).astype(BF16)
    zsel = ((iota((rows, n), 0) // 4) % n == iota((rows, n), 1)).astype(BF16)
    spread = mm(zsel, codes.astype(BF16))
    x = mm(order, points)
    spread = jnp.where(lane % 64 == (row // each) * 4 + row % 4, spread, 0.0).astype(BF16)
    from_half, to = iota((128, 384), 0) // 64, iota((128, 384), 1)
    pick = (from_half == jnp.where(to < 256, to // 128, (to // 64) % 2)).astype(BF16)
    code = mm(spread, pick)
    bits = jnp.abs(code[:, 256:384]).astype(jnp.int32) - 1
    bit = (lane % 64) % 13
    mask = jnp.where(bit < 7, jnp.left_shift(1, bit), jnp.left_shift(3, jnp.maximum(bit - 7, 0)))
    held = jnp.logical_and(jnp.bitwise_and(bits, mask) == mask, lane % 64 < 39)
    factors = mm(held.astype(F32).astype(BF16), table)
    xr = turn(x)
    sides = []
    for h in range(2):
        d2 = jnp.where(first, x, xr) if h == 0 else jnp.where(first, xr, x)
        c = code[:, h * 128 : (h + 1) * 128]
        hi = jnp.where(first, c, -c) >= 0.0
        lo = (jnp.abs(c) > 128.0) != first
        sides.append((d2, hi, lo))

    def inverse(vs, h):
        _, hi, lo = sides[h]
        masked = [jnp.where(hi, v, 0.0).astype(BF16) for v in vs]
        outs = [[] for _ in vs]
        for pair in range(4):
            part = slice(pair * each, (pair + 1) * each)
            stacked = masked[0][part] if len(vs) == 1 else jnp.concatenate([v[part] for v in masked], axis=0)
            got = mm(stacked, wbuf[h * 4 + pair, 0:128, :], NT)
            for i in range(len(vs)):
                outs[i].append(got[i * each : (i + 1) * each])
        res = []
        for out in outs:
            y = jnp.where(lo, jnp.concatenate(out, axis=0), 0.0)
            res.append(y + turn(y))
        return res

    def couple(parts, h):
        outs = [[] for _ in parts]
        for pair in range(4):
            part = slice(pair * each, (pair + 1) * each)
            c = wbuf[h * 4 + pair, 128:192, :]
            stacked = parts[0][part] if len(parts) == 1 else jnp.concatenate([v[part] for v in parts], axis=0)
            got = mm(stacked, jnp.concatenate([c, c], axis=0), NT)
            for i in range(len(parts)):
                outs[i].append(got[i * each : (i + 1) * each])
        return [jnp.concatenate(o, axis=0) for o in outs]

    ys = [inverse([sides[h][0]], h)[0] for h in range(2)]
    uvs = [
        couple([jnp.where(first, ys[h], 0.0).astype(BF16), jnp.where(first, 0.0, ys[h]).astype(BF16)], h)
        for h in range(2)
    ]
    pqs = [inverse(uvs[h], h) for h in range(2)]
    answers = []
    for h in range(2):
        f = [factors[:, h * 384 + i * 128 : h * 384 + (i + 1) * 128] for i in range(3)]
        mixed = f[0] * ys[h] - f[1] * pqs[h][0] - f[2] * pqs[h][1]
        z = total * sides[h][0] - couple([mixed.astype(BF16)], h)[0]
        high = z.astype(BF16).astype(F32)
        a, b = inverse([high, z - high], h)
        answers.append((a + b) * 0.125)
    packed = jnp.where(first, answers[0], answers[1]).astype(BF16)
    return mm(order, packed, TN).astype(BF16)


def kernel(
    pot_hbm, types_hbm, sat_hbm, pat_hbm, inv_hbm, cpl_hbm, skin_hbm, out_ref,
    pot, typ, sat, pat, inv, cpl, skin, place, table, wbuf, send, recv, bsend, brecv, csend, crecv, hsend, hrecv,
    load_sem, ready, wready, hready, ps, pr, cs, cr, bs, br, ws, wr, hs, hr,
):
    dom, x = lax.axis_index("dom"), lax.axis_index("cell")
    c, z, y = lax.rem(dom, 2), lax.rem(dom // 2, NZ), dom // (2 * NZ)

    def at(yy, zz, cc):
        return ((yy * NZ + zz) * 2 + cc, x)

    ahead = {d: lax.rem(z + d, NZ) for d in OFFSETS}
    behind = {d: lax.rem(z + NZ - d, NZ) for d in OFFSETS}
    zpeer = {d: at(y, ahead[d], c) for d in OFFSETS}
    zback = {d: at(y, behind[d], c) for d in OFFSETS}
    wpeer, later = {}, {}
    key = y * 2 + 1 - c
    for k in range(1, 8):
        yy, cc = lax.rem(y + NY - k % 4, NY), c if k < 4 else 1 - c
        wpeer[k] = at(yy, z, cc)
        later[k] = yy * 2 + 1 - cc > key
    index = dom * NX + x
    after = ((index + 1) // NX, lax.rem(index + 1, NX))
    before = ((index - 1 + NX) // NX - 1, lax.rem(index - 1 + NX, NX))
    has_after, has_before = index < 2 * NY * NZ * NX - 1, index > 0

    def follows(xx, cc, zz):
        return jnp.logical_or(xx < NX - 1, jnp.logical_and(cc == 1, zz < NZ - 1))

    back_dom = before[0]
    i_first = jnp.logical_and(has_after, follows(x, c, z))
    i_last = jnp.logical_and(has_after, jnp.logical_not(follows(x, c, z)))
    b_follows = follows(before[1], lax.rem(back_dom, 2), lax.rem(back_dom // 2, NZ))
    b_first = jnp.logical_and(has_before, b_follows)
    b_last = jnp.logical_and(has_before, jnp.logical_not(b_follows))

    barrier = pltpu.get_barrier_semaphore()
    for d in OFFSETS:
        @pl.when(z + d < NZ)
        def _(d=d):
            pl.semaphore_signal(barrier, inc=1, device_id=zpeer[d], device_id_type=MESH)
    for k in wpeer:
        @pl.when(later[k])
        def _(k=k):
            pl.semaphore_signal(barrier, inc=1, device_id=wpeer[k], device_id_type=MESH)

    @pl.when(i_first)
    def _():
        pl.semaphore_signal(barrier, inc=1, device_id=after, device_id_type=MESH)

    @pl.when(b_last)
    def _():
        pl.semaphore_signal(barrier, inc=1, device_id=before, device_id_type=MESH)

    loads = [
        pltpu.make_async_copy(src, dst, load_sem.at[i])
        for i, (src, dst) in enumerate([
            (types_hbm, typ), (sat_hbm, sat), (pat_hbm, pat), (pot_hbm, pot), (inv_hbm, inv), (cpl_hbm, cpl),
            (skin_hbm, skin),
        ])
    ]
    for load in loads:
        load.start()
    n_earlier = key + z + b_first.astype(jnp.int32) + i_last.astype(jnp.int32)

    @pl.when(n_earlier > 0)
    def _():
        pl.semaphore_wait(barrier, n_earlier)

    for d in reversed(OFFSETS):
        @pl.when(z - d >= 0)
        def _(d=d):
            pl.semaphore_signal(ready.at[d], inc=1, device_id=zback[d], device_id_type=MESH)
    for k in wpeer:
        @pl.when(jnp.logical_not(later[k]))
        def _(k=k):
            at_peer = k // 4 * 4 + (4 - k % 4) % 4
            pl.semaphore_signal(wready.at[at_peer], inc=1, device_id=wpeer[k], device_id_type=MESH)

    @pl.when(i_last)
    def _():
        pl.semaphore_signal(hready.at[1], inc=1, device_id=after, device_id_type=MESH)

    @pl.when(b_first)
    def _():
        pl.semaphore_signal(hready.at[0], inc=1, device_id=before, device_id_type=MESH)

    for load in loads:
        load.wait()

    field = pot[...]
    t = typ[...]
    onehot = (iota((128, 256), 0) == t).astype(BF16)
    earlier = (iota((256, 256), 0) < iota((256, 256), 1)).astype(BF16)
    rank = jnp.sum(onehot.astype(F32) * mm(onehot, earlier), axis=0, keepdims=True).astype(jnp.int32)
    t_y, t_z, t_c = t // (2 * NZ), (t // 2) % NZ, t % 2
    row = t_z * 16 + ((t_y - y + NY) % NY) * 4 + rank
    side = (t_c - c + 2) % 2
    both = jnp.concatenate([jnp.where(side == 0, row, -1), jnp.where(side == 1, row, -1)], axis=1)
    place[...] = (iota((256, 512), 0) == both).astype(BF16)
    level, bits = sat[...], pat[...]
    code = (1 + (level % 2) * 128 + bits) * jnp.where(level >= 2, -1, 1)
    code = jnp.broadcast_to(code.astype(F32), (64, 256)).astype(BF16)
    drive = field.astype(BF16)
    none = jnp.zeros((64, 256), BF16)
    spread = jnp.concatenate(
        [jnp.concatenate([a, none], axis=1) if i == 0 else jnp.concatenate([none, a], axis=1)
         for a in (drive, code) for i in range(2)], axis=0
    )
    placed = mm(place[...], spread, NT)
    keep = iota((NZ, 16, 128), 2) % 64 == iota((NZ, 16, 128), 1)
    send[...] = placed[:, 0:128].astype(BF16).reshape(NZ, 16, 128)
    csend[...] = jnp.sum(jnp.where(keep, placed[:, 128:256].reshape(NZ, 16, 128), 0.0), axis=1, keepdims=True)

    out, back, backin = {}, {}, {}
    for d in OFFSETS:
        out[d] = [
            pltpu.make_async_remote_copy(
                csend.at[ahead[d]], crecv.at[z], cs.at[d], cr.at[d], device_id=zpeer[d], device_id_type=MESH
            ),
            pltpu.make_async_remote_copy(
                send.at[ahead[d]], recv.at[z], ps.at[d], pr.at[d], device_id=zpeer[d], device_id_type=MESH
            ),
        ]
        back[d] = pltpu.make_async_remote_copy(
            bsend.at[behind[d]], brecv.at[z], bs.at[d], br.at[d], device_id=zback[d], device_id_type=MESH
        )
    for d in OFFSETS:
        @pl.when(z + d >= NZ)
        def _(d=d):
            for copy in out[d]:
                copy.start()

    w = inv[...]
    wbuf[0, 0:128, :] = jnp.concatenate([w[0:128].astype(F32), w[128:256].astype(F32)], axis=1).astype(BF16)
    block = cpl[...].astype(F32)
    wbuf[0, 128:192, :] = jnp.concatenate([block, block.T], axis=1).astype(BF16)
    weights = {
        k: pltpu.make_async_remote_copy(
            wbuf.at[0], wbuf.at[k], ws.at[k], wr.at[k], device_id=wpeer[k], device_id_type=MESH
        )
        for k in wpeer
    }
    for want in (False, True):
        for k in weights:
            @pl.when(later[k] == want)
            def _(k=k, want=want):
                if want:
                    pl.semaphore_wait(wready.at[k], 1)
                weights[k].start()

    eye = iota((64, 128), 0) == iota((64, 128), 1)
    hsend[0] = jnp.sum(jnp.where(eye, field[:, 255:256], 0.0), axis=0, keepdims=True)
    hsend[1] = jnp.sum(jnp.where(eye, field[:, 0:1], 0.0), axis=0, keepdims=True)
    to_after = pltpu.make_async_remote_copy(
        hsend.at[0], hrecv.at[0], hs.at[0], hr.at[0], device_id=after, device_id_type=MESH
    )
    to_before = pltpu.make_async_remote_copy(
        hsend.at[1], hrecv.at[1], hs.at[1], hr.at[1], device_id=before, device_id_type=MESH
    )

    @pl.when(i_first)
    def _():
        pl.semaphore_wait(hready.at[0], 1)

    @pl.when(b_last)
    def _():
        pl.semaphore_wait(hready.at[1], 1)

    pl.when(has_after)(to_after.start)
    pl.when(has_before)(to_before.start)

    for d in OFFSETS:
        @pl.when(z + d < NZ)
        def _(d=d):
            pl.semaphore_wait(ready.at[d], 1)
            for copy in out[d]:
                copy.start()
    recv[z] = send[z]
    crecv[z] = csend[z]

    table[...] = coefficients(skin)
    total = skin[0]
    for k in range(1, 8):
        total = total + skin[k]

    for k in weights:
        weights[k].wait_recv()
    for d in OFFSETS:
        for copy in out[d]:
            copy.wait_recv()
    answer = solve(recv[...].reshape(256, 128), crecv[...].reshape(NZ, 128), wbuf, table[...], total)
    bsend[...] = answer.reshape(NZ, 16, 128)
    for d in reversed(OFFSETS):
        back[d].start()
    brecv[z] = bsend[z]

    pl.when(has_before)(to_after.wait_recv)
    pl.when(has_after)(to_before.wait_recv)
    lane = iota((64, 256), 1)
    left = jnp.sum(jnp.where(jnp.logical_and(eye, has_before), hrecv[0], 0.0), axis=1, keepdims=True)
    right = jnp.sum(jnp.where(jnp.logical_and(eye, has_after), hrecv[1], 0.0), axis=1, keepdims=True)
    left = jnp.where(lane == 0, left, pltpu.roll(field, 1, 1))
    right = jnp.where(lane == 255, right, pltpu.roll(field, 255, 1))
    pot[...] = field + 0.25 * (left - 2.0 * field + right)

    for d in OFFSETS:
        back[d].wait_recv()
    got = mm(brecv[...].reshape(256, 128), place[...], TN)
    out_ref[...] = pot[...] - (got[0:64, 0:256] + got[64:128, 256:512])

    for k in weights:
        weights[k].wait_send()
    for d in OFFSETS:
        for copy in out[d]:
            copy.wait_send()
        back[d].wait_send()
    pl.when(has_after)(to_after.wait_send)
    pl.when(has_before)(to_before.wait_send)


def body(potential, types, saturation, pattern, inverses, coupling, skin):
    dma = pltpu.SemaphoreType.DMA
    return pl.pallas_call(
        kernel,
        out_shape=jax.ShapeDtypeStruct((64, 256), F32),
        in_specs=[pl.BlockSpec(memory_space=pl.ANY)] * 7,
        out_specs=pl.BlockSpec(memory_space=pltpu.VMEM),
        scratch_shapes=[
            pltpu.VMEM((64, 256), F32),
            pltpu.VMEM((1, 256), jnp.int32),
            pltpu.VMEM((1, 256), jnp.int32),
            pltpu.VMEM((1, 256), jnp.int32),
            pltpu.VMEM((256, 64), BF16),
            pltpu.VMEM((64, 64), BF16),
            pltpu.SMEM((8,), F32),
            pltpu.VMEM((256, 512), BF16),
            pltpu.VMEM((128, 768), BF16),
            pltpu.VMEM((8, 192, 128), BF16),
            pltpu.VMEM((NZ, 16, 128), BF16),
            pltpu.VMEM((NZ, 16, 128), BF16),
            pltpu.VMEM((NZ, 16, 128), BF16),
            pltpu.VMEM((NZ, 16, 128), BF16),
            pltpu.VMEM((NZ, 1, 128), F32),
            pltpu.VMEM((NZ, 1, 128), F32),
            pltpu.VMEM((2, 1, 128), F32),
            pltpu.VMEM((2, 1, 128), F32),
            dma((7,)),
            pltpu.SemaphoreType.REGULAR((NZ,)),
            pltpu.SemaphoreType.REGULAR((8,)),
            pltpu.SemaphoreType.REGULAR((2,)),
            *[dma((NZ,)) for _ in range(6)],
            *[dma((8,)) for _ in range(2)],
            *[dma((2,)) for _ in range(2)],
        ],
        compiler_params=pltpu.CompilerParams(
            collective_id=0, has_side_effects=True, vmem_limit_bytes=64 * 1024 * 1024
        ),
        name="regroup_solve",
    )(
        potential,
        types.reshape(1, 256),
        saturation.reshape(1, 256),
        pattern.reshape(1, 256),
        inverses.reshape(256, 64),
        coupling.reshape(64, 64),
        skin,
    )


def solution(mesh):
    placed = (
        P(None, ("dom", "cell")),
        P(("dom", "cell"), None),
        P(("dom", "cell")),
        P(("dom", "cell")),
        P("dom", None, None, None),
        P("dom", None, None),
        P(),
    )
    return jax.shard_map(
        body, mesh=mesh, in_specs=placed, out_specs=P(None, ("dom", "cell")), check_vma=False
    )
```

```python
import functools

import jax
import jax.numpy as jnp
from jax import lax
from jax.experimental import pallas as pl
from jax.experimental.pallas import tpu as pltpu
from jax.sharding import PartitionSpec as P

MESH = pl.DeviceIdType.MESH
F32 = jnp.float32
BF16 = jnp.bfloat16
NY, NZ, NX = 4, 16, 4
NT = (((1,), (1,)), ((), ()))
TN = (((0,), (0,)), ((), ()))
NN = (((1,), (0,)), ((), ()))
GROUP = 4
FAR = range(GROUP + 1, 2 * GROUP + 2)
OFFSETS = sorted(range(1, NZ), key=lambda d: min(d, NZ - d))


def mm(a, b, dims=NN):
    return lax.dot_general(a, b, dims, preferred_element_type=F32)


def iota(shape, axis):
    return lax.broadcasted_iota(jnp.int32, shape, axis)


def turn(x):
    return pltpu.roll(x, 64, 1)


def coefficients(skin):
    row, lane = iota((128, 128), 0), iota((128, 128), 1)
    place_in = row % 64
    bit, part, first = place_in % 13, place_in // 13, lane < 64

    def chosen(lower, upper):
        value = jnp.zeros((128, 128), F32)
        for i in range(13):
            a = skin[lower[i]] if i in lower else 0.0
            b = skin[upper[i]] if i in upper else 0.0
            value = jnp.where(bit == i, jnp.where(first, a, b), value)
        return value

    above, here = {i: i + 1 for i in range(7)}, {i: i for i in range(7)}
    above2, here2 = {7 + i: i + 2 for i in range(6)}, {7 + i: i for i in range(6)}
    value = jnp.concatenate([chosen(above, here), chosen(above2, above), chosen(here, here2)], axis=1)
    row, part = iota((128, 384), 0), (iota((128, 384), 0) % 64) // 13
    high = value.astype(BF16).astype(F32)
    rest = value - high
    middle = rest.astype(BF16).astype(F32)
    value = jnp.where(part == 0, high, jnp.where(part == 1, middle, jnp.where(part == 2, rest - middle, 0.0)))
    return jnp.concatenate([jnp.where(row // 64 == h, value, 0.0) for h in range(2)], axis=1).astype(BF16)


def solve(points, codes, wbuf, table, total):
    n = codes.shape[0]
    rows, each = 16 * n, 4 * n
    row, lane = iota((rows, 128), 0), iota((rows, 128), 1)
    first = lane < 64
    r2, c2 = iota((rows, rows), 0), iota((rows, rows), 1)
    order = ((r2 // each) * 4 + ((r2 // 4) % n) * 16 + r2 % 4 == c2).astype(BF16)
    zsel = ((iota((rows, n), 0) // 4) % n == iota((rows, n), 1)).astype(BF16)
    spread = mm(zsel, codes.astype(BF16))
    x = mm(order, points)
    spread = jnp.where(lane % 64 == (row // each) * 4 + row % 4, spread, 0.0).astype(BF16)
    from_half, to = iota((128, 384), 0) // 64, iota((128, 384), 1)
    pick = (from_half == jnp.where(to < 256, to // 128, (to // 64) % 2)).astype(BF16)
    code = mm(spread, pick)
    bits = jnp.abs(code[:, 256:384]).astype(jnp.int32) - 1
    bit = (lane % 64) % 13
    mask = jnp.where(bit < 7, jnp.left_shift(1, bit), jnp.left_shift(3, jnp.maximum(bit - 7, 0)))
    held = jnp.logical_and(jnp.bitwise_and(bits, mask) == mask, lane % 64 < 39)
    factors = mm(held.astype(F32).astype(BF16), table)
    xr = turn(x)
    sides = []
    for h in range(2):
        d2 = jnp.where(first, x, xr) if h == 0 else jnp.where(first, xr, x)
        c = code[:, h * 128 : (h + 1) * 128]
        hi = jnp.where(first, c, -c) >= 0.0
        lo = (jnp.abs(c) > 128.0) != first
        sides.append((d2, hi, lo))

    def inverse(vs, h):
        _, hi, lo = sides[h]
        masked = [jnp.where(hi, v, 0.0).astype(BF16) for v in vs]
        outs = [[] for _ in vs]
        for pair in range(4):
            part = slice(pair * each, (pair + 1) * each)
            stacked = masked[0][part] if len(vs) == 1 else jnp.concatenate([v[part] for v in masked], axis=0)
            got = mm(stacked, wbuf[h * 4 + pair, 0:128, :], NT)
            for i in range(len(vs)):
                outs[i].append(got[i * each : (i + 1) * each])
        res = []
        for out in outs:
            y = jnp.where(lo, jnp.concatenate(out, axis=0), 0.0)
            res.append(y + turn(y))
        return res

    def couple(parts, h):
        outs = [[] for _ in parts]
        for pair in range(4):
            part = slice(pair * each, (pair + 1) * each)
            c = wbuf[h * 4 + pair, 128:192, :]
            stacked = parts[0][part] if len(parts) == 1 else jnp.concatenate([v[part] for v in parts], axis=0)
            got = mm(stacked, jnp.concatenate([c, c], axis=0), NT)
            for i in range(len(parts)):
                outs[i].append(got[i * each : (i + 1) * each])
        return [jnp.concatenate(o, axis=0) for o in outs]

    ys = [inverse([sides[h][0]], h)[0] for h in range(2)]
    uvs = [
        couple([jnp.where(first, ys[h], 0.0).astype(BF16), jnp.where(first, 0.0, ys[h]).astype(BF16)], h)
        for h in range(2)
    ]
    pqs = [inverse(uvs[h], h) for h in range(2)]
    answers = []
    for h in range(2):
        f = [factors[:, h * 384 + i * 128 : h * 384 + (i + 1) * 128] for i in range(3)]
        mixed = f[0] * ys[h] - f[1] * pqs[h][0] - f[2] * pqs[h][1]
        z = total * sides[h][0] - couple([mixed.astype(BF16)], h)[0]
        high = z.astype(BF16).astype(F32)
        a, b = inverse([high, z - high], h)
        answers.append((a + b) * 0.125)
    packed = jnp.where(first, answers[0], answers[1]).astype(BF16)
    return mm(order, packed, TN).astype(BF16)


def kernel(
    pot_hbm, types_hbm, sat_hbm, pat_hbm, inv_hbm, cpl_hbm, skin_hbm, out_ref,
    pot, typ, sat, pat, inv, cpl, skin, place, table, wbuf, send, recv, bsend, brecv, csend, crecv, hsend, hrecv, rbuf, crbuf,
    load_sem, ready, wready, hready, ps, pr, cs, cr, bs, br, ws, wr, hs, hr, bds, bdr, fs, cfs,
):
    dom, x = lax.axis_index("dom"), lax.axis_index("cell")
    c, z, y = lax.rem(dom, 2), lax.rem(dom // 2, NZ), dom // (2 * NZ)

    def at(yy, zz, cc):
        return ((yy * NZ + zz) * 2 + cc, x)

    ahead = {d: lax.rem(z + d, NZ) for d in OFFSETS}
    behind = {d: lax.rem(z + NZ - d, NZ) for d in OFFSETS}
    zpeer = {d: at(y, ahead[d], c) for d in OFFSETS}
    zback = {d: at(y, behind[d], c) for d in OFFSETS}
    wpeer, later = {}, {}
    key = y * 2 + 1 - c
    for k in range(1, 8):
        yy, cc = lax.rem(y + NY - k % 4, NY), c if k < 4 else 1 - c
        wpeer[k] = at(yy, z, cc)
        later[k] = yy * 2 + 1 - cc > key
    index = dom * NX + x
    after = ((index + 1) // NX, lax.rem(index + 1, NX))
    before = ((index - 1 + NX) // NX - 1, lax.rem(index - 1 + NX, NX))
    has_after, has_before = index < 2 * NY * NZ * NX - 1, index > 0

    i_first = jnp.logical_and(has_after, x < NX - 1)
    i_last = jnp.logical_and(has_after, x == NX - 1)
    b_first = jnp.logical_and(has_before, x > 0)
    b_last = jnp.logical_and(has_before, x == 0)
    relayed = z < GROUP
    relays = jnp.logical_and(z >= GROUP, z < 2 * GROUP)

    barrier = pltpu.get_barrier_semaphore()
    for d in OFFSETS:
        @pl.when(z + d < NZ)
        def _(d=d):
            pl.semaphore_signal(barrier, inc=1, device_id=zpeer[d], device_id_type=MESH)
    for k in wpeer:
        @pl.when(later[k])
        def _(k=k):
            pl.semaphore_signal(barrier, inc=1, device_id=wpeer[k], device_id_type=MESH)

    @pl.when(i_first)
    def _():
        pl.semaphore_signal(barrier, inc=1, device_id=after, device_id_type=MESH)

    @pl.when(b_last)
    def _():
        pl.semaphore_signal(barrier, inc=1, device_id=before, device_id_type=MESH)

    loads = [
        pltpu.make_async_copy(src, dst, load_sem.at[i])
        for i, (src, dst) in enumerate([
            (types_hbm, typ), (sat_hbm, sat), (pat_hbm, pat), (pot_hbm, pot), (inv_hbm, inv), (cpl_hbm, cpl),
            (skin_hbm, skin),
        ])
    ]
    for load in loads:
        load.start()
    n_earlier = key + z + b_first.astype(jnp.int32) + i_last.astype(jnp.int32)

    @pl.when(n_earlier > 0)
    def _():
        pl.semaphore_wait(barrier, n_earlier)

    for d in reversed(OFFSETS):
        @pl.when(z - d >= 0)
        def _(d=d):
            pl.semaphore_signal(ready.at[d], inc=1, device_id=zback[d], device_id_type=MESH)
    for k in wpeer:
        @pl.when(jnp.logical_not(later[k]))
        def _(k=k):
            at_peer = k // 4 * 4 + (4 - k % 4) % 4
            pl.semaphore_signal(wready.at[at_peer], inc=1, device_id=wpeer[k], device_id_type=MESH)

    @pl.when(i_last)
    def _():
        pl.semaphore_signal(hready.at[1], inc=1, device_id=after, device_id_type=MESH)

    @pl.when(b_first)
    def _():
        pl.semaphore_signal(hready.at[0], inc=1, device_id=before, device_id_type=MESH)

    for load in loads:
        load.wait()

    field = pot[...]
    t = typ[...]
    onehot = (iota((128, 256), 0) == t).astype(BF16)
    earlier = (iota((256, 256), 0) < iota((256, 256), 1)).astype(BF16)
    rank = jnp.sum(onehot.astype(F32) * mm(onehot, earlier), axis=0, keepdims=True).astype(jnp.int32)
    t_y, t_z, t_c = t // (2 * NZ), (t // 2) % NZ, t % 2
    row = t_z * 16 + ((t_y - y + NY) % NY) * 4 + rank
    side = (t_c - c + 2) % 2
    both = jnp.concatenate([jnp.where(side == 0, row, -1), jnp.where(side == 1, row, -1)], axis=1)
    place[...] = (iota((256, 512), 0) == both).astype(BF16)
    level, bits = sat[...], pat[...]
    code = (1 + (level % 2) * 128 + bits) * jnp.where(level >= 2, -1, 1)
    code = jnp.broadcast_to(code.astype(F32), (64, 256)).astype(BF16)
    drive = field.astype(BF16)
    none = jnp.zeros((64, 256), BF16)
    spread = jnp.concatenate(
        [jnp.concatenate([a, none], axis=1) if i == 0 else jnp.concatenate([none, a], axis=1)
         for a in (drive, code) for i in range(2)], axis=0
    )
    placed = mm(place[...], spread, NT)
    keep = iota((NZ, 16, 128), 2) % 64 == iota((NZ, 16, 128), 1)
    send[...] = placed[:, 0:128].astype(BF16).reshape(NZ, 16, 128)
    csend[...] = jnp.sum(jnp.where(keep, placed[:, 128:256].reshape(NZ, 16, 128), 0.0), axis=1, keepdims=True)

    out, back, backin = {}, {}, {}
    for d in OFFSETS:
        out[d] = [
            pltpu.make_async_remote_copy(
                csend.at[ahead[d]], crecv.at[z], cs.at[d], cr.at[d], device_id=zpeer[d], device_id_type=MESH
            ),
            pltpu.make_async_remote_copy(
                send.at[ahead[d]], recv.at[z], ps.at[d], pr.at[d], device_id=zpeer[d], device_id_type=MESH
            ),
        ]
        back[d] = pltpu.make_async_remote_copy(
            bsend.at[behind[d]], brecv.at[z], bs.at[d], br.at[d], device_id=zback[d], device_id_type=MESH
        )
    for d in OFFSETS:
        @pl.when(z + d >= NZ)
        def _(d=d):
            for copy in out[d]:
                copy.start()

    w = inv[...]
    wbuf[0, 0:128, :] = jnp.concatenate([w[0:128].astype(F32), w[128:256].astype(F32)], axis=1).astype(BF16)
    block = cpl[...].astype(F32)
    wbuf[0, 128:192, :] = jnp.concatenate([block, block.T], axis=1).astype(BF16)
    weights = {
        k: pltpu.make_async_remote_copy(
            wbuf.at[0], wbuf.at[k], ws.at[k], wr.at[k], device_id=wpeer[k], device_id_type=MESH
        )
        for k in wpeer
    }
    for want in (False, True):
        for k in weights:
            @pl.when(later[k] == want)
            def _(k=k, want=want):
                if want:
                    pl.semaphore_wait(wready.at[k], 1)
                weights[k].start()

    span = pl.ds(lax.rem(z + FAR[0], NZ - len(FAR) + 1), len(FAR))
    bundle = [
        pltpu.make_async_remote_copy(
            src.at[span], dst, bds.at[i], bdr.at[i], device_id=zpeer[GROUP], device_id_type=MESH
        )
        for i, (src, dst) in enumerate([(csend, crbuf), (send, rbuf)])
    ]
    origin = jnp.maximum(z - GROUP, 0)
    onward = {}
    for j in range(1, len(FAR) + 1):
        onward[j] = [
            pltpu.make_async_remote_copy(
                src.at[j - 1], dst.at[origin], ss.at[j - 1], rs.at[j + GROUP],
                device_id=zpeer[j], device_id_type=MESH,
            )
            for src, dst, ss, rs in ((crbuf, crecv, cfs, cr), (rbuf, recv, fs, pr))
        ]

    def send_on(d):
        higher = z + d < NZ

        @pl.when(jnp.logical_and(higher, jnp.logical_not(relayed)) if d in FAR else higher)
        def _():
            pl.semaphore_wait(ready.at[d], 1)
            for copy in out[d]:
                copy.start()

    for d in range(1, GROUP + 2):
        send_on(d)
        if d == GROUP:
            @pl.when(relayed)
            def _():
                for copy in bundle:
                    copy.start()

    @pl.when(relays)
    def _():
        for copy in bundle:
            copy.wait_recv()
        for j in reversed(onward):
            for copy in onward[j]:
                copy.start()

    for d in range(GROUP + 2, NZ):
        send_on(d)
    recv[z] = send[z]
    crecv[z] = csend[z]

    eye = iota((64, 128), 0) == iota((64, 128), 1)
    hsend[0] = jnp.sum(jnp.where(eye, field[:, 255:256], 0.0), axis=0, keepdims=True)
    hsend[1] = jnp.sum(jnp.where(eye, field[:, 0:1], 0.0), axis=0, keepdims=True)
    to_after = pltpu.make_async_remote_copy(
        hsend.at[0], hrecv.at[0], hs.at[0], hr.at[0], device_id=after, device_id_type=MESH
    )
    to_before = pltpu.make_async_remote_copy(
        hsend.at[1], hrecv.at[1], hs.at[1], hr.at[1], device_id=before, device_id_type=MESH
    )

    @pl.when(i_first)
    def _():
        pl.semaphore_wait(hready.at[0], 1)

    @pl.when(b_last)
    def _():
        pl.semaphore_wait(hready.at[1], 1)

    pl.when(has_after)(to_after.start)
    pl.when(has_before)(to_before.start)

    table[...] = coefficients(skin)
    total = skin[0]
    for k in range(1, 8):
        total = total + skin[k]

    for k in weights:
        weights[k].wait_recv()
    spreads = table[...]
    for start, stop in ((0, GROUP), (GROUP, NZ)):
        for d in OFFSETS:
            @pl.when(jnp.logical_and(behind[d] >= start, behind[d] < stop))
            def _(d=d):
                for copy in out[d]:
                    copy.wait_recv()
        n = stop - start
        answer = solve(
            recv[start:stop].reshape(n * 16, 128), crecv[start:stop].reshape(n, 128), wbuf, spreads, total
        )
        bsend[start:stop] = answer.reshape(n, 16, 128)
        for d in reversed(OFFSETS):
            @pl.when(jnp.logical_and(behind[d] >= start, behind[d] < stop))
            def _(d=d):
                back[d].start()
    brecv[z] = bsend[z]

    pl.when(has_before)(to_after.wait_recv)
    pl.when(has_after)(to_before.wait_recv)
    lane = iota((64, 256), 1)
    left = jnp.sum(jnp.where(jnp.logical_and(eye, has_before), hrecv[0], 0.0), axis=1, keepdims=True)
    right = jnp.sum(jnp.where(jnp.logical_and(eye, has_after), hrecv[1], 0.0), axis=1, keepdims=True)
    left = jnp.where(lane == 0, left, pltpu.roll(field, 1, 1))
    right = jnp.where(lane == 255, right, pltpu.roll(field, 255, 1))
    pot[...] = field + 0.25 * (left - 2.0 * field + right)

    for d in OFFSETS:
        back[d].wait_recv()
    got = mm(brecv[...].reshape(256, 128), place[...], TN)
    out_ref[...] = pot[...] - (got[0:64, 0:256] + got[64:128, 256:512])

    for k in weights:
        weights[k].wait_send()
    for d in OFFSETS:
        if d in FAR:
            @pl.when(jnp.logical_not(relayed))
            def _(d=d):
                for copy in out[d]:
                    copy.wait_send()

            @pl.when(relayed)
            def _(d=d):
                pl.semaphore_wait(ready.at[d], 1)
        else:
            for copy in out[d]:
                copy.wait_send()
        back[d].wait_send()

    @pl.when(relayed)
    def _():
        for copy in bundle:
            copy.wait_send()

    @pl.when(relays)
    def _():
        for j in onward:
            for copy in onward[j]:
                copy.wait_send()

    pl.when(has_after)(to_after.wait_send)
    pl.when(has_before)(to_before.wait_send)


def body(potential, types, saturation, pattern, inverses, coupling, skin):
    dma = pltpu.SemaphoreType.DMA
    return pl.pallas_call(
        kernel,
        out_shape=jax.ShapeDtypeStruct((64, 256), F32),
        in_specs=[pl.BlockSpec(memory_space=pl.ANY)] * 7,
        out_specs=pl.BlockSpec(memory_space=pltpu.VMEM),
        scratch_shapes=[
            pltpu.VMEM((64, 256), F32),
            pltpu.VMEM((1, 256), jnp.int32),
            pltpu.VMEM((1, 256), jnp.int32),
            pltpu.VMEM((1, 256), jnp.int32),
            pltpu.VMEM((256, 64), BF16),
            pltpu.VMEM((64, 64), BF16),
            pltpu.SMEM((8,), F32),
            pltpu.VMEM((256, 512), BF16),
            pltpu.VMEM((128, 768), BF16),
            pltpu.VMEM((8, 192, 128), BF16),
            pltpu.VMEM((NZ, 16, 128), BF16),
            pltpu.VMEM((NZ, 16, 128), BF16),
            pltpu.VMEM((NZ, 16, 128), BF16),
            pltpu.VMEM((NZ, 16, 128), BF16),
            pltpu.VMEM((NZ, 1, 128), F32),
            pltpu.VMEM((NZ, 1, 128), F32),
            pltpu.VMEM((2, 1, 128), F32),
            pltpu.VMEM((2, 1, 128), F32),
            pltpu.VMEM((len(FAR), 16, 128), BF16),
            pltpu.VMEM((len(FAR), 1, 128), F32),
            dma((7,)),
            pltpu.SemaphoreType.REGULAR((NZ,)),
            pltpu.SemaphoreType.REGULAR((8,)),
            pltpu.SemaphoreType.REGULAR((2,)),
            *[dma((NZ,)) for _ in range(6)],
            *[dma((8,)) for _ in range(2)],
            *[dma((2,)) for _ in range(4)],
            *[dma((len(FAR),)) for _ in range(2)],
        ],
        compiler_params=pltpu.CompilerParams(
            collective_id=0, has_side_effects=True, vmem_limit_bytes=64 * 1024 * 1024
        ),
        name="regroup_solve",
    )(
        potential,
        types.reshape(1, 256),
        saturation.reshape(1, 256),
        pattern.reshape(1, 256),
        inverses.reshape(256, 64),
        coupling.reshape(64, 64),
        skin,
    )


def solution(mesh):
    placed = (
        P(None, ("dom", "cell")),
        P(("dom", "cell"), None),
        P(("dom", "cell")),
        P(("dom", "cell")),
        P("dom", None, None, None),
        P("dom", None, None),
        P(),
    )
    return jax.shard_map(
        body, mesh=mesh, in_specs=placed, out_specs=P(None, ("dom", "cell")), check_vma=False
    )
```

```python
import functools

import jax
import jax.numpy as jnp
from jax import lax
from jax.experimental import pallas as pl
from jax.experimental.pallas import tpu as pltpu
from jax.sharding import PartitionSpec as P

MESH = pl.DeviceIdType.MESH
F32 = jnp.float32
BF16 = jnp.bfloat16
NY, NZ, NX = 4, 16, 4
NT = (((1,), (1,)), ((), ()))
TN = (((0,), (0,)), ((), ()))
NN = (((1,), (0,)), ((), ()))
GROUP, HALF = 4, NZ // 2
FAR = range(GROUP + 1, 2 * GROUP + 2)
OFFSETS = sorted(range(1, NZ), key=lambda d: min(d, NZ - d))


def mm(a, b, dims=NN):
    return lax.dot_general(a, b, dims, preferred_element_type=F32)


def iota(shape, axis):
    return lax.broadcasted_iota(jnp.int32, shape, axis)


def turn(x):
    return pltpu.roll(x, 64, 1)


def coefficients(skin):
    row, lane = iota((128, 128), 0), iota((128, 128), 1)
    place_in = row % 64
    bit, part, first = place_in % 13, place_in // 13, lane < 64

    def chosen(lower, upper):
        value = jnp.zeros((128, 128), F32)
        for i in range(13):
            a = skin[lower[i]] if i in lower else 0.0
            b = skin[upper[i]] if i in upper else 0.0
            value = jnp.where(bit == i, jnp.where(first, a, b), value)
        return value

    above, here = {i: i + 1 for i in range(7)}, {i: i for i in range(7)}
    above2, here2 = {7 + i: i + 2 for i in range(6)}, {7 + i: i for i in range(6)}
    value = jnp.concatenate([chosen(above, here), chosen(above2, above), chosen(here, here2)], axis=1)
    row, part = iota((128, 384), 0), (iota((128, 384), 0) % 64) // 13
    high = value.astype(BF16).astype(F32)
    rest = value - high
    middle = rest.astype(BF16).astype(F32)
    value = jnp.where(part == 0, high, jnp.where(part == 1, middle, jnp.where(part == 2, rest - middle, 0.0)))
    return jnp.concatenate([jnp.where(row // 64 == h, value, 0.0) for h in range(2)], axis=1).astype(BF16)


def product(a, c):
    low = iota((128, 128), 1) < 64
    a = a.astype(F32)
    levels = jnp.concatenate([jnp.where(low, a, 0.0), jnp.where(low, 0.0, a)], axis=0).astype(BF16)
    return mm(levels, jnp.concatenate([c, c], axis=0)).astype(BF16)


def solve(points, codes, wbuf, gbuf, table, total):
    n = codes.shape[0]
    rows = 16 * n
    row, lane = iota((rows, 128), 0), iota((rows, 128), 1)
    first = lane < 64
    pair = (row // 4) % 4
    spread = jnp.broadcast_to(codes.reshape(n, 1, 128), (n, 16, 128)).reshape(rows, 128)
    spread = jnp.where(lane % 64 == row % 16, spread, 0.0).astype(BF16)
    from_half, to = iota((128, 384), 0) // 64, iota((128, 384), 1)
    pick = (from_half == jnp.where(to < 256, to // 128, (to // 64) % 2)).astype(BF16)
    code = mm(spread, pick)
    bits = jnp.abs(code[:, 256:384]).astype(jnp.int32) - 1
    bit = (lane % 64) % 13
    mask = jnp.where(bit < 7, jnp.left_shift(1, bit), jnp.left_shift(3, jnp.maximum(bit - 7, 0)))
    held = jnp.logical_and(jnp.bitwise_and(bits, mask) == mask, lane % 64 < 39)
    factors = mm(held.astype(F32).astype(BF16), table)
    x = points.astype(F32)
    xr = turn(x)

    def by_pair(v):
        return jnp.concatenate([jnp.where(pair == p, v, 0.0).astype(BF16) for p in range(4)], axis=1)

    def doubled(v, lo):
        v = jnp.where(lo, v, 0.0)
        return v + turn(v)

    sides, ys, pqs, answers = [], [], [], []
    for h in range(2):
        c = code[:, h * 128 : (h + 1) * 128]
        sides.append((c < 0.0, (jnp.abs(c) > 128.0) != first))
        upper = sides[h][0]
        d2 = jnp.where(first, x, xr) if h == 0 else jnp.where(first, xr, x)
        blocks = jnp.concatenate([wbuf[h * 4 + p, 0:128, :] for p in range(4)], axis=1)
        ys.append(doubled(mm(by_pair(jnp.where(upper != first, d2, 0.0)), blocks, NT), sides[h][1]))

    def coupled(v, h):
        return mm(v, jnp.concatenate([gbuf[h * 4 + p] for p in range(4)], axis=1), NT)

    for h in range(2):
        upper, lo = sides[h]
        y = ys[h]
        both = jnp.concatenate([by_pair(jnp.where(first, y, 0.0)), by_pair(jnp.where(first, 0.0, y))], axis=0)
        got = coupled(both, h)
        pqs.append([doubled(jnp.where(upper, g[:, 128:256], g[:, 0:128]), lo) for g in (got[:rows], got[rows:])])
    for h in range(2):
        upper, lo = sides[h]
        f = [factors[:, h * 384 + i * 128 : h * 384 + (i + 1) * 128] for i in range(3)]
        mixed = f[0] * ys[h] - f[1] * pqs[h][0] - f[2] * pqs[h][1]
        got = coupled(by_pair(mixed), h)
        rest = doubled(jnp.where(upper, got[:, 128:256], got[:, 0:128]), lo)
        answers.append((total * ys[h] - rest) * 0.125)
    return jnp.where(first, answers[0], answers[1]).astype(BF16)


def kernel(
    pot_hbm, types_hbm, sat_hbm, pat_hbm, inv_hbm, cpl_hbm, skin_hbm, out_ref,
    pot, typ, sat, pat, inv, cpl, skin, place, table, wbuf, gbuf, send, recv, bsend, brecv, csend, crecv, hsend, hrecv, rbuf, crbuf,
    load_sem, ready, wready, hready, allhere, ps, pr, cs, cr, bs, br, ws, wr, hs, hr, bds, bdr, fs, cfs,
):
    dom, x = lax.axis_index("dom"), lax.axis_index("cell")
    c, z, y = lax.rem(dom, 2), lax.rem(dom // 2, NZ), dom // (2 * NZ)

    def at(yy, zz, cc):
        return ((yy * NZ + zz) * 2 + cc, x)

    ahead = {d: lax.rem(z + d, NZ) for d in OFFSETS}
    behind = {d: lax.rem(z + NZ - d, NZ) for d in OFFSETS}
    zpeer = {d: at(y, ahead[d], c) for d in OFFSETS}
    special = jnp.logical_and(x == 0, jnp.logical_and(y == 0, c == 0))
    shift = special.astype(jnp.int32)

    def turn_of(zz):
        return jnp.where(jnp.logical_and(special, zz == 0), NZ, jnp.minimum(zz, HALF))

    def slot_of(zz):
        return jnp.where(zz < HALF, lax.rem(zz + HALF - shift, HALF), zz)

    zback = {d: at(y, behind[d], c) for d in OFFSETS}
    mine, slot = turn_of(z), slot_of(z)
    ahead_later = {d: turn_of(ahead[d]) > mine for d in OFFSETS}
    ahead_alike = {d: turn_of(ahead[d]) == mine for d in OFFSETS}
    ahead_earlier = {d: turn_of(ahead[d]) < mine for d in OFFSETS}
    ahead_last = {d: turn_of(ahead[d]) == NZ for d in OFFSETS}
    behind_earlier = {d: turn_of(behind[d]) < mine for d in OFFSETS}
    n_behind = jnp.where(mine == NZ, NZ - 1, mine - shift)
    early, late = mine < HALF, mine == HALF
    wpeer, later = {}, {}
    for k in range(1, 4):
        yy = lax.rem(y + NY - k, NY)
        wpeer[k] = at(yy, z, c)
        later[k] = yy > y
    wpeer[4] = at(y, z, 1 - c)
    later[4] = c == 1
    index = dom * NX + x
    after = ((index + 1) // NX, lax.rem(index + 1, NX))
    before = ((index - 1 + NX) // NX - 1, lax.rem(index - 1 + NX, NX))
    has_after, has_before = index < 2 * NY * NZ * NX - 1, index > 0

    ahead_next = jnp.logical_or(x < NX - 1, jnp.logical_and(c == 1, z < NZ - 1))
    behind_next = jnp.logical_or(x > 0, jnp.logical_and(c == 0, z > 0))
    i_first = jnp.logical_and(has_after, ahead_next)
    i_last = jnp.logical_and(has_after, jnp.logical_not(ahead_next))
    b_first = jnp.logical_and(has_before, behind_next)
    b_last = jnp.logical_and(has_before, jnp.logical_not(behind_next))
    relayed = mine < GROUP
    relays = jnp.logical_and(jnp.logical_and(z >= GROUP, z < 2 * GROUP), turn_of(z - GROUP) < GROUP)

    barrier = pltpu.get_barrier_semaphore()
    for d in OFFSETS:
        @pl.when(ahead_later[d])
        def _(d=d):
            pl.semaphore_signal(barrier, inc=1, device_id=zpeer[d], device_id_type=MESH)
    for k in wpeer:
        @pl.when(later[k])
        def _(k=k):
            pl.semaphore_signal(barrier, inc=1, device_id=wpeer[k], device_id_type=MESH)

    @pl.when(i_first)
    def _():
        pl.semaphore_signal(barrier, inc=1, device_id=after, device_id_type=MESH)

    @pl.when(b_last)
    def _():
        pl.semaphore_signal(barrier, inc=1, device_id=before, device_id_type=MESH)

    loads = [
        pltpu.make_async_copy(src, dst, load_sem.at[i])
        for i, (src, dst) in enumerate([
            (types_hbm, typ), (sat_hbm, sat), (pat_hbm, pat), (pot_hbm, pot), (inv_hbm, inv), (cpl_hbm, cpl),
            (skin_hbm, skin),
        ])
    ]
    for load in loads:
        load.start()
    n_earlier = y + 1 - c + n_behind + b_first.astype(jnp.int32) + i_last.astype(jnp.int32)

    @pl.when(n_earlier > 0)
    def _():
        pl.semaphore_wait(barrier, n_earlier)

    for d in reversed(OFFSETS):
        @pl.when(behind_earlier[d])
        def _(d=d):
            pl.semaphore_signal(ready.at[d], inc=1, device_id=zback[d], device_id_type=MESH)
    for k in wpeer:
        @pl.when(jnp.logical_not(later[k]))
        def _(k=k):
            at_peer = k if k == 4 else 4 - k
            pl.semaphore_signal(wready.at[at_peer], inc=1, device_id=wpeer[k], device_id_type=MESH)

    @pl.when(i_last)
    def _():
        pl.semaphore_signal(hready.at[1], inc=1, device_id=after, device_id_type=MESH)

    @pl.when(b_first)
    def _():
        pl.semaphore_signal(hready.at[0], inc=1, device_id=before, device_id_type=MESH)

    loads[4].wait()
    loads[5].wait()
    w = inv[...]
    wbuf[0, 0:128, :] = jnp.concatenate([w[0:128].astype(F32), w[128:256].astype(F32)], axis=1).astype(BF16)
    block = cpl[...].astype(F32)
    wbuf[0, 128:192, :] = jnp.concatenate([block, block.T], axis=1).astype(BF16)
    weights = {
        k: pltpu.make_async_remote_copy(
            wbuf.at[max(k - 4, 0)], wbuf.at[k], ws.at[k], wr.at[k], device_id=wpeer[min(k, 4)], device_id_type=MESH
        )
        for k in range(1, 8)
    }
    for want in (False, True):
        for k in (2, 1, 3, 4):
            if want and k == 4:
                continue

            @pl.when(later[k] == want)
            def _(k=k, want=want):
                if want:
                    pl.semaphore_wait(wready.at[k], 1)
                weights[k].start()

    for i in (0, 1, 2, 3, 6):
        loads[i].wait()

    field = pot[...]
    t = typ[...]
    onehot = (iota((128, 256), 0) == t).astype(BF16)
    earlier = (iota((256, 256), 0) < iota((256, 256), 1)).astype(BF16)
    rank = jnp.sum(onehot.astype(F32) * mm(onehot, earlier), axis=0, keepdims=True).astype(jnp.int32)
    t_y, t_z, t_c = t // (2 * NZ), (t // 2) % NZ, t % 2
    row = t_z * 16 + ((t_y - y + NY) % NY) * 4 + rank
    side = (t_c - c + 2) % 2
    both = jnp.concatenate([jnp.where(side == 0, row, -1), jnp.where(side == 1, row, -1)], axis=1)
    place[...] = (iota((256, 512), 0) == both).astype(BF16)
    level, bits = sat[...], pat[...]
    code = (1 + (level % 2) * 128 + bits) * jnp.where(level >= 2, -1, 1)
    code = jnp.broadcast_to(code.astype(F32), (64, 256)).astype(BF16)
    drive = field.astype(BF16)
    none = jnp.zeros((64, 256), BF16)
    spread = jnp.concatenate(
        [jnp.concatenate([a, none], axis=1) if i == 0 else jnp.concatenate([none, a], axis=1)
         for a in (drive, code) for i in range(2)], axis=0
    )
    placed = mm(place[...], spread, NT)
    keep = iota((NZ, 16, 128), 2) % 64 == iota((NZ, 16, 128), 1)
    send[...] = placed[:, 0:128].astype(BF16).reshape(NZ, 16, 128)
    csend[...] = jnp.sum(jnp.where(keep, placed[:, 128:256].reshape(NZ, 16, 128), 0.0), axis=1, keepdims=True)

    out, back, backin = {}, {}, {}
    for d in OFFSETS:
        out[d] = [
            pltpu.make_async_remote_copy(
                csend.at[ahead[d]], crecv.at[slot], cs.at[d], cr.at[d], device_id=zpeer[d], device_id_type=MESH
            ),
            pltpu.make_async_remote_copy(
                send.at[ahead[d]], recv.at[slot], ps.at[d], pr.at[d], device_id=zpeer[d], device_id_type=MESH
            ),
        ]
        back[d] = pltpu.make_async_remote_copy(
            bsend.at[slot_of(behind[d])], brecv.at[z], bs.at[d], br.at[d], device_id=zback[d], device_id_type=MESH
        )
    for d in OFFSETS:
        @pl.when(ahead_earlier[d])
        def _(d=d):
            for copy in out[d]:
                copy.start()

    eye = iota((64, 128), 0) == iota((64, 128), 1)
    hsend[0] = jnp.sum(jnp.where(eye, field[:, 255:256], 0.0), axis=0, keepdims=True)
    hsend[1] = jnp.sum(jnp.where(eye, field[:, 0:1], 0.0), axis=0, keepdims=True)
    to_after = pltpu.make_async_remote_copy(
        hsend.at[0], hrecv.at[0], hs.at[0], hr.at[0], device_id=after, device_id_type=MESH
    )
    to_before = pltpu.make_async_remote_copy(
        hsend.at[1], hrecv.at[1], hs.at[1], hr.at[1], device_id=before, device_id_type=MESH
    )

    pl.when(i_last)(to_after.start)
    pl.when(b_first)(to_before.start)

    span = pl.ds(lax.rem(z + FAR[0], NZ - len(FAR) + 1), len(FAR))
    bundle = [
        pltpu.make_async_remote_copy(
            src.at[span], dst, bds.at[i], bdr.at[i], device_id=zpeer[GROUP], device_id_type=MESH
        )
        for i, (src, dst) in enumerate([(csend, crbuf), (send, rbuf)])
    ]
    from_slot = slot_of(jnp.maximum(z - GROUP, 0))
    onward = {}
    for j in range(1, len(FAR) + 1):
        onward[j] = [
            pltpu.make_async_remote_copy(
                src.at[j - 1], dst.at[from_slot], ss.at[j - 1], rs.at[j + GROUP],
                device_id=zpeer[j], device_id_type=MESH,
            )
            for src, dst, ss, rs in ((crbuf, crecv, cfs, cr), (rbuf, recv, fs, pr))
        ]

    def send_on(d):
        goes = jnp.logical_and(jnp.logical_and(early, ahead_later[d]), jnp.logical_not(ahead_last[d]))

        @pl.when(jnp.logical_and(goes, jnp.logical_not(relayed)) if d in FAR else goes)
        def _():
            pl.semaphore_wait(ready.at[d], 1)
            for copy in out[d]:
                copy.start()

    for d in (*range(1, GROUP + 2), *range(NZ - 1, FAR[-1], -1), *range(FAR[-1], GROUP + 1, -1)):
        send_on(d)
        if d == GROUP:
            @pl.when(relayed)
            def _():
                for copy in bundle:
                    copy.start()

        if d in onward:
            @pl.when(relays)
            def _(d=d):
                if d == 1:
                    for copy in bundle:
                        copy.wait_recv()
                for copy in onward[d]:
                    copy.start()

    @pl.when(z == HALF - 1)
    def _():
        for d in range(1, GROUP + 1):
            pl.semaphore_signal(allhere, inc=1, device_id=zpeer[d], device_id_type=MESH)

    @pl.when(z == 1)
    def _():
        for d in range(HALF - 1, FAR[-1] + 1):
            pl.semaphore_wait(ready.at[d], 1)
        for d in range(NZ - 2, NZ - 2 - GROUP, -1):
            pl.semaphore_signal(allhere, inc=1, device_id=zpeer[d], device_id_type=MESH)

    @pl.when(later[4])
    def _():
        pl.semaphore_wait(wready.at[4], 1)
        weights[4].start()

    recv[slot] = send[z]
    crecv[slot] = csend[z]

    @pl.when(i_first)
    def _():
        pl.semaphore_wait(hready.at[0], 1)
        to_after.start()

    table[...] = coefficients(skin)
    total = skin[0]
    for k in range(1, 8):
        total = total + skin[k]

    gbuf[0] = product(wbuf[0, 0:128, :], wbuf[0, 128:192, :])
    for k in (1, 3, 2):
        weights[k].wait_recv()
        weights[k + 4].start()
    for k in (1, 3, 2, 4, 5, 7, 6):
        if k >= 4:
            weights[k].wait_recv()
        gbuf[k] = product(wbuf[k, 0:128, :], wbuf[k, 128:192, :])

    spreads = table[...]
    for start, stop in ((0, GROUP), (GROUP, 2 * GROUP), (2 * GROUP, NZ)):
        for d in OFFSETS:
            @pl.when(jnp.logical_and(slot_of(behind[d]) >= start, slot_of(behind[d]) < stop))
            def _(d=d):
                for copy in out[d]:
                    copy.wait_recv()
        n = stop - start
        answer = solve(
            recv[start:stop].reshape(n * 16, 128), crecv[start:stop].reshape(n, 128), wbuf, gbuf, spreads, total
        )
        bsend[start:stop] = answer.reshape(n, 16, 128)
        for d in reversed(OFFSETS):
            @pl.when(jnp.logical_and(slot_of(behind[d]) >= start, slot_of(behind[d]) < stop))
            def _(d=d):
                back[d].start()
        if start == 0:
            @pl.when(late)
            def _():
                pl.semaphore_wait(allhere, 1)
                for d in OFFSETS:
                    @pl.when(ahead_alike[d])
                    def _(d=d):
                        for copy in out[d]:
                            copy.start()

            for d in OFFSETS:
                @pl.when(ahead_last[d])
                def _(d=d):
                    pl.semaphore_wait(ready.at[d], 1)
                    for copy in out[d]:
                        copy.start()
    brecv[z] = bsend[slot]

    @pl.when(b_last)
    def _():
        pl.semaphore_wait(hready.at[1], 1)
        to_before.start()

    pl.when(has_before)(to_after.wait_recv)
    pl.when(has_after)(to_before.wait_recv)
    lane = iota((64, 256), 1)
    left = jnp.sum(jnp.where(jnp.logical_and(eye, has_before), hrecv[0], 0.0), axis=1, keepdims=True)
    right = jnp.sum(jnp.where(jnp.logical_and(eye, has_after), hrecv[1], 0.0), axis=1, keepdims=True)
    left = jnp.where(lane == 0, left, pltpu.roll(field, 1, 1))
    right = jnp.where(lane == 255, right, pltpu.roll(field, 255, 1))
    pot[...] = field + 0.25 * (left - 2.0 * field + right)

    for d in OFFSETS:
        back[d].wait_recv()
    got = mm(brecv[...].reshape(256, 128), place[...], TN)
    out_ref[...] = pot[...] - (got[0:64, 0:256] + got[64:128, 256:512])

    for k in weights:
        weights[k].wait_send()
    for d in OFFSETS:
        if d in FAR:
            @pl.when(jnp.logical_not(relayed))
            def _(d=d):
                for copy in out[d]:
                    copy.wait_send()

            @pl.when(jnp.logical_and(relayed, z != 1) if d >= HALF - 1 else relayed)
            def _(d=d):
                pl.semaphore_wait(ready.at[d], 1)
        else:
            for copy in out[d]:
                copy.wait_send()
        back[d].wait_send()

    @pl.when(relayed)
    def _():
        for copy in bundle:
            copy.wait_send()

    @pl.when(relays)
    def _():
        for j in onward:
            for copy in onward[j]:
                copy.wait_send()

    pl.when(has_after)(to_after.wait_send)
    pl.when(has_before)(to_before.wait_send)


def body(potential, types, saturation, pattern, inverses, coupling, skin):
    dma = pltpu.SemaphoreType.DMA
    return pl.pallas_call(
        kernel,
        out_shape=jax.ShapeDtypeStruct((64, 256), F32),
        in_specs=[pl.BlockSpec(memory_space=pl.ANY)] * 7,
        out_specs=pl.BlockSpec(memory_space=pltpu.VMEM),
        scratch_shapes=[
            pltpu.VMEM((64, 256), F32),
            pltpu.VMEM((1, 256), jnp.int32),
            pltpu.VMEM((1, 256), jnp.int32),
            pltpu.VMEM((1, 256), jnp.int32),
            pltpu.VMEM((256, 64), BF16),
            pltpu.VMEM((64, 64), BF16),
            pltpu.SMEM((8,), F32),
            pltpu.VMEM((256, 512), BF16),
            pltpu.VMEM((128, 768), BF16),
            pltpu.VMEM((8, 192, 128), BF16),
            pltpu.VMEM((8, 256, 128), BF16),
            pltpu.VMEM((NZ, 16, 128), BF16),
            pltpu.VMEM((NZ, 16, 128), BF16),
            pltpu.VMEM((NZ, 16, 128), BF16),
            pltpu.VMEM((NZ, 16, 128), BF16),
            pltpu.VMEM((NZ, 1, 128), F32),
            pltpu.VMEM((NZ, 1, 128), F32),
            pltpu.VMEM((2, 1, 128), F32),
            pltpu.VMEM((2, 1, 128), F32),
            pltpu.VMEM((len(FAR), 16, 128), BF16),
            pltpu.VMEM((len(FAR), 1, 128), F32),
            dma((7,)),
            pltpu.SemaphoreType.REGULAR((NZ,)),
            pltpu.SemaphoreType.REGULAR((8,)),
            pltpu.SemaphoreType.REGULAR((2,)),
            pltpu.SemaphoreType.REGULAR,
            *[dma((NZ,)) for _ in range(6)],
            *[dma((8,)) for _ in range(2)],
            *[dma((2,)) for _ in range(4)],
            *[dma((len(FAR),)) for _ in range(2)],
        ],
        compiler_params=pltpu.CompilerParams(
            collective_id=0, has_side_effects=True, vmem_limit_bytes=64 * 1024 * 1024
        ),
        name="regroup_solve",
    )(
        potential,
        types.reshape(1, 256),
        saturation.reshape(1, 256),
        pattern.reshape(1, 256),
        inverses.reshape(256, 64),
        coupling.reshape(64, 64),
        skin,
    )


def solution(mesh):
    placed = (
        P(None, ("dom", "cell")),
        P(("dom", "cell"), None),
        P(("dom", "cell")),
        P(("dom", "cell")),
        P("dom", None, None, None),
        P("dom", None, None),
        P(),
    )
    return jax.shard_map(
        body, mesh=mesh, in_specs=placed, out_specs=P(None, ("dom", "cell")), check_vma=False
    )
```

```python
import functools

import jax
import jax.numpy as jnp
from jax import lax
from jax.experimental import pallas as pl
from jax.experimental.pallas import tpu as pltpu
from jax.sharding import PartitionSpec as P

MESH = pl.DeviceIdType.MESH
F32 = jnp.float32
BF16 = jnp.bfloat16
NY, NZ, NX = 4, 16, 4
NT = (((1,), (1,)), ((), ()))
TN = (((0,), (0,)), ((), ()))
NN = (((1,), (0,)), ((), ()))
GROUP, HALF = 4, NZ // 2
FAR = range(GROUP + 1, 2 * GROUP + 2)
OFFSETS = sorted(range(1, NZ), key=lambda d: min(d, NZ - d))


def mm(a, b, dims=NN):
    return lax.dot_general(a, b, dims, preferred_element_type=F32)


def iota(shape, axis):
    return lax.broadcasted_iota(jnp.int32, shape, axis)


def turn(x):
    return pltpu.roll(x, 64, 1)


def coefficients(skin):
    row, lane = iota((128, 128), 0), iota((128, 128), 1)
    place_in = row % 64
    bit, part, first = place_in % 13, place_in // 13, lane < 64

    def chosen(lower, upper):
        value = jnp.zeros((128, 128), F32)
        for i in range(13):
            a = skin[lower[i]] if i in lower else 0.0
            b = skin[upper[i]] if i in upper else 0.0
            value = jnp.where(bit == i, jnp.where(first, a, b), value)
        return value

    above, here = {i: i + 1 for i in range(7)}, {i: i for i in range(7)}
    above2, here2 = {7 + i: i + 2 for i in range(6)}, {7 + i: i for i in range(6)}
    value = jnp.concatenate([chosen(above, here), chosen(above2, above), chosen(here, here2)], axis=1)
    row, part = iota((128, 384), 0), (iota((128, 384), 0) % 64) // 13
    high = value.astype(BF16).astype(F32)
    rest = value - high
    middle = rest.astype(BF16).astype(F32)
    value = jnp.where(part == 0, high, jnp.where(part == 1, middle, jnp.where(part == 2, rest - middle, 0.0)))
    return jnp.concatenate([jnp.where(row // 64 == h, value, 0.0) for h in range(2)], axis=1).astype(BF16)


def product(a, c):
    low = iota((128, 128), 1) < 64
    a = a.astype(F32)
    levels = jnp.concatenate([jnp.where(low, a, 0.0), jnp.where(low, 0.0, a)], axis=0).astype(BF16)
    return mm(levels, jnp.concatenate([c, c], axis=0)).astype(BF16)


def solve(points, codes, wbuf, gbuf, table, total):
    n = codes.shape[0]
    rows = 16 * n
    row, lane = iota((rows, 128), 0), iota((rows, 128), 1)
    first = lane < 64
    pair = (row // 4) % 4
    spread = jnp.broadcast_to(codes.reshape(n, 1, 128), (n, 16, 128)).reshape(rows, 128)
    spread = jnp.where(lane % 64 == row % 16, spread, 0.0).astype(BF16)
    from_half, to = iota((128, 384), 0) // 64, iota((128, 384), 1)
    pick = (from_half == jnp.where(to < 256, to // 128, (to // 64) % 2)).astype(BF16)
    code = mm(spread, pick)
    bits = jnp.abs(code[:, 256:384]).astype(jnp.int32) - 1
    bit = (lane % 64) % 13
    mask = jnp.where(bit < 7, jnp.left_shift(1, bit), jnp.left_shift(3, jnp.maximum(bit - 7, 0)))
    held = jnp.logical_and(jnp.bitwise_and(bits, mask) == mask, lane % 64 < 39)
    factors = mm(held.astype(F32).astype(BF16), table)
    x = points.astype(F32)
    xr = turn(x)

    def by_pair(v):
        return jnp.concatenate([jnp.where(pair == p, v, 0.0).astype(BF16) for p in range(4)], axis=1)

    def doubled(v, lo):
        v = jnp.where(lo, v, 0.0)
        return v + turn(v)

    sides, ys, pqs, answers = [], [], [], []
    for h in range(2):
        c = code[:, h * 128 : (h + 1) * 128]
        sides.append((c < 0.0, (jnp.abs(c) > 128.0) != first))
        upper = sides[h][0]
        d2 = jnp.where(first, x, xr) if h == 0 else jnp.where(first, xr, x)
        blocks = jnp.concatenate([wbuf[h * 4 + p, 0:128, :] for p in range(4)], axis=1)
        ys.append(doubled(mm(by_pair(jnp.where(upper != first, d2, 0.0)), blocks, NT), sides[h][1]))

    def coupled(v, h):
        return mm(v, jnp.concatenate([gbuf[h * 4 + p] for p in range(4)], axis=1), NT)

    for h in range(2):
        upper, lo = sides[h]
        y = ys[h]
        both = jnp.concatenate([by_pair(jnp.where(first, y, 0.0)), by_pair(jnp.where(first, 0.0, y))], axis=0)
        got = coupled(both, h)
        pqs.append([doubled(jnp.where(upper, g[:, 128:256], g[:, 0:128]), lo) for g in (got[:rows], got[rows:])])
    for h in range(2):
        upper, lo = sides[h]
        f = [factors[:, h * 384 + i * 128 : h * 384 + (i + 1) * 128] for i in range(3)]
        mixed = f[0] * ys[h] - f[1] * pqs[h][0] - f[2] * pqs[h][1]
        got = coupled(by_pair(mixed), h)
        rest = doubled(jnp.where(upper, got[:, 128:256], got[:, 0:128]), lo)
        answers.append((total * ys[h] - rest) * 0.125)
    return jnp.where(first, answers[0], answers[1]).astype(BF16)


def kernel(
    pot_hbm, types_hbm, sat_hbm, pat_hbm, inv_hbm, cpl_hbm, skin_hbm, out_ref,
    pot, typ, sat, pat, inv, cpl, skin, place, table, wbuf, gbuf, send, recv, bsend, brecv, csend, crecv, hsend, hrecv, rbuf, crbuf,
    load_sem, ready, wready, hready, allhere, ps, pr, cs, cr, bs, br, ws, wr, hs, hr, bds, bdr, fs, cfs,
):
    dom, x = lax.axis_index("dom"), lax.axis_index("cell")
    c, z, y = lax.rem(dom, 2), lax.rem(dom // 2, NZ), dom // (2 * NZ)

    def at(yy, zz, cc):
        return ((yy * NZ + zz) * 2 + cc, x)

    ahead = {d: lax.rem(z + d, NZ) for d in OFFSETS}
    behind = {d: lax.rem(z + NZ - d, NZ) for d in OFFSETS}
    zpeer = {d: at(y, ahead[d], c) for d in OFFSETS}
    special = jnp.logical_and(x == 0, jnp.logical_and(y == 0, c == 0))
    shift = special.astype(jnp.int32)

    def turn_of(zz):
        return jnp.where(jnp.logical_and(special, zz == 0), NZ, jnp.minimum(zz, HALF))

    def slot_of(zz):
        return jnp.where(jnp.logical_and(special, zz == 0), HALF, zz + (zz >= HALF).astype(jnp.int32))

    zback = {d: at(y, behind[d], c) for d in OFFSETS}
    mine, slot = turn_of(z), slot_of(z)
    def apart(a, b):
        far = jnp.logical_and(b >= HALF, b < HALF + GROUP)
        return jnp.logical_and(special, jnp.logical_and(a == 0, far))

    def alike(zz):
        return jnp.logical_or(turn_of(zz) == mine, jnp.logical_or(apart(z, zz), apart(zz, z)))

    ahead_alike = {d: alike(ahead[d]) for d in OFFSETS}
    ahead_later = {d: jnp.logical_and(turn_of(ahead[d]) > mine, jnp.logical_not(ahead_alike[d])) for d in OFFSETS}
    ahead_earlier = {d: jnp.logical_and(turn_of(ahead[d]) < mine, jnp.logical_not(ahead_alike[d])) for d in OFFSETS}
    ahead_last = {d: jnp.logical_and(turn_of(ahead[d]) == NZ, jnp.logical_not(ahead_alike[d])) for d in OFFSETS}
    behind_earlier = {
        d: jnp.logical_and(turn_of(behind[d]) < mine, jnp.logical_not(alike(behind[d]))) for d in OFFSETS
    }
    n_behind = jnp.where(mine == NZ, NZ - 1 - GROUP, mine - shift)
    early, late, lone = mine < HALF, mine == HALF, mine == NZ
    wpeer, later = {}, {}
    for k in range(1, 4):
        yy = lax.rem(y + NY - k, NY)
        wpeer[k] = at(yy, z, c)
        later[k] = yy > y
    wpeer[4] = at(y, z, 1 - c)
    later[4] = c == 1
    index = dom * NX + x
    after = ((index + 1) // NX, lax.rem(index + 1, NX))
    before = ((index - 1 + NX) // NX - 1, lax.rem(index - 1 + NX, NX))
    has_after, has_before = index < 2 * NY * NZ * NX - 1, index > 0

    ahead_next = jnp.logical_or(x < NX - 1, jnp.logical_and(c == 1, z < NZ - 1))
    behind_next = jnp.logical_or(x > 0, jnp.logical_and(c == 0, z > 0))
    i_first = jnp.logical_and(has_after, ahead_next)
    i_last = jnp.logical_and(has_after, jnp.logical_not(ahead_next))
    b_first = jnp.logical_and(has_before, behind_next)
    b_last = jnp.logical_and(has_before, jnp.logical_not(behind_next))
    relayed = mine < GROUP
    relays = jnp.logical_and(jnp.logical_and(z >= GROUP, z < 2 * GROUP), turn_of(z - GROUP) < GROUP)

    barrier = pltpu.get_barrier_semaphore()
    for d in OFFSETS:
        @pl.when(ahead_later[d])
        def _(d=d):
            pl.semaphore_signal(barrier, inc=1, device_id=zpeer[d], device_id_type=MESH)
    for k in wpeer:
        @pl.when(later[k])
        def _(k=k):
            pl.semaphore_signal(barrier, inc=1, device_id=wpeer[k], device_id_type=MESH)

    @pl.when(i_first)
    def _():
        pl.semaphore_signal(barrier, inc=1, device_id=after, device_id_type=MESH)

    @pl.when(b_last)
    def _():
        pl.semaphore_signal(barrier, inc=1, device_id=before, device_id_type=MESH)

    loads = [
        pltpu.make_async_copy(src, dst, load_sem.at[i])
        for i, (src, dst) in enumerate([
            (types_hbm, typ), (sat_hbm, sat), (pat_hbm, pat), (pot_hbm, pot), (inv_hbm, inv), (cpl_hbm, cpl),
            (skin_hbm, skin),
        ])
    ]
    for load in loads:
        load.start()
    n_earlier = y + 1 - c + n_behind + b_first.astype(jnp.int32) + i_last.astype(jnp.int32)

    @pl.when(n_earlier > 0)
    def _():
        pl.semaphore_wait(barrier, n_earlier)

    for d in reversed(OFFSETS):
        @pl.when(behind_earlier[d])
        def _(d=d):
            pl.semaphore_signal(ready.at[d], inc=1, device_id=zback[d], device_id_type=MESH)
    for k in wpeer:
        @pl.when(jnp.logical_not(later[k]))
        def _(k=k):
            at_peer = k if k == 4 else 4 - k
            pl.semaphore_signal(wready.at[at_peer], inc=1, device_id=wpeer[k], device_id_type=MESH)

    @pl.when(i_last)
    def _():
        pl.semaphore_signal(hready.at[1], inc=1, device_id=after, device_id_type=MESH)

    @pl.when(b_first)
    def _():
        pl.semaphore_signal(hready.at[0], inc=1, device_id=before, device_id_type=MESH)

    loads[4].wait()
    loads[5].wait()
    w = inv[...]
    wbuf[0, 0:128, :] = jnp.concatenate([w[0:128].astype(F32), w[128:256].astype(F32)], axis=1).astype(BF16)
    block = cpl[...].astype(F32)
    wbuf[0, 128:192, :] = jnp.concatenate([block, block.T], axis=1).astype(BF16)
    weights = {
        k: pltpu.make_async_remote_copy(
            wbuf.at[max(k - 4, 0)], wbuf.at[k], ws.at[k], wr.at[k], device_id=wpeer[min(k, 4)], device_id_type=MESH
        )
        for k in range(1, 8)
    }
    for want in (False, True):
        for k in (2, 1, 3, 4):
            if want and k == 4:
                continue

            @pl.when(later[k] == want)
            def _(k=k, want=want):
                if want:
                    pl.semaphore_wait(wready.at[k], 1)
                weights[k].start()

    for i in (0, 1, 2, 3, 6):
        loads[i].wait()

    field = pot[...]
    t = typ[...]
    onehot = (iota((128, 256), 0) == t).astype(BF16)
    earlier = (iota((256, 256), 0) < iota((256, 256), 1)).astype(BF16)
    rank = jnp.sum(onehot.astype(F32) * mm(onehot, earlier), axis=0, keepdims=True).astype(jnp.int32)
    t_y, t_z, t_c = t // (2 * NZ), (t // 2) % NZ, t % 2
    row = t_z * 16 + ((t_y - y + NY) % NY) * 4 + rank
    side = (t_c - c + 2) % 2
    both = jnp.concatenate([jnp.where(side == 0, row, -1), jnp.where(side == 1, row, -1)], axis=1)
    place[...] = (iota((256, 512), 0) == both).astype(BF16)
    level, bits = sat[...], pat[...]
    code = (1 + (level % 2) * 128 + bits) * jnp.where(level >= 2, -1, 1)
    code = jnp.broadcast_to(code.astype(F32), (64, 256)).astype(BF16)
    drive = field.astype(BF16)
    none = jnp.zeros((64, 256), BF16)
    spread = jnp.concatenate(
        [jnp.concatenate([a, none], axis=1) if i == 0 else jnp.concatenate([none, a], axis=1)
         for a in (drive, code) for i in range(2)], axis=0
    )
    placed = mm(place[...], spread, NT)
    keep = iota((NZ, 16, 128), 2) % 64 == iota((NZ, 16, 128), 1)
    send[...] = placed[:, 0:128].astype(BF16).reshape(NZ, 16, 128)
    csend[...] = jnp.sum(jnp.where(keep, placed[:, 128:256].reshape(NZ, 16, 128), 0.0), axis=1, keepdims=True)

    out, back, backin = {}, {}, {}
    for d in OFFSETS:
        out[d] = [
            pltpu.make_async_remote_copy(
                csend.at[ahead[d]], crecv.at[slot], cs.at[d], cr.at[d], device_id=zpeer[d], device_id_type=MESH
            ),
            pltpu.make_async_remote_copy(
                send.at[ahead[d]], recv.at[slot], ps.at[d], pr.at[d], device_id=zpeer[d], device_id_type=MESH
            ),
        ]
        back[d] = pltpu.make_async_remote_copy(
            bsend.at[slot_of(behind[d])], brecv.at[z], bs.at[d], br.at[d], device_id=zback[d], device_id_type=MESH
        )
    for d in OFFSETS:
        @pl.when(ahead_earlier[d])
        def _(d=d):
            for copy in out[d]:
                copy.start()

    eye = iota((64, 128), 0) == iota((64, 128), 1)
    hsend[0] = jnp.sum(jnp.where(eye, field[:, 255:256], 0.0), axis=0, keepdims=True)
    hsend[1] = jnp.sum(jnp.where(eye, field[:, 0:1], 0.0), axis=0, keepdims=True)
    to_after = pltpu.make_async_remote_copy(
        hsend.at[0], hrecv.at[0], hs.at[0], hr.at[0], device_id=after, device_id_type=MESH
    )
    to_before = pltpu.make_async_remote_copy(
        hsend.at[1], hrecv.at[1], hs.at[1], hr.at[1], device_id=before, device_id_type=MESH
    )

    pl.when(i_last)(to_after.start)
    pl.when(b_first)(to_before.start)

    span = pl.ds(lax.rem(z + FAR[0], NZ - len(FAR) + 1), len(FAR))
    bundle = [
        pltpu.make_async_remote_copy(
            src.at[span], dst, bds.at[i], bdr.at[i], device_id=zpeer[GROUP], device_id_type=MESH
        )
        for i, (src, dst) in enumerate([(csend, crbuf), (send, rbuf)])
    ]
    from_slot = slot_of(jnp.maximum(z - GROUP, 0))
    onward = {}
    for j in range(1, len(FAR) + 1):
        onward[j] = [
            pltpu.make_async_remote_copy(
                src.at[j - 1], dst.at[from_slot], ss.at[j - 1], rs.at[j + GROUP],
                device_id=zpeer[j], device_id_type=MESH,
            )
            for src, dst, ss, rs in ((crbuf, crecv, cfs, cr), (rbuf, recv, fs, pr))
        ]

    def send_on(d):
        goes = jnp.logical_and(jnp.logical_and(early, ahead_later[d]), jnp.logical_not(ahead_last[d]))

        @pl.when(jnp.logical_and(goes, jnp.logical_not(relayed)) if d in FAR else goes)
        def _():
            pl.semaphore_wait(ready.at[d], 1)
            for copy in out[d]:
                copy.start()

    for d in (*range(1, GROUP + 2), *range(NZ - 1, FAR[-1], -1), *range(FAR[-1], GROUP + 1, -1)):
        send_on(d)
        if d == GROUP:
            @pl.when(relayed)
            def _():
                for copy in bundle:
                    copy.start()

        if d in onward:
            @pl.when(relays)
            def _(d=d):
                if d == 1:
                    for copy in bundle:
                        copy.wait_recv()
                for copy in onward[d]:
                    copy.start()

    def tell(when, at_offset, told):
        @pl.when(when)
        def _():
            @pl.when(special)
            def _():
                pl.semaphore_wait(ready.at[at_offset], 1)
                for copy in out[at_offset]:
                    copy.start()

            if told[0] != 1:
                for d in range(HALF - 1, FAR[-1] + 1):
                    pl.semaphore_wait(ready.at[d], 1)

                @pl.when(special)
                def _():
                    pl.semaphore_signal(allhere, inc=1, device_id=zpeer[at_offset], device_id_type=MESH)

            for d in told:
                pl.semaphore_signal(allhere, inc=1, device_id=zpeer[d], device_id_type=MESH)

    tell(z == HALF - 1, HALF + 1, range(1, GROUP + 1))
    tell(z == 1, NZ - 1, range(NZ - 2, NZ - 2 - GROUP, -1))

    def send_alike():
        pl.semaphore_wait(allhere, 1)
        for d in OFFSETS:
            @pl.when(ahead_alike[d])
            def _(d=d):
                for copy in out[d]:
                    copy.start()

    pl.when(lone)(send_alike)

    @pl.when(later[4])
    def _():
        pl.semaphore_wait(wready.at[4], 1)
        weights[4].start()

    empty = jnp.where(special, 0, HALF)
    recv[empty] = jnp.zeros((16, 128), BF16)
    crecv[empty] = jnp.zeros((1, 128), F32)
    recv[slot] = send[z]
    crecv[slot] = csend[z]

    @pl.when(i_first)
    def _():
        pl.semaphore_wait(hready.at[0], 1)
        to_after.start()

    @pl.when(jnp.logical_and(b_last, z > 0))
    def _():
        pl.semaphore_wait(hready.at[1], 1)
        to_before.start()

    table[...] = coefficients(skin)
    total = skin[0]
    for k in range(1, 8):
        total = total + skin[k]

    gbuf[0] = product(wbuf[0, 0:128, :], wbuf[0, 128:192, :])
    for k in (1, 3, 2):
        weights[k].wait_recv()
        weights[k + 4].start()
    for k in (1, 3, 2, 4, 5, 7, 6):
        if k >= 4:
            weights[k].wait_recv()
        gbuf[k] = product(wbuf[k, 0:128, :], wbuf[k, 128:192, :])

    spreads = table[...]
    for start, stop in ((0, GROUP), (GROUP, HALF + 1), (HALF + 1, NZ + 1)):
        for d in OFFSETS:
            @pl.when(jnp.logical_and(slot_of(behind[d]) >= start, slot_of(behind[d]) < stop))
            def _(d=d):
                for copy in out[d]:
                    copy.wait_recv()
        n = stop - start
        answer = solve(
            recv[start:stop].reshape(n * 16, 128), crecv[start:stop].reshape(n, 128), wbuf, gbuf, spreads, total
        )
        bsend[start:stop] = answer.reshape(n, 16, 128)
        for d in reversed(OFFSETS):
            @pl.when(jnp.logical_and(slot_of(behind[d]) >= start, slot_of(behind[d]) < stop))
            def _(d=d):
                back[d].start()
        if start == 0:
            pl.when(late)(send_alike)
            for d in OFFSETS:
                @pl.when(jnp.logical_and(ahead_last[d], jnp.logical_and(z != 1, z != HALF - 1)))
                def _(d=d):
                    pl.semaphore_wait(ready.at[d], 1)
                    for copy in out[d]:
                        copy.start()
    brecv[z] = bsend[slot]

    @pl.when(jnp.logical_and(b_last, z == 0))
    def _():
        pl.semaphore_wait(hready.at[1], 1)
        to_before.start()

    pl.when(has_before)(to_after.wait_recv)
    pl.when(has_after)(to_before.wait_recv)
    lane = iota((64, 256), 1)
    left = jnp.sum(jnp.where(jnp.logical_and(eye, has_before), hrecv[0], 0.0), axis=1, keepdims=True)
    right = jnp.sum(jnp.where(jnp.logical_and(eye, has_after), hrecv[1], 0.0), axis=1, keepdims=True)
    left = jnp.where(lane == 0, left, pltpu.roll(field, 1, 1))
    right = jnp.where(lane == 255, right, pltpu.roll(field, 255, 1))
    pot[...] = field + 0.25 * (left - 2.0 * field + right)

    for d in OFFSETS:
        back[d].wait_recv()
    got = mm(brecv[...].reshape(256, 128), place[...], TN)
    out_ref[...] = pot[...] - (got[0:64, 0:256] + got[64:128, 256:512])

    for k in weights:
        weights[k].wait_send()
    for d in OFFSETS:
        if d in FAR:
            @pl.when(jnp.logical_not(relayed))
            def _(d=d):
                for copy in out[d]:
                    copy.wait_send()

            @pl.when(jnp.logical_and(relayed, z != 1) if d >= HALF - 1 else relayed)
            def _(d=d):
                pl.semaphore_wait(ready.at[d], 1)
        else:
            for copy in out[d]:
                copy.wait_send()
        back[d].wait_send()

    @pl.when(relayed)
    def _():
        for copy in bundle:
            copy.wait_send()

    @pl.when(relays)
    def _():
        for j in onward:
            for copy in onward[j]:
                copy.wait_send()

    pl.when(has_after)(to_after.wait_send)
    pl.when(has_before)(to_before.wait_send)


def body(potential, types, saturation, pattern, inverses, coupling, skin):
    dma = pltpu.SemaphoreType.DMA
    return pl.pallas_call(
        kernel,
        out_shape=jax.ShapeDtypeStruct((64, 256), F32),
        in_specs=[pl.BlockSpec(memory_space=pl.ANY)] * 7,
        out_specs=pl.BlockSpec(memory_space=pltpu.VMEM),
        scratch_shapes=[
            pltpu.VMEM((64, 256), F32),
            pltpu.VMEM((1, 256), jnp.int32),
            pltpu.VMEM((1, 256), jnp.int32),
            pltpu.VMEM((1, 256), jnp.int32),
            pltpu.VMEM((256, 64), BF16),
            pltpu.VMEM((64, 64), BF16),
            pltpu.SMEM((8,), F32),
            pltpu.VMEM((256, 512), BF16),
            pltpu.VMEM((128, 768), BF16),
            pltpu.VMEM((8, 192, 128), BF16),
            pltpu.VMEM((8, 256, 128), BF16),
            pltpu.VMEM((NZ, 16, 128), BF16),
            pltpu.VMEM((NZ + 1, 16, 128), BF16),
            pltpu.VMEM((NZ + 1, 16, 128), BF16),
            pltpu.VMEM((NZ, 16, 128), BF16),
            pltpu.VMEM((NZ, 1, 128), F32),
            pltpu.VMEM((NZ + 1, 1, 128), F32),
            pltpu.VMEM((2, 1, 128), F32),
            pltpu.VMEM((2, 1, 128), F32),
            pltpu.VMEM((len(FAR), 16, 128), BF16),
            pltpu.VMEM((len(FAR), 1, 128), F32),
            dma((7,)),
            pltpu.SemaphoreType.REGULAR((NZ,)),
            pltpu.SemaphoreType.REGULAR((8,)),
            pltpu.SemaphoreType.REGULAR((2,)),
            pltpu.SemaphoreType.REGULAR,
            *[dma((NZ,)) for _ in range(6)],
            *[dma((8,)) for _ in range(2)],
            *[dma((2,)) for _ in range(4)],
            *[dma((len(FAR),)) for _ in range(2)],
        ],
        compiler_params=pltpu.CompilerParams(
            collective_id=0, has_side_effects=True, vmem_limit_bytes=32 * 1024 * 1024
        ),
        name="regroup_solve",
    )(
        *[
            pltpu.with_memory_space_constraint(array, pltpu.HBM)
            for array in (
                potential,
                types.reshape(1, 256),
                saturation.reshape(1, 256),
                pattern.reshape(1, 256),
                inverses.reshape(256, 64),
                coupling.reshape(64, 64),
                skin,
            )
        ]
    )


def solution(mesh):
    placed = (
        P(None, ("dom", "cell")),
        P(("dom", "cell"), None),
        P(("dom", "cell")),
        P(("dom", "cell")),
        P("dom", None, None, None),
        P("dom", None, None),
        P(),
    )
    return jax.shard_map(
        body, mesh=mesh, in_specs=placed, out_specs=P(None, ("dom", "cell")), check_vma=False
    )
```

```python
import functools

import jax
import jax.numpy as jnp
from jax import lax
from jax.experimental import pallas as pl
from jax.experimental.pallas import tpu as pltpu
from jax.sharding import PartitionSpec as P

MESH = pl.DeviceIdType.MESH
F32 = jnp.float32
BF16 = jnp.bfloat16
NY, NZ, NX = 4, 16, 4
NT = (((1,), (1,)), ((), ()))
TN = (((0,), (0,)), ((), ()))
NN = (((1,), (0,)), ((), ()))
GROUP, HALF = 4, NZ // 2
FAR = range(GROUP + 1, 2 * GROUP + 2)
OFFSETS = sorted(range(1, NZ), key=lambda d: min(d, NZ - d))


def mm(a, b, dims=NN):
    return lax.dot_general(a, b, dims, preferred_element_type=F32)


def iota(shape, axis):
    return lax.broadcasted_iota(jnp.int32, shape, axis)


def turn(x):
    return pltpu.roll(x, 64, 1)


def coefficients(skin):
    row, lane = iota((128, 128), 0), iota((128, 128), 1)
    place_in = row % 64
    bit, part, first = place_in % 13, place_in // 13, lane < 64

    def chosen(lower, upper):
        value = jnp.zeros((128, 128), F32)
        for i in range(13):
            a = skin[lower[i]] if i in lower else 0.0
            b = skin[upper[i]] if i in upper else 0.0
            value = jnp.where(bit == i, jnp.where(first, a, b), value)
        return value

    above, here = {i: i + 1 for i in range(7)}, {i: i for i in range(7)}
    above2, here2 = {7 + i: i + 2 for i in range(6)}, {7 + i: i for i in range(6)}
    value = jnp.concatenate([chosen(above, here), chosen(above2, above), chosen(here, here2)], axis=1)
    row, part = iota((128, 384), 0), (iota((128, 384), 0) % 64) // 13
    high = value.astype(BF16).astype(F32)
    rest = value - high
    middle = rest.astype(BF16).astype(F32)
    value = jnp.where(part == 0, high, jnp.where(part == 1, middle, jnp.where(part == 2, rest - middle, 0.0)))
    return jnp.concatenate([jnp.where(row // 64 == h, value, 0.0) for h in range(2)], axis=1).astype(BF16)


def product(a, c):
    low = iota((128, 128), 1) < 64
    a = a.astype(F32)
    levels = jnp.concatenate([jnp.where(low, a, 0.0), jnp.where(low, 0.0, a)], axis=0).astype(BF16)
    return mm(levels, jnp.concatenate([c, c], axis=0)).astype(BF16)


def solve(points, codes, wbuf, gbuf, table, total):
    n = codes.shape[0]
    rows = 16 * n
    row, lane = iota((rows, 128), 0), iota((rows, 128), 1)
    first = lane < 64
    pair = (row // 4) % 4
    spread = jnp.broadcast_to(codes.reshape(n, 1, 128), (n, 16, 128)).reshape(rows, 128)
    spread = jnp.where(lane % 64 == row % 16, spread, 0.0).astype(BF16)
    from_half, to = iota((128, 384), 0) // 64, iota((128, 384), 1)
    pick = (from_half == jnp.where(to < 256, to // 128, (to // 64) % 2)).astype(BF16)
    code = mm(spread, pick)
    bits = jnp.abs(code[:, 256:384]).astype(jnp.int32) - 1
    bit = (lane % 64) % 13
    mask = jnp.where(bit < 7, jnp.left_shift(1, bit), jnp.left_shift(3, jnp.maximum(bit - 7, 0)))
    held = jnp.logical_and(jnp.bitwise_and(bits, mask) == mask, lane % 64 < 39)
    factors = mm(held.astype(F32).astype(BF16), table)
    x = points.astype(F32)
    xr = turn(x)

    def by_pair(v):
        return jnp.concatenate([jnp.where(pair == p, v, 0.0).astype(BF16) for p in range(4)], axis=1)

    def doubled(v, lo):
        v = jnp.where(lo, v, 0.0)
        return v + turn(v)

    sides, ys, pqs, answers = [], [], [], []
    for h in range(2):
        c = code[:, h * 128 : (h + 1) * 128]
        sides.append((c < 0.0, (jnp.abs(c) > 128.0) != first))
        upper = sides[h][0]
        d2 = jnp.where(first, x, xr) if h == 0 else jnp.where(first, xr, x)
        blocks = jnp.concatenate([wbuf[h * 4 + p, 0:128, :] for p in range(4)], axis=1)
        ys.append(doubled(mm(by_pair(jnp.where(upper != first, d2, 0.0)), blocks, NT), sides[h][1]))

    def coupled(v, h):
        return mm(v, jnp.concatenate([gbuf[h * 4 + p] for p in range(4)], axis=1), NT)

    for h in range(2):
        upper, lo = sides[h]
        y = ys[h]
        both = jnp.concatenate([by_pair(jnp.where(first, y, 0.0)), by_pair(jnp.where(first, 0.0, y))], axis=0)
        got = coupled(both, h)
        pqs.append([doubled(jnp.where(upper, g[:, 128:256], g[:, 0:128]), lo) for g in (got[:rows], got[rows:])])
    for h in range(2):
        upper, lo = sides[h]
        f = [factors[:, h * 384 + i * 128 : h * 384 + (i + 1) * 128] for i in range(3)]
        mixed = f[0] * ys[h] - f[1] * pqs[h][0] - f[2] * pqs[h][1]
        got = coupled(by_pair(mixed), h)
        rest = doubled(jnp.where(upper, got[:, 128:256], got[:, 0:128]), lo)
        answers.append((total * ys[h] - rest) * 0.125)
    return jnp.where(first, answers[0], answers[1]).astype(BF16)


def kernel(
    pot_hbm, types_hbm, sat_hbm, pat_hbm, inv_hbm, cpl_hbm, skin_hbm, out_ref,
    pot, typ, sat, pat, inv, cpl, skin, place, table, wbuf, gbuf, send, recv, bsend, brecv, csend, crecv, hsend, hrecv, rbuf, crbuf,
    load_sem, ready, wready, hready, allhere, rowhere, ps, pr, cs, cr, bs, br, ws, wr, hs, hr, bds, bdr, fs, cfs,
):
    dom, x = lax.axis_index("dom"), lax.axis_index("cell")
    c, z, y = lax.rem(dom, 2), lax.rem(dom // 2, NZ), dom // (2 * NZ)

    def at(yy, zz, cc):
        return ((yy * NZ + zz) * 2 + cc, x)

    ahead = {d: lax.rem(z + d, NZ) for d in OFFSETS}
    behind = {d: lax.rem(z + NZ - d, NZ) for d in OFFSETS}
    zpeer = {d: at(y, ahead[d], c) for d in OFFSETS}
    special = jnp.logical_and(x == 0, jnp.logical_and(y == 0, c == 0))
    shift = special.astype(jnp.int32)

    def turn_of(zz):
        return jnp.where(jnp.logical_and(special, zz == 0), NZ, jnp.minimum(zz, HALF))

    def slot_of(zz):
        return jnp.where(jnp.logical_and(special, zz == 0), HALF, zz + (zz >= HALF) * 1)

    zback = {d: at(y, behind[d], c) for d in OFFSETS}
    mine, slot = turn_of(z), slot_of(z)
    def apart(a, b):
        far = jnp.logical_and(b >= HALF, b < HALF + GROUP)
        return jnp.logical_and(special, jnp.logical_and(a == 0, far))

    def alike(zz):
        return jnp.logical_or(turn_of(zz) == mine, jnp.logical_or(apart(z, zz), apart(zz, z)))

    ahead_alike = {d: alike(ahead[d]) for d in OFFSETS}
    ahead_later = {d: jnp.logical_and(turn_of(ahead[d]) > mine, jnp.logical_not(ahead_alike[d])) for d in OFFSETS}
    ahead_earlier = {d: jnp.logical_and(turn_of(ahead[d]) < mine, jnp.logical_not(ahead_alike[d])) for d in OFFSETS}
    ahead_last = {d: jnp.logical_and(turn_of(ahead[d]) == NZ, jnp.logical_not(ahead_alike[d])) for d in OFFSETS}
    behind_earlier = {
        d: jnp.logical_and(turn_of(behind[d]) < mine, jnp.logical_not(alike(behind[d]))) for d in OFFSETS
    }
    n_behind = jnp.where(mine == NZ, NZ - 1 - GROUP, mine - shift)
    early, late, lone = mine < HALF, mine == HALF, mine == NZ
    wpeer, later = {}, {}
    for k in range(1, 4):
        yy = lax.rem(y + NY - k, NY)
        wpeer[k] = at(yy, z, c)
        later[k] = yy > y
    wpeer[4] = at(y, z, 1 - c)
    later[4] = c == 1
    index = dom * NX + x
    after = ((index + 1) // NX, lax.rem(index + 1, NX))
    before = ((index - 1 + NX) // NX - 1, lax.rem(index - 1 + NX, NX))
    has_after, has_before = index < 2 * NY * NZ * NX - 1, index > 0

    ahead_next = jnp.logical_or(x < NX - 1, jnp.logical_and(c == 1, z < NZ - 1))
    behind_next = jnp.logical_or(x > 0, jnp.logical_and(c == 0, z > 0))
    part_after = jnp.logical_and(jnp.logical_and(x == NX - 1, c == 1), jnp.logical_and(z > 0, z < NZ - 1))
    part_before = jnp.logical_and(jnp.logical_and(x == 0, c == 0), z > 1)
    tells_after = jnp.logical_and(jnp.logical_and(x == NX - 1, c == 1), z == 0)
    tells_before = jnp.logical_and(jnp.logical_and(x == 0, c == 0), z == 1)
    i_first = jnp.logical_and(has_after, jnp.logical_and(ahead_next, jnp.logical_not(part_after)))
    i_last = jnp.logical_and(has_after, jnp.logical_not(ahead_next))
    b_first = jnp.logical_and(has_before, jnp.logical_and(behind_next, jnp.logical_not(part_before)))
    b_last = jnp.logical_and(has_before, jnp.logical_not(behind_next))
    relayed = mine < GROUP
    relays = jnp.logical_and(jnp.logical_and(z >= GROUP, z < 2 * GROUP), turn_of(z - GROUP) < GROUP)

    barrier = pltpu.get_barrier_semaphore()
    for d in OFFSETS:
        @pl.when(ahead_later[d])
        def _(d=d):
            pl.semaphore_signal(barrier, inc=1, device_id=zpeer[d], device_id_type=MESH)
    for k in wpeer:
        @pl.when(later[k])
        def _(k=k):
            pl.semaphore_signal(barrier, inc=1, device_id=wpeer[k], device_id_type=MESH)

    @pl.when(i_first)
    def _():
        pl.semaphore_signal(barrier, inc=1, device_id=after, device_id_type=MESH)

    @pl.when(b_last)
    def _():
        pl.semaphore_signal(barrier, inc=1, device_id=before, device_id_type=MESH)

    loads = [
        pltpu.make_async_copy(src, dst, load_sem.at[i])
        for i, (src, dst) in enumerate([
            (types_hbm, typ), (sat_hbm, sat), (pat_hbm, pat), (pot_hbm, pot), (inv_hbm, inv), (cpl_hbm, cpl),
            (skin_hbm, skin),
        ])
    ]
    for load in loads:
        load.start()
    n_earlier = y + 1 - c + n_behind + b_first.astype(jnp.int32) + i_last.astype(jnp.int32)

    @pl.when(n_earlier > 0)
    def _():
        pl.semaphore_wait(barrier, n_earlier)

    for d in reversed(OFFSETS):
        @pl.when(behind_earlier[d])
        def _(d=d):
            pl.semaphore_signal(ready.at[d], inc=1, device_id=zback[d], device_id_type=MESH)
    for k in wpeer:
        @pl.when(jnp.logical_not(later[k]))
        def _(k=k):
            at_peer = k if k == 4 else 4 - k
            pl.semaphore_signal(wready.at[at_peer], inc=1, device_id=wpeer[k], device_id_type=MESH)

    @pl.when(i_last)
    def _():
        pl.semaphore_signal(hready.at[1], inc=1, device_id=after, device_id_type=MESH)

    @pl.when(b_first)
    def _():
        pl.semaphore_signal(hready.at[0], inc=1, device_id=before, device_id_type=MESH)

    loads[4].wait()
    loads[5].wait()
    w = inv[...]
    wbuf[0, 0:128, :] = jnp.concatenate([w[0:128].astype(F32), w[128:256].astype(F32)], axis=1).astype(BF16)
    block = cpl[...].astype(F32)
    wbuf[0, 128:192, :] = jnp.concatenate([block, block.T], axis=1).astype(BF16)
    weights = {
        k: pltpu.make_async_remote_copy(
            wbuf.at[max(k - 4, 0)], wbuf.at[k], ws.at[k], wr.at[k], device_id=wpeer[min(k, 4)], device_id_type=MESH
        )
        for k in range(1, 8)
    }
    for want in (False, True):
        for k in (2, 1, 3, 4):
            if want and k == 4:
                continue

            @pl.when(later[k] == want)
            def _(k=k, want=want):
                if want:
                    pl.semaphore_wait(wready.at[k], 1)
                weights[k].start()

    for i in (0, 1, 2, 3, 6):
        loads[i].wait()

    field = pot[...]
    t = typ[...]
    onehot = (iota((128, 256), 0) == t).astype(BF16)
    earlier = (iota((256, 256), 0) < iota((256, 256), 1)).astype(BF16)
    rank = jnp.sum(onehot.astype(F32) * mm(onehot, earlier), axis=0, keepdims=True).astype(jnp.int32)
    t_y, t_z, t_c = t // (2 * NZ), (t // 2) % NZ, t % 2
    row = t_z * 16 + ((t_y - y + NY) % NY) * 4 + rank
    side = (t_c - c + 2) % 2
    both = jnp.concatenate([jnp.where(side == 0, row, -1), jnp.where(side == 1, row, -1)], axis=1)
    place[...] = (iota((256, 512), 0) == both).astype(BF16)
    level, bits = sat[...], pat[...]
    code = (1 + (level % 2) * 128 + bits) * jnp.where(level >= 2, -1, 1)
    code = jnp.broadcast_to(code.astype(F32), (64, 256)).astype(BF16)
    drive = field.astype(BF16)
    none = jnp.zeros((64, 256), BF16)
    spread = jnp.concatenate(
        [jnp.concatenate([a, none], axis=1) if i == 0 else jnp.concatenate([none, a], axis=1)
         for a in (drive, code) for i in range(2)], axis=0
    )
    placed = mm(place[...], spread, NT)
    keep = iota((NZ, 16, 128), 2) % 64 == iota((NZ, 16, 128), 1)
    send[...] = placed[:, 0:128].astype(BF16).reshape(NZ, 16, 128)
    csend[...] = jnp.sum(jnp.where(keep, placed[:, 128:256].reshape(NZ, 16, 128), 0.0), axis=1, keepdims=True)

    out, back, backin = {}, {}, {}
    for d in OFFSETS:
        out[d] = [
            pltpu.make_async_remote_copy(
                csend.at[ahead[d]], crecv.at[slot], cs.at[d], cr.at[d], device_id=zpeer[d], device_id_type=MESH
            ),
            pltpu.make_async_remote_copy(
                send.at[ahead[d]], recv.at[slot], ps.at[d], pr.at[d], device_id=zpeer[d], device_id_type=MESH
            ),
        ]
        back[d] = pltpu.make_async_remote_copy(
            bsend.at[slot_of(behind[d])], brecv.at[z], bs.at[d], br.at[d], device_id=zback[d], device_id_type=MESH
        )
    for d in OFFSETS:
        @pl.when(ahead_earlier[d])
        def _(d=d):
            for copy in out[d]:
                copy.start()

    eye = iota((64, 128), 0) == iota((64, 128), 1)
    hsend[0] = jnp.sum(jnp.where(eye, field[:, 255:256], 0.0), axis=0, keepdims=True)
    hsend[1] = jnp.sum(jnp.where(eye, field[:, 0:1], 0.0), axis=0, keepdims=True)
    to_after = pltpu.make_async_remote_copy(
        hsend.at[0], hrecv.at[0], hs.at[0], hr.at[0], device_id=after, device_id_type=MESH
    )
    to_before = pltpu.make_async_remote_copy(
        hsend.at[1], hrecv.at[1], hs.at[1], hr.at[1], device_id=before, device_id_type=MESH
    )

    pl.when(i_last)(to_after.start)
    pl.when(b_first)(to_before.start)

    span = pl.ds(lax.rem(z + FAR[0], NZ - len(FAR) + 1), len(FAR))
    bundle = [
        pltpu.make_async_remote_copy(
            src.at[span], dst, bds.at[i], bdr.at[i], device_id=zpeer[GROUP], device_id_type=MESH
        )
        for i, (src, dst) in enumerate([(csend, crbuf), (send, rbuf)])
    ]
    from_slot = slot_of(jnp.maximum(z - GROUP, 0))
    onward = {}
    for j in range(1, len(FAR) + 1):
        onward[j] = [
            pltpu.make_async_remote_copy(
                src.at[j - 1], dst.at[from_slot], ss.at[j - 1], rs.at[j + GROUP],
                device_id=zpeer[j], device_id_type=MESH,
            )
            for src, dst, ss, rs in ((crbuf, crecv, cfs, cr), (rbuf, recv, fs, pr))
        ]

    def send_on(d):
        goes = jnp.logical_and(jnp.logical_and(early, ahead_later[d]), jnp.logical_not(ahead_last[d]))

        @pl.when(jnp.logical_and(goes, jnp.logical_not(relayed)) if d in FAR else goes)
        def _():
            pl.semaphore_wait(ready.at[d], 1)
            for copy in out[d]:
                copy.start()

    for d in (*range(1, GROUP + 2), *range(NZ - 1, FAR[-1], -1), *range(FAR[-1], GROUP + 1, -1)):
        send_on(d)
        if d == GROUP:
            @pl.when(relayed)
            def _():
                for copy in bundle:
                    copy.start()

        if d in onward:
            @pl.when(relays)
            def _(d=d):
                if d == 1:
                    for copy in bundle:
                        copy.wait_recv()
                for copy in onward[d]:
                    copy.start()

    @pl.when(relayed)
    def _():
        for d in FAR:
            pl.semaphore_wait(ready.at[d], 1)

    def tell(when, at_offset, told):
        @pl.when(when)
        def _():
            @pl.when(special)
            def _():
                pl.semaphore_wait(ready.at[at_offset], 1)
                for copy in out[at_offset]:
                    copy.start()

            if told[0] != 1:
                @pl.when(special)
                def _():
                    pl.semaphore_signal(allhere, inc=1, device_id=zpeer[at_offset], device_id_type=MESH)

            for d in told:
                pl.semaphore_signal(allhere, inc=1, device_id=zpeer[d], device_id_type=MESH)

    tell(z == HALF - 1, HALF + 1, range(1, GROUP + 1))
    tell(z == 1, NZ - 1, range(NZ - 2, NZ - 2 - GROUP, -1))

    def send_alike():
        pl.semaphore_wait(allhere, 1)
        for d in OFFSETS:
            @pl.when(ahead_alike[d])
            def _(d=d):
                for copy in out[d]:
                    copy.start()

    pl.when(lone)(send_alike)

    @pl.when(later[4])
    def _():
        pl.semaphore_wait(wready.at[4], 1)
        weights[4].start()

    empty = jnp.where(special, 0, HALF)
    recv[empty] = jnp.zeros((16, 128), BF16)
    crecv[empty] = jnp.zeros((1, 128), F32)
    recv[slot] = send[z]
    crecv[slot] = csend[z]

    @pl.when(i_first)
    def _():
        pl.semaphore_wait(hready.at[0], 1)
        to_after.start()

    @pl.when(jnp.logical_and(b_last, z > 0))
    def _():
        pl.semaphore_wait(hready.at[1], 1)
        to_before.start()

    @pl.when(tells_after)
    def _():
        pl.semaphore_signal(rowhere, inc=1, device_id=after, device_id_type=MESH)

    @pl.when(tells_before)
    def _():
        pl.semaphore_signal(rowhere, inc=1, device_id=before, device_id_type=MESH)

    table[...] = coefficients(skin)
    total = skin[0]
    for k in range(1, 8):
        total = total + skin[k]

    gbuf[0] = product(wbuf[0, 0:128, :], wbuf[0, 128:192, :])
    for k in (1, 3, 2):
        weights[k].wait_recv()
        weights[k + 4].start()
    for k in (1, 3, 2, 4, 5, 7, 6):
        if k >= 4:
            weights[k].wait_recv()
        gbuf[k] = product(wbuf[k, 0:128, :], wbuf[k, 128:192, :])

    spreads = table[...]
    for start, stop in ((0, GROUP), (GROUP, HALF + 1), (HALF + 1, NZ + 1)):
        sources = [j for j in range(NZ) if start <= j + (j >= HALF) < stop] + ([0] if start == GROUP else [])
        apply = {j: (special if start == GROUP else jnp.logical_not(special)) if j == 0 else True for j in sources}
        for j in sources:
            @pl.when(jnp.logical_and(z != j, apply[j]))
            def _(j=j):
                d = lax.rem(z - j + NZ, NZ)
                for src, dst, ss, rs in ((csend, crecv, cs, cr), (send, recv, ps, pr)):
                    pltpu.make_async_remote_copy(
                        src.at[j], dst.at[j], ss.at[d], rs.at[d], device_id=at(y, j, c), device_id_type=MESH
                    ).wait_recv()

        n = stop - start
        answer = solve(
            recv[start:stop].reshape(n * 16, 128), crecv[start:stop].reshape(n, 128), wbuf, gbuf, spreads, total
        )
        bsend[start:stop] = answer.reshape(n, 16, 128)
        for j in sources:
            @pl.when(jnp.logical_and(z != j, apply[j]))
            def _(j=j):
                d = lax.rem(z - j + NZ, NZ)
                pltpu.make_async_remote_copy(
                    bsend.at[slot_of(j)], brecv.at[z], bs.at[d], br.at[d], device_id=at(y, j, c), device_id_type=MESH
                ).start()

        if start == 0:
            pl.when(late)(send_alike)

            @pl.when(jnp.logical_or(tells_after, tells_before))
            def _():
                pl.semaphore_wait(rowhere, 1)
                for d in range(1, NZ - 1):
                    pl.semaphore_signal(rowhere, inc=1, device_id=zpeer[d], device_id_type=MESH)

            for d in OFFSETS:
                @pl.when(jnp.logical_and(ahead_last[d], jnp.logical_and(z != 1, z != HALF - 1)))
                def _(d=d):
                    pl.semaphore_wait(ready.at[d], 1)
                    for copy in out[d]:
                        copy.start()
    brecv[z] = bsend[slot]

    @pl.when(jnp.logical_and(b_last, z == 0))
    def _():
        pl.semaphore_wait(hready.at[1], 1)
        to_before.start()

    @pl.when(part_after)
    def _():
        pl.semaphore_wait(rowhere, 1)
        to_after.start()

    @pl.when(part_before)
    def _():
        pl.semaphore_wait(rowhere, 1)
        to_before.start()

    pl.when(has_before)(to_after.wait_recv)
    pl.when(has_after)(to_before.wait_recv)
    lane = iota((64, 256), 1)
    left = jnp.sum(jnp.where(jnp.logical_and(eye, has_before), hrecv[0], 0.0), axis=1, keepdims=True)
    right = jnp.sum(jnp.where(jnp.logical_and(eye, has_after), hrecv[1], 0.0), axis=1, keepdims=True)
    left = jnp.where(lane == 0, left, pltpu.roll(field, 1, 1))
    right = jnp.where(lane == 255, right, pltpu.roll(field, 255, 1))
    pot[...] = field + 0.25 * (left - 2.0 * field + right)

    for k in weights:
        weights[k].wait_send()
    for d in OFFSETS:
        if d in FAR:
            @pl.when(jnp.logical_not(relayed))
            def _(d=d):
                for copy in out[d]:
                    copy.wait_send()
        else:
            for copy in out[d]:
                copy.wait_send()
        back[d].wait_send()

    @pl.when(relayed)
    def _():
        for copy in bundle:
            copy.wait_send()

    @pl.when(relays)
    def _():
        for j in onward:
            for copy in onward[j]:
                copy.wait_send()

    pl.when(has_after)(to_after.wait_send)
    pl.when(has_before)(to_before.wait_send)

    for d in OFFSETS:
        back[d].wait_recv()
    got = mm(brecv[...].reshape(256, 128), place[...], TN)
    out_ref[...] = pot[...] - (got[0:64, 0:256] + got[64:128, 256:512])


def body(potential, types, saturation, pattern, inverses, coupling, skin):
    dma = pltpu.SemaphoreType.DMA
    return pl.pallas_call(
        kernel,
        out_shape=jax.ShapeDtypeStruct((64, 256), F32),
        in_specs=[pl.BlockSpec(memory_space=pl.ANY)] * 7,
        out_specs=pl.BlockSpec(memory_space=pltpu.VMEM),
        scratch_shapes=[
            pltpu.VMEM((64, 256), F32),
            pltpu.VMEM((1, 256), jnp.int32),
            pltpu.VMEM((1, 256), jnp.int32),
            pltpu.VMEM((1, 256), jnp.int32),
            pltpu.VMEM((256, 64), BF16),
            pltpu.VMEM((64, 64), BF16),
            pltpu.SMEM((8,), F32),
            pltpu.VMEM((256, 512), BF16),
            pltpu.VMEM((128, 768), BF16),
            pltpu.VMEM((8, 192, 128), BF16),
            pltpu.VMEM((8, 256, 128), BF16),
            pltpu.VMEM((NZ, 16, 128), BF16),
            pltpu.VMEM((NZ + 1, 16, 128), BF16),
            pltpu.VMEM((NZ + 1, 16, 128), BF16),
            pltpu.VMEM((NZ, 16, 128), BF16),
            pltpu.VMEM((NZ, 1, 128), F32),
            pltpu.VMEM((NZ + 1, 1, 128), F32),
            pltpu.VMEM((2, 1, 128), F32),
            pltpu.VMEM((2, 1, 128), F32),
            pltpu.VMEM((len(FAR), 16, 128), BF16),
            pltpu.VMEM((len(FAR), 1, 128), F32),
            dma((7,)),
            pltpu.SemaphoreType.REGULAR((NZ,)),
            pltpu.SemaphoreType.REGULAR((8,)),
            pltpu.SemaphoreType.REGULAR((2,)),
            pltpu.SemaphoreType.REGULAR,
            pltpu.SemaphoreType.REGULAR,
            *[dma((NZ,)) for _ in range(6)],
            *[dma((8,)) for _ in range(2)],
            *[dma((2,)) for _ in range(4)],
            *[dma((len(FAR),)) for _ in range(2)],
        ],
        compiler_params=pltpu.CompilerParams(
            collective_id=0, has_side_effects=True, vmem_limit_bytes=32 * 1024 * 1024
        ),
        name="regroup_solve",
    )(
        *[
            pltpu.with_memory_space_constraint(array, pltpu.HBM)
            for array in (
                potential,
                types.reshape(1, 256),
                saturation.reshape(1, 256),
                pattern.reshape(1, 256),
                inverses.reshape(256, 64),
                coupling.reshape(64, 64),
                skin,
            )
        ]
    )


def solution(mesh):
    placed = (
        P(None, ("dom", "cell")),
        P(("dom", "cell"), None),
        P(("dom", "cell")),
        P(("dom", "cell")),
        P("dom", None, None, None),
        P("dom", None, None),
        P(),
    )
    return jax.shard_map(
        body, mesh=mesh, in_specs=placed, out_specs=P(None, ("dom", "cell")), check_vma=False
    )
```

```python
import functools

import jax
import jax.numpy as jnp
from jax import lax
from jax.experimental import pallas as pl
from jax.experimental.pallas import tpu as pltpu
from jax.sharding import PartitionSpec as P

MESH = pl.DeviceIdType.MESH
F32 = jnp.float32
BF16 = jnp.bfloat16
NY, NZ, NX = 4, 16, 4
NT = (((1,), (1,)), ((), ()))
TN = (((0,), (0,)), ((), ()))
NN = (((1,), (0,)), ((), ()))
GROUP, HALF = 4, NZ // 2
FAR = range(GROUP + 1, 2 * GROUP + 2)
OFFSETS = sorted(range(1, NZ), key=lambda d: min(d, NZ - d))


def mm(a, b, dims=NN):
    return lax.dot_general(a, b, dims, preferred_element_type=F32)


def iota(shape, axis):
    return lax.broadcasted_iota(jnp.int32, shape, axis)


def turn(x):
    return pltpu.roll(x, 64, 1)


def coefficients(skin):
    row, lane = iota((128, 128), 0), iota((128, 128), 1)
    place_in = row % 64
    bit, part, first = place_in % 13, place_in // 13, lane < 64

    def chosen(lower, upper):
        value = jnp.zeros((128, 128), F32)
        for i in range(13):
            a = skin[lower[i]] if i in lower else 0.0
            b = skin[upper[i]] if i in upper else 0.0
            value = jnp.where(bit == i, jnp.where(first, a, b), value)
        return value

    above, here = {i: i + 1 for i in range(7)}, {i: i for i in range(7)}
    above2, here2 = {7 + i: i + 2 for i in range(6)}, {7 + i: i for i in range(6)}
    value = jnp.concatenate([chosen(above, here), chosen(above2, above), chosen(here, here2)], axis=1)
    row, part = iota((128, 384), 0), (iota((128, 384), 0) % 64) // 13
    high = value.astype(BF16).astype(F32)
    rest = value - high
    middle = rest.astype(BF16).astype(F32)
    value = jnp.where(part == 0, high, jnp.where(part == 1, middle, jnp.where(part == 2, rest - middle, 0.0)))
    return jnp.concatenate([jnp.where(row // 64 == h, value, 0.0) for h in range(2)], axis=1).astype(BF16)


def product(a, c):
    low = iota((128, 128), 1) < 64
    a = a.astype(F32)
    levels = jnp.concatenate([jnp.where(low, a, 0.0), jnp.where(low, 0.0, a)], axis=0).astype(BF16)
    return mm(levels, jnp.concatenate([c, c], axis=0)).astype(BF16)


def solve(points, codes, wbuf, gbuf, table, total):
    n = codes.shape[0]
    rows = 16 * n
    row, lane = iota((rows, 128), 0), iota((rows, 128), 1)
    first = lane < 64
    pair = (row // 4) % 4
    spread = jnp.broadcast_to(codes.reshape(n, 1, 128), (n, 16, 128)).reshape(rows, 128)
    spread = jnp.where(lane % 64 == row % 16, spread, 0.0).astype(BF16)
    from_half, to = iota((128, 384), 0) // 64, iota((128, 384), 1)
    pick = (from_half == jnp.where(to < 256, to // 128, (to // 64) % 2)).astype(BF16)
    code = mm(spread, pick)
    bits = jnp.abs(code[:, 256:384]).astype(jnp.int32) - 1
    bit = (lane % 64) % 13
    mask = jnp.where(bit < 7, jnp.left_shift(1, bit), jnp.left_shift(3, jnp.maximum(bit - 7, 0)))
    held = jnp.logical_and(jnp.bitwise_and(bits, mask) == mask, lane % 64 < 39)
    factors = mm(held.astype(F32).astype(BF16), table)
    x = points.astype(F32)
    xr = turn(x)

    def by_pair(v):
        return jnp.concatenate([jnp.where(pair == p, v, 0.0).astype(BF16) for p in range(4)], axis=1)

    def doubled(v, lo):
        v = jnp.where(lo, v, 0.0)
        return v + turn(v)

    sides, ys, pqs, answers = [], [], [], []
    for h in range(2):
        c = code[:, h * 128 : (h + 1) * 128]
        sides.append((c < 0.0, (jnp.abs(c) > 128.0) != first))
        upper = sides[h][0]
        d2 = jnp.where(first, x, xr) if h == 0 else jnp.where(first, xr, x)
        blocks = jnp.concatenate([wbuf[h * 4 + p, 0:128, :] for p in range(4)], axis=1)
        ys.append(doubled(mm(by_pair(jnp.where(upper != first, d2, 0.0)), blocks, NT), sides[h][1]))

    def coupled(v, h):
        return mm(v, jnp.concatenate([gbuf[h * 4 + p] for p in range(4)], axis=1), NT)

    for h in range(2):
        upper, lo = sides[h]
        y = ys[h]
        both = jnp.concatenate([by_pair(jnp.where(first, y, 0.0)), by_pair(jnp.where(first, 0.0, y))], axis=0)
        got = coupled(both, h)
        pqs.append([doubled(jnp.where(upper, g[:, 128:256], g[:, 0:128]), lo) for g in (got[:rows], got[rows:])])
    for h in range(2):
        upper, lo = sides[h]
        f = [factors[:, h * 384 + i * 128 : h * 384 + (i + 1) * 128] for i in range(3)]
        mixed = f[0] * ys[h] - f[1] * pqs[h][0] - f[2] * pqs[h][1]
        got = coupled(by_pair(mixed), h)
        rest = doubled(jnp.where(upper, got[:, 128:256], got[:, 0:128]), lo)
        answers.append((total * ys[h] - rest) * 0.125)
    return jnp.where(first, answers[0], answers[1]).astype(BF16)


def kernel(
    pot_hbm, types_hbm, sat_hbm, pat_hbm, inv_hbm, cpl_hbm, skin_hbm, out_ref,
    pot, typ, sat, pat, inv, cpl, skin, place, table, wbuf, gbuf, send, recv, bsend, brecv, csend, crecv, hsend, hrecv, rbuf, crbuf,
    load_sem, ready, wready, hready, allhere, rowhere, ps, pr, cs, cr, bs, br, ws, wr, hs, hr, bds, bdr, fs, cfs,
):
    dom, x = lax.axis_index("dom"), lax.axis_index("cell")
    c, z, y = dom & 1, (dom >> 1) & (NZ - 1), dom >> 5

    def at(yy, zz, cc):
        return ((yy * NZ + zz) * 2 + cc, x)

    ahead = {d: (z + d) & (NZ - 1) for d in OFFSETS}
    behind = {d: (z - d) & (NZ - 1) for d in OFFSETS}
    zpeer = {d: at(y, ahead[d], c) for d in OFFSETS}
    special = jnp.logical_and(x == 0, jnp.logical_and(y == 0, c == 0))
    shift = special.astype(jnp.int32)

    def turn_of(zz):
        return jnp.where(jnp.logical_and(special, zz == 0), NZ, jnp.minimum(zz, HALF))

    def slot_of(zz):
        return jnp.where(jnp.logical_and(special, zz == 0), HALF, zz + (zz >= HALF) * 1)

    zback = {d: at(y, behind[d], c) for d in OFFSETS}
    mine, slot = turn_of(z), slot_of(z)
    n_behind = jnp.where(mine == NZ, NZ - 1 - GROUP, mine - shift)
    middle = jnp.logical_and(z >= HALF, z < HALF + GROUP)
    early, late, lone = mine < HALF, mine == HALF, mine == NZ
    wpeer, later = {}, {}
    for k in range(1, 4):
        yy = (y - k) & (NY - 1)
        wpeer[k] = at(yy, z, c)
        later[k] = yy > y
    wpeer[4] = at(y, z, 1 - c)
    later[4] = c == 1
    index = dom * NX + x
    after = ((index + 1) >> 2, (index + 1) & (NX - 1))
    before = ((index - 1) >> 2, (index - 1) & (NX - 1))
    has_after, has_before = index < 2 * NY * NZ * NX - 1, index > 0

    ahead_next = jnp.logical_or(x < NX - 1, jnp.logical_and(c == 1, z < NZ - 1))
    behind_next = jnp.logical_or(x > 0, jnp.logical_and(c == 0, z > 0))
    part_after = jnp.logical_and(jnp.logical_and(x == NX - 1, c == 1), jnp.logical_and(z > 0, z < NZ - 1))
    part_before = jnp.logical_and(jnp.logical_and(x == 0, c == 0), z > 1)
    tells_after = jnp.logical_and(jnp.logical_and(x == NX - 1, c == 1), z == 0)
    tells_before = jnp.logical_and(jnp.logical_and(x == 0, c == 0), z == 1)
    i_first = jnp.logical_and(has_after, jnp.logical_and(ahead_next, jnp.logical_not(part_after)))
    i_last = jnp.logical_and(has_after, jnp.logical_not(ahead_next))
    b_first = jnp.logical_and(has_before, jnp.logical_and(behind_next, jnp.logical_not(part_before)))
    b_last = jnp.logical_and(has_before, jnp.logical_not(behind_next))
    relayed = mine < GROUP
    relays = jnp.logical_and(jnp.logical_and(z >= GROUP, z < 2 * GROUP), turn_of(z - GROUP) < GROUP)

    barrier = pltpu.get_barrier_semaphore()
    @pl.when(early)
    def _():
        for j in range(1, NZ):
            @pl.when(z < j)
            def _(j=j):
                pl.semaphore_signal(barrier, inc=1, device_id=at(y, j, c), device_id_type=MESH)

    @pl.when(jnp.logical_and(jnp.logical_and(special, z > 0), jnp.logical_not(middle)))
    def _():
        pl.semaphore_signal(barrier, inc=1, device_id=at(y, 0, c), device_id_type=MESH)

    for k in (1, 3, 4):
        @pl.when(later[k])
        def _(k=k):
            pl.semaphore_signal(barrier, inc=1, device_id=wpeer[k], device_id_type=MESH)

    @pl.when(i_first)
    def _():
        pl.semaphore_signal(barrier, inc=1, device_id=after, device_id_type=MESH)

    @pl.when(b_last)
    def _():
        pl.semaphore_signal(barrier, inc=1, device_id=before, device_id_type=MESH)

    loads = [
        pltpu.make_async_copy(src, dst, load_sem.at[i])
        for i, (src, dst) in enumerate([
            (types_hbm, typ), (sat_hbm, sat), (pat_hbm, pat), (pot_hbm, pot), (inv_hbm, inv), (cpl_hbm, cpl),
            (skin_hbm, skin),
        ])
    ]
    for load in loads:
        load.start()
    n_earlier = jnp.minimum(y, 1) + y // 3 + 1 - c + n_behind + b_first.astype(jnp.int32) + i_last.astype(jnp.int32)

    @pl.when(n_earlier > 0)
    def _():
        pl.semaphore_wait(barrier, n_earlier)

    near_lone = (*range(1, HALF), *range(HALF + GROUP, NZ))
    precedes = {j: jnp.logical_and(z > 0, jnp.logical_not(special)) if j == 0 else z > j for j in range(HALF)}
    for j in range(HALF):
        @pl.when(precedes[j])
        def _(j=j):
            pl.semaphore_signal(ready.at[(z - j) & (NZ - 1)], inc=1, device_id=at(y, j, c), device_id_type=MESH)

    @pl.when(lone)
    def _():
        for j in near_lone:
            pl.semaphore_signal(ready.at[NZ - j], inc=1, device_id=at(y, j, c), device_id_type=MESH)

    for k in (1, 3, 4):
        @pl.when(jnp.logical_not(later[k]))
        def _(k=k):
            at_peer = k if k == 4 else 4 - k
            pl.semaphore_signal(wready.at[at_peer], inc=1, device_id=wpeer[k], device_id_type=MESH)

    @pl.when(i_last)
    def _():
        pl.semaphore_signal(hready.at[1], inc=1, device_id=after, device_id_type=MESH)

    @pl.when(b_first)
    def _():
        pl.semaphore_signal(hready.at[0], inc=1, device_id=before, device_id_type=MESH)

    loads[4].wait()
    loads[5].wait()
    w = inv[...]
    wbuf[0, 0:128, :] = jnp.concatenate([w[0:128].astype(F32), w[128:256].astype(F32)], axis=1).astype(BF16)
    block = cpl[...].astype(F32)
    wbuf[0, 128:192, :] = jnp.concatenate([block, block.T], axis=1).astype(BF16)
    weights = {
        k: pltpu.make_async_remote_copy(
            wbuf.at[max(k - 4, 0)], wbuf.at[k], ws.at[k], wr.at[k], device_id=wpeer[min(k, 4)], device_id_type=MESH
        )
        for k in range(1, 8)
    }
    for want in (False, True):
        for k in (3, 1, 4):
            if want and k == 4:
                continue

            @pl.when(later[k] == want)
            def _(k=k, want=want):
                if want:
                    pl.semaphore_wait(wready.at[k], 1)
                weights[k].start()

    @pl.when(jnp.logical_and(y > 0, later[3]))
    def _():
        for k in (3, 1):
            pl.semaphore_signal(wready.at[2], inc=1, device_id=wpeer[k], device_id_type=MESH)

    for i in (0, 1, 2, 3, 6):
        loads[i].wait()

    field = pot[...]
    t = typ[...]
    onehot = (iota((128, 256), 0) == t).astype(BF16)
    earlier = (iota((256, 256), 0) < iota((256, 256), 1)).astype(BF16)
    rank = jnp.sum(onehot.astype(F32) * mm(onehot, earlier), axis=0, keepdims=True).astype(jnp.int32)
    t_y, t_z, t_c = t // (2 * NZ), (t // 2) % NZ, t % 2
    row = t_z * 16 + ((t_y - y + NY) % NY) * 4 + rank
    side = (t_c - c + 2) % 2
    both = jnp.concatenate([jnp.where(side == 0, row, -1), jnp.where(side == 1, row, -1)], axis=1)
    place[...] = (iota((256, 512), 0) == both).astype(BF16)
    level, bits = sat[...], pat[...]
    code = (1 + (level % 2) * 128 + bits) * jnp.where(level >= 2, -1, 1)
    code = jnp.broadcast_to(code.astype(F32), (64, 256)).astype(BF16)
    drive = field.astype(BF16)
    none = jnp.zeros((64, 256), BF16)
    spread = jnp.concatenate(
        [jnp.concatenate([a, none], axis=1) if i == 0 else jnp.concatenate([none, a], axis=1)
         for a in (drive, code) for i in range(2)], axis=0
    )
    placed = mm(place[...], spread, NT)
    keep = iota((NZ, 16, 128), 2) % 64 == iota((NZ, 16, 128), 1)
    send[...] = placed[:, 0:128].astype(BF16).reshape(NZ, 16, 128)
    csend[...] = jnp.sum(jnp.where(keep, placed[:, 128:256].reshape(NZ, 16, 128), 0.0), axis=1, keepdims=True)

    out, back, backin = {}, {}, {}
    for d in OFFSETS:
        out[d] = [
            pltpu.make_async_remote_copy(
                csend.at[ahead[d]], crecv.at[slot], cs.at[d], cr.at[d], device_id=zpeer[d], device_id_type=MESH
            ),
            pltpu.make_async_remote_copy(
                send.at[ahead[d]], recv.at[slot], ps.at[d], pr.at[d], device_id=zpeer[d], device_id_type=MESH
            ),
        ]
        back[d] = pltpu.make_async_remote_copy(
            bsend.at[slot_of(behind[d])], brecv.at[z], bs.at[d], br.at[d], device_id=zback[d], device_id_type=MESH
        )
    def send_to(j):
        d = (j - z) & (NZ - 1)
        for src, dst, ss, rs in ((csend, crecv, cs, cr), (send, recv, ps, pr)):
            pltpu.make_async_remote_copy(
                src.at[j], dst.at[slot], ss.at[d], rs.at[d], device_id=at(y, j, c), device_id_type=MESH
            ).start()

    for j in range(HALF):
        pl.when(precedes[j])(functools.partial(send_to, j))

    @pl.when(lone)
    def _():
        for j in near_lone:
            send_to(j)


    eye = iota((64, 128), 0) == iota((64, 128), 1)
    hsend[0] = jnp.sum(jnp.where(eye, field[:, 255:256], 0.0), axis=0, keepdims=True)
    hsend[1] = jnp.sum(jnp.where(eye, field[:, 0:1], 0.0), axis=0, keepdims=True)
    to_after = pltpu.make_async_remote_copy(
        hsend.at[0], hrecv.at[0], hs.at[0], hr.at[0], device_id=after, device_id_type=MESH
    )
    to_before = pltpu.make_async_remote_copy(
        hsend.at[1], hrecv.at[1], hs.at[1], hr.at[1], device_id=before, device_id_type=MESH
    )

    pl.semaphore_wait(wready.at[2], 1)
    weights[2].start()
    pl.when(i_last)(to_after.start)
    pl.when(b_first)(to_before.start)

    span = pl.ds(lax.rem(z + FAR[0], NZ - len(FAR) + 1), len(FAR))
    bundle = [
        pltpu.make_async_remote_copy(
            src.at[span], dst, bds.at[i], bdr.at[i], device_id=zpeer[GROUP], device_id_type=MESH
        )
        for i, (src, dst) in enumerate([(csend, crbuf), (send, rbuf)])
    ]
    from_slot = slot_of(jnp.maximum(z - GROUP, 0))
    onward = {}
    for j in range(1, len(FAR) + 1):
        onward[j] = [
            pltpu.make_async_remote_copy(
                src.at[j - 1], dst.at[from_slot], ss.at[j - 1], rs.at[j + GROUP],
                device_id=zpeer[j], device_id_type=MESH,
            )
            for src, dst, ss, rs in ((crbuf, crecv, cfs, cr), (rbuf, recv, fs, pr))
        ]

    def send_on(d):
        @pl.when(jnp.logical_and(z + d < NZ, jnp.logical_not(relayed)) if d in FAR else z + d < NZ)
        def _():
            pl.semaphore_wait(ready.at[d], 1)
            for copy in out[d]:
                copy.start()

    @pl.when(early)
    def _():
        for d in (*range(1, GROUP + 2), *range(NZ - 1, FAR[-1], -1), *range(FAR[-1], GROUP + 1, -1)):
            send_on(d)
            if d == GROUP:
                @pl.when(relayed)
                def _():
                    for copy in bundle:
                        copy.start()

            if d in onward:
                @pl.when(relays)
                def _(d=d):
                    if d == 1:
                        for copy in bundle:
                            copy.wait_recv()
                    for copy in onward[d]:
                        copy.start()

    @pl.when(relayed)
    def _():
        for d in FAR:
            pl.semaphore_wait(ready.at[d], 1)

    def tell(when, at_offset, told):
        @pl.when(when)
        def _():
            @pl.when(special)
            def _():
                pl.semaphore_wait(ready.at[at_offset], 1)
                for copy in out[at_offset]:
                    copy.start()

            if told[0] != 1:
                @pl.when(special)
                def _():
                    pl.semaphore_signal(allhere, inc=1, device_id=zpeer[at_offset], device_id_type=MESH)

            for d in told:
                pl.semaphore_signal(allhere, inc=1, device_id=zpeer[d], device_id_type=MESH)

    tell(z == HALF - 1, HALF + 1, range(1, GROUP + 1))
    tell(z == 1, NZ - 1, range(NZ - 2, NZ - 2 - GROUP, -1))

    @pl.when(lone)
    def _():
        pl.semaphore_wait(allhere, 1)
        for j in range(HALF, HALF + GROUP):
            send_to(j)


    @pl.when(later[4])
    def _():
        pl.semaphore_wait(wready.at[4], 1)
        weights[4].start()

    empty = jnp.where(special, 0, HALF)
    recv[empty] = jnp.zeros((16, 128), BF16)
    crecv[empty] = jnp.zeros((1, 128), F32)
    recv[slot] = send[z]
    crecv[slot] = csend[z]

    @pl.when(i_first)
    def _():
        pl.semaphore_wait(hready.at[0], 1)
        to_after.start()

    @pl.when(jnp.logical_and(b_last, z > 0))
    def _():
        pl.semaphore_wait(hready.at[1], 1)
        to_before.start()

    @pl.when(tells_after)
    def _():
        pl.semaphore_signal(rowhere, inc=1, device_id=after, device_id_type=MESH)

    @pl.when(tells_before)
    def _():
        pl.semaphore_signal(rowhere, inc=1, device_id=before, device_id_type=MESH)

    table[...] = coefficients(skin)
    total = skin[0]
    for k in range(1, 8):
        total = total + skin[k]

    gbuf[0] = product(wbuf[0, 0:128, :], wbuf[0, 128:192, :])
    for k in (1, 3, 2):
        weights[k].wait_recv()
        weights[k + 4].start()
    for ks in ((1, 3, 2), (4, 5, 7, 6)):
        for k in ks:
            if k >= 4:
                weights[k].wait_recv()
        for k in ks:
            gbuf[k] = product(wbuf[k, 0:128, :], wbuf[k, 128:192, :])

    spreads = table[...]
    for start, stop in ((0, GROUP), (GROUP, HALF + 1), (HALF + 1, NZ + 1)):
        sources = [j for j in range(NZ) if start <= j + (j >= HALF) < stop] + ([0] if start == GROUP else [])
        apply = {j: (special if start == GROUP else jnp.logical_not(special)) if j == 0 else True for j in sources}
        for j in sources:
            @pl.when(jnp.logical_and(z != j, apply[j]))
            def _(j=j):
                d = (z - j) & (NZ - 1)
                for src, dst, ss, rs in ((csend, crecv, cs, cr), (send, recv, ps, pr)):
                    pltpu.make_async_remote_copy(
                        src.at[j], dst.at[j], ss.at[d], rs.at[d], device_id=at(y, j, c), device_id_type=MESH
                    ).wait_recv()

        n = stop - start
        answer = solve(
            recv[start:stop].reshape(n * 16, 128), crecv[start:stop].reshape(n, 128), wbuf, gbuf, spreads, total
        )
        bsend[start:stop] = answer.reshape(n, 16, 128)
        for j in sources:
            @pl.when(jnp.logical_and(z != j, apply[j]))
            def _(j=j):
                d = (z - j) & (NZ - 1)
                pltpu.make_async_remote_copy(
                    bsend.at[slot_of(j)], brecv.at[z], bs.at[d], br.at[d], device_id=at(y, j, c), device_id_type=MESH
                ).start()

        if start == 0:
            @pl.when(late)
            def _():
                pl.semaphore_wait(allhere, 1)
                for j in range(HALF, NZ):
                    pl.when(z != j)(functools.partial(send_to, j))

                @pl.when(jnp.logical_and(special, middle))
                def _():
                    send_to(0)

            @pl.when(jnp.logical_or(tells_after, tells_before))
            def _():
                pl.semaphore_wait(rowhere, 1)
                for d in range(1, NZ - 1):
                    pl.semaphore_signal(rowhere, inc=1, device_id=zpeer[d], device_id_type=MESH)

            others = jnp.logical_and(jnp.logical_and(z > 1, z != HALF - 1), jnp.logical_not(middle))

            @pl.when(jnp.logical_and(special, others))
            def _():
                pl.semaphore_wait(ready.at[(NZ - z) & (NZ - 1)], 1)
                send_to(0)

    brecv[z] = bsend[slot]

    @pl.when(jnp.logical_and(b_last, z == 0))
    def _():
        pl.semaphore_wait(hready.at[1], 1)
        to_before.start()

    @pl.when(part_after)
    def _():
        pl.semaphore_wait(rowhere, 1)
        to_after.start()

    @pl.when(part_before)
    def _():
        pl.semaphore_wait(rowhere, 1)
        to_before.start()

    pl.when(has_before)(to_after.wait_recv)
    pl.when(has_after)(to_before.wait_recv)
    lane = iota((64, 256), 1)
    left = jnp.sum(jnp.where(jnp.logical_and(eye, has_before), hrecv[0], 0.0), axis=1, keepdims=True)
    right = jnp.sum(jnp.where(jnp.logical_and(eye, has_after), hrecv[1], 0.0), axis=1, keepdims=True)
    left = jnp.where(lane == 0, left, pltpu.roll(field, 1, 1))
    right = jnp.where(lane == 255, right, pltpu.roll(field, 255, 1))
    pot[...] = field + 0.25 * (left - 2.0 * field + right)

    for k in weights:
        weights[k].wait_send()
    for d in OFFSETS:
        if d in FAR:
            @pl.when(jnp.logical_not(relayed))
            def _(d=d):
                for copy in out[d]:
                    copy.wait_send()
        else:
            for copy in out[d]:
                copy.wait_send()
        back[d].wait_send()

    @pl.when(relayed)
    def _():
        for copy in bundle:
            copy.wait_send()

    @pl.when(relays)
    def _():
        for j in onward:
            for copy in onward[j]:
                copy.wait_send()

    pl.when(has_after)(to_after.wait_send)
    pl.when(has_before)(to_before.wait_send)

    for d in OFFSETS:
        back[d].wait_recv()
    got = mm(brecv[...].reshape(256, 128), place[...], TN)
    out_ref[...] = pot[...] - (got[0:64, 0:256] + got[64:128, 256:512])


def body(potential, types, saturation, pattern, inverses, coupling, skin):
    dma = pltpu.SemaphoreType.DMA
    return pl.pallas_call(
        kernel,
        out_shape=jax.ShapeDtypeStruct((64, 256), F32),
        in_specs=[pl.BlockSpec(memory_space=pl.ANY)] * 7,
        out_specs=pl.BlockSpec(memory_space=pltpu.VMEM),
        scratch_shapes=[
            pltpu.VMEM((64, 256), F32),
            pltpu.VMEM((1, 256), jnp.int32),
            pltpu.VMEM((1, 256), jnp.int32),
            pltpu.VMEM((1, 256), jnp.int32),
            pltpu.VMEM((256, 64), BF16),
            pltpu.VMEM((64, 64), BF16),
            pltpu.SMEM((8,), F32),
            pltpu.VMEM((256, 512), BF16),
            pltpu.VMEM((128, 768), BF16),
            pltpu.VMEM((8, 192, 128), BF16),
            pltpu.VMEM((8, 256, 128), BF16),
            pltpu.VMEM((NZ, 16, 128), BF16),
            pltpu.VMEM((NZ + 1, 16, 128), BF16),
            pltpu.VMEM((NZ + 1, 16, 128), BF16),
            pltpu.VMEM((NZ, 16, 128), BF16),
            pltpu.VMEM((NZ, 1, 128), F32),
            pltpu.VMEM((NZ + 1, 1, 128), F32),
            pltpu.VMEM((2, 1, 128), F32),
            pltpu.VMEM((2, 1, 128), F32),
            pltpu.VMEM((len(FAR), 16, 128), BF16),
            pltpu.VMEM((len(FAR), 1, 128), F32),
            dma((7,)),
            pltpu.SemaphoreType.REGULAR((NZ,)),
            pltpu.SemaphoreType.REGULAR((8,)),
            pltpu.SemaphoreType.REGULAR((2,)),
            pltpu.SemaphoreType.REGULAR,
            pltpu.SemaphoreType.REGULAR,
            *[dma((NZ,)) for _ in range(6)],
            *[dma((8,)) for _ in range(2)],
            *[dma((2,)) for _ in range(4)],
            *[dma((len(FAR),)) for _ in range(2)],
        ],
        compiler_params=pltpu.CompilerParams(
            collective_id=0, has_side_effects=True, vmem_limit_bytes=32 * 1024 * 1024
        ),
        name="regroup_solve",
    )(
        *[
            pltpu.with_memory_space_constraint(array, pltpu.HBM)
            for array in (
                potential,
                types.reshape(1, 256),
                saturation.reshape(1, 256),
                pattern.reshape(1, 256),
                inverses.reshape(256, 64),
                coupling.reshape(64, 64),
                skin,
            )
        ]
    )


def solution(mesh):
    placed = (
        P(None, ("dom", "cell")),
        P(("dom", "cell"), None),
        P(("dom", "cell")),
        P(("dom", "cell")),
        P("dom", None, None, None),
        P("dom", None, None),
        P(),
    )
    return jax.shard_map(
        body, mesh=mesh, in_specs=placed, out_specs=P(None, ("dom", "cell")), check_vma=False
    )
```

```python
import functools

import jax
import jax.numpy as jnp
from jax import lax
from jax.experimental import pallas as pl
from jax.experimental.pallas import tpu as pltpu
from jax.sharding import PartitionSpec as P

MESH = pl.DeviceIdType.MESH
F32 = jnp.float32
BF16 = jnp.bfloat16
NY, NZ, NX = 4, 16, 4
NT = (((1,), (1,)), ((), ()))
TN = (((0,), (0,)), ((), ()))
NN = (((1,), (0,)), ((), ()))
GROUP, HALF = 4, NZ // 2
FAR = range(GROUP + 1, 2 * GROUP + 2)
OFFSETS = sorted(range(1, NZ), key=lambda d: min(d, NZ - d))


def mm(a, b, dims=NN):
    return lax.dot_general(a, b, dims, preferred_element_type=F32)


def iota(shape, axis):
    return lax.broadcasted_iota(jnp.int32, shape, axis)


def turn(x):
    return pltpu.roll(x, 64, 1)


def coefficients(skin):
    row, lane = iota((128, 128), 0), iota((128, 128), 1)
    place_in = row % 64
    bit, part, first = place_in % 13, place_in // 13, lane < 64

    def chosen(lower, upper):
        value = jnp.zeros((128, 128), F32)
        for i in range(13):
            a = skin[lower[i]] if i in lower else 0.0
            b = skin[upper[i]] if i in upper else 0.0
            value = jnp.where(bit == i, jnp.where(first, a, b), value)
        return value

    above, here = {i: i + 1 for i in range(7)}, {i: i for i in range(7)}
    above2, here2 = {7 + i: i + 2 for i in range(6)}, {7 + i: i for i in range(6)}
    value = jnp.concatenate([chosen(above, here), chosen(above2, above), chosen(here, here2)], axis=1)
    row, part = iota((128, 384), 0), (iota((128, 384), 0) % 64) // 13
    high = value.astype(BF16).astype(F32)
    rest = value - high
    middle = rest.astype(BF16).astype(F32)
    value = jnp.where(part == 0, high, jnp.where(part == 1, middle, jnp.where(part == 2, rest - middle, 0.0)))
    return jnp.concatenate([jnp.where(row // 64 == h, value, 0.0) for h in range(2)], axis=1).astype(BF16)


def product(a, c):
    low = iota((128, 128), 1) < 64
    a = a.astype(F32)
    levels = jnp.concatenate([jnp.where(low, a, 0.0), jnp.where(low, 0.0, a)], axis=0).astype(BF16)
    return mm(levels, jnp.concatenate([c, c], axis=0)).astype(BF16)


def solve(points, codes, wbuf, gbuf, table, total):
    n = codes.shape[0]
    rows = 16 * n
    row, lane = iota((rows, 128), 0), iota((rows, 128), 1)
    first = lane < 64
    pair = (row // 4) % 4
    spread = jnp.broadcast_to(codes.reshape(n, 1, 128), (n, 16, 128)).reshape(rows, 128)
    spread = jnp.where(lane % 64 == row % 16, spread, 0.0).astype(BF16)
    from_half, to = iota((128, 384), 0) // 64, iota((128, 384), 1)
    pick = (from_half == jnp.where(to < 256, to // 128, (to // 64) % 2)).astype(BF16)
    code = mm(spread, pick)
    bits = jnp.abs(code[:, 256:384]).astype(jnp.int32) - 1
    bit = (lane % 64) % 13
    mask = jnp.where(bit < 7, jnp.left_shift(1, bit), jnp.left_shift(3, jnp.maximum(bit - 7, 0)))
    held = jnp.logical_and(jnp.bitwise_and(bits, mask) == mask, lane % 64 < 39)
    factors = mm(held.astype(F32).astype(BF16), table)
    x = points.astype(F32)
    xr = turn(x)

    def by_pair(v):
        return jnp.concatenate([jnp.where(pair == p, v, 0.0).astype(BF16) for p in range(4)], axis=1)

    def doubled(v, lo):
        v = jnp.where(lo, v, 0.0)
        return v + turn(v)

    sides, ys, pqs, answers = [], [], [], []
    for h in range(2):
        c = code[:, h * 128 : (h + 1) * 128]
        sides.append((c < 0.0, (jnp.abs(c) > 128.0) != first))
        upper = sides[h][0]
        d2 = jnp.where(first, x, xr) if h == 0 else jnp.where(first, xr, x)
        blocks = jnp.concatenate([wbuf[h * 4 + p, 0:128, :] for p in range(4)], axis=1)
        ys.append(doubled(mm(by_pair(jnp.where(upper != first, d2, 0.0)), blocks, NT), sides[h][1]))

    def coupled(v, h):
        return mm(v, jnp.concatenate([gbuf[h * 4 + p] for p in range(4)], axis=1), NT)

    for h in range(2):
        upper, lo = sides[h]
        y = ys[h]
        both = jnp.concatenate([by_pair(jnp.where(first, y, 0.0)), by_pair(jnp.where(first, 0.0, y))], axis=0)
        got = coupled(both, h)
        pqs.append([doubled(jnp.where(upper, g[:, 128:256], g[:, 0:128]), lo) for g in (got[:rows], got[rows:])])
    for h in range(2):
        upper, lo = sides[h]
        f = [factors[:, h * 384 + i * 128 : h * 384 + (i + 1) * 128] for i in range(3)]
        mixed = f[0] * ys[h] - f[1] * pqs[h][0] - f[2] * pqs[h][1]
        got = coupled(by_pair(mixed), h)
        rest = doubled(jnp.where(upper, got[:, 128:256], got[:, 0:128]), lo)
        answers.append((total * ys[h] - rest) * 0.125)
    return jnp.where(first, answers[0], answers[1]).astype(BF16)


def kernel(
    pot_hbm, types_hbm, sat_hbm, pat_hbm, inv_hbm, cpl_hbm, skin_hbm, out_ref,
    pot, typ, sat, pat, inv, cpl, skin, place, table, wbuf, gbuf, send, recv, bsend, brecv, csend, crecv, hsend, hrecv, rbuf, crbuf,
    load_sem, ready, wready, hready, allhere, rowhere, ps, pr, cs, cr, bs, br, ws, wr, hs, hr, bds, bdr, fs, cfs,
):
    dom, x = lax.axis_index("dom"), lax.axis_index("cell")
    c, z, y = dom & 1, (dom >> 1) & (NZ - 1), dom >> 5

    def at(yy, zz, cc):
        return ((yy * NZ + zz) * 2 + cc, x)

    ahead = {d: (z + d) & (NZ - 1) for d in OFFSETS}
    behind = {d: (z - d) & (NZ - 1) for d in OFFSETS}
    zpeer = {d: at(y, ahead[d], c) for d in OFFSETS}
    special = jnp.logical_and(x == 0, jnp.logical_and(y == 0, c == 0))
    shift = special.astype(jnp.int32)

    def turn_of(zz):
        return jnp.where(jnp.logical_and(special, zz == 0), NZ, jnp.minimum(zz, HALF))

    def slot_of(zz):
        return jnp.where(jnp.logical_and(special, zz == 0), HALF, zz + (zz >= HALF) * 1)

    zback = {d: at(y, behind[d], c) for d in OFFSETS}
    mine, slot = turn_of(z), slot_of(z)
    n_behind = jnp.where(mine == NZ, NZ - 1 - GROUP, mine - shift)
    middle = jnp.logical_and(z >= HALF, z < HALF + GROUP)
    early, late, lone = mine < HALF, mine == HALF, mine == NZ
    wpeer, later = {}, {}
    for k in range(1, 4):
        yy = (y - k) & (NY - 1)
        wpeer[k] = at(yy, z, c)
        later[k] = yy > y
    wpeer[4] = at(y, z, 1 - c)
    later[4] = c == 1
    index = dom * NX + x
    after = ((index + 1) >> 2, (index + 1) & (NX - 1))
    before = ((index - 1) >> 2, (index - 1) & (NX - 1))
    has_after, has_before = index < 2 * NY * NZ * NX - 1, index > 0

    ahead_next = jnp.logical_or(x < NX - 1, jnp.logical_and(c == 1, z < NZ - 1))
    behind_next = jnp.logical_or(x > 0, jnp.logical_and(c == 0, z > 0))
    part_after = jnp.logical_and(jnp.logical_and(x == NX - 1, c == 1), jnp.logical_and(z > 0, z < NZ - 1))
    part_before = jnp.logical_and(jnp.logical_and(x == 0, c == 0), z > 1)
    tells_after = jnp.logical_and(jnp.logical_and(x == NX - 1, c == 1), z == 0)
    tells_before = jnp.logical_and(jnp.logical_and(x == 0, c == 0), z == 1)
    i_first = jnp.logical_and(has_after, jnp.logical_and(ahead_next, jnp.logical_not(part_after)))
    i_last = jnp.logical_and(has_after, jnp.logical_not(ahead_next))
    b_first = jnp.logical_and(has_before, jnp.logical_and(behind_next, jnp.logical_not(part_before)))
    b_last = jnp.logical_and(has_before, jnp.logical_not(behind_next))
    relayed = mine < GROUP
    relays = jnp.logical_and(z >= GROUP, z <= GROUP + 2)
    present = [
        jnp.logical_or(z == GROUP + 1, z == GROUP + 2),
        jnp.logical_or(z == GROUP + 1, jnp.logical_and(z == GROUP, jnp.logical_not(special))),
    ]

    barrier = pltpu.get_barrier_semaphore()
    @pl.when(early)
    def _():
        for j in range(1, NZ):
            @pl.when(z < j)
            def _(j=j):
                pl.semaphore_signal(barrier, inc=1, device_id=at(y, j, c), device_id_type=MESH)

    @pl.when(jnp.logical_and(jnp.logical_and(special, z > 0), jnp.logical_not(middle)))
    def _():
        pl.semaphore_signal(barrier, inc=1, device_id=at(y, 0, c), device_id_type=MESH)

    for k in (1, 3, 4):
        @pl.when(later[k])
        def _(k=k):
            pl.semaphore_signal(barrier, inc=1, device_id=wpeer[k], device_id_type=MESH)

    @pl.when(i_first)
    def _():
        pl.semaphore_signal(barrier, inc=1, device_id=after, device_id_type=MESH)

    @pl.when(b_last)
    def _():
        pl.semaphore_signal(barrier, inc=1, device_id=before, device_id_type=MESH)

    loads = [
        pltpu.make_async_copy(src, dst, load_sem.at[i])
        for i, (src, dst) in enumerate([
            (types_hbm, typ), (sat_hbm, sat), (pat_hbm, pat), (pot_hbm, pot), (inv_hbm, inv), (cpl_hbm, cpl),
            (skin_hbm, skin),
        ])
    ]
    for load in loads:
        load.start()
    n_earlier = jnp.minimum(y, 1) + y // 3 + 1 - c + n_behind + b_first.astype(jnp.int32) + i_last.astype(jnp.int32)

    @pl.when(n_earlier > 0)
    def _():
        pl.semaphore_wait(barrier, n_earlier)

    near_lone = (*range(1, HALF), *range(HALF + GROUP, NZ))
    precedes = {j: jnp.logical_and(z > 0, jnp.logical_not(special)) if j == 0 else z > j for j in range(HALF)}
    for j in range(HALF):
        @pl.when(precedes[j])
        def _(j=j):
            pl.semaphore_signal(ready.at[(z - j) & (NZ - 1)], inc=1, device_id=at(y, j, c), device_id_type=MESH)

    @pl.when(lone)
    def _():
        for j in near_lone:
            pl.semaphore_signal(ready.at[NZ - j], inc=1, device_id=at(y, j, c), device_id_type=MESH)

    for k in (1, 3, 4):
        @pl.when(jnp.logical_not(later[k]))
        def _(k=k):
            at_peer = k if k == 4 else 4 - k
            pl.semaphore_signal(wready.at[at_peer], inc=1, device_id=wpeer[k], device_id_type=MESH)

    @pl.when(i_last)
    def _():
        pl.semaphore_signal(hready.at[1], inc=1, device_id=after, device_id_type=MESH)

    @pl.when(b_first)
    def _():
        pl.semaphore_signal(hready.at[0], inc=1, device_id=before, device_id_type=MESH)

    loads[4].wait()
    loads[5].wait()
    w = inv[...]
    wbuf[0, 0:128, :] = jnp.concatenate([w[0:128].astype(F32), w[128:256].astype(F32)], axis=1).astype(BF16)
    block = cpl[...].astype(F32)
    wbuf[0, 128:192, :] = jnp.concatenate([block, block.T], axis=1).astype(BF16)
    weights = {
        k: pltpu.make_async_remote_copy(
            wbuf.at[max(k - 4, 0)], wbuf.at[k], ws.at[k], wr.at[k], device_id=wpeer[min(k, 4)], device_id_type=MESH
        )
        for k in range(1, 8)
    }
    for want in (False, True):
        for k in (3, 1, 4):
            if want and k == 4:
                continue

            @pl.when(later[k] == want)
            def _(k=k, want=want):
                if want:
                    pl.semaphore_wait(wready.at[k], 1)
                weights[k].start()

    @pl.when(jnp.logical_and(y > 0, later[3]))
    def _():
        for k in (3, 1):
            pl.semaphore_signal(wready.at[2], inc=1, device_id=wpeer[k], device_id_type=MESH)

    for i in (0, 1, 2, 3, 6):
        loads[i].wait()

    field = pot[...]
    t = typ[...]
    onehot = (iota((128, 256), 0) == t).astype(BF16)
    earlier = (iota((256, 256), 0) < iota((256, 256), 1)).astype(BF16)
    rank = jnp.sum(onehot.astype(F32) * mm(onehot, earlier), axis=0, keepdims=True).astype(jnp.int32)
    t_y, t_z, t_c = t // (2 * NZ), (t // 2) % NZ, t % 2
    row = t_z * 16 + ((t_y - y + NY) % NY) * 4 + rank
    side = (t_c - c + 2) % 2
    both = jnp.concatenate([jnp.where(side == 0, row, -1), jnp.where(side == 1, row, -1)], axis=1)
    place[...] = (iota((256, 512), 0) == both).astype(BF16)
    level, bits = sat[...], pat[...]
    code = (1 + (level % 2) * 128 + bits) * jnp.where(level >= 2, -1, 1)
    code = jnp.broadcast_to(code.astype(F32), (64, 256)).astype(BF16)
    drive = field.astype(BF16)
    none = jnp.zeros((64, 256), BF16)
    spread = jnp.concatenate(
        [jnp.concatenate([a, none], axis=1) if i == 0 else jnp.concatenate([none, a], axis=1)
         for a in (drive, code) for i in range(2)], axis=0
    )
    placed = mm(place[...], spread, NT)
    keep = iota((NZ, 16, 128), 2) % 64 == iota((NZ, 16, 128), 1)
    send[...] = placed[:, 0:128].astype(BF16).reshape(NZ, 16, 128)
    csend[...] = jnp.sum(jnp.where(keep, placed[:, 128:256].reshape(NZ, 16, 128), 0.0), axis=1, keepdims=True)

    out, back, backin = {}, {}, {}
    for d in OFFSETS:
        out[d] = [
            pltpu.make_async_remote_copy(
                csend.at[ahead[d]], crecv.at[slot], cs.at[d], cr.at[d], device_id=zpeer[d], device_id_type=MESH
            ),
            pltpu.make_async_remote_copy(
                send.at[ahead[d]], recv.at[slot], ps.at[d], pr.at[d], device_id=zpeer[d], device_id_type=MESH
            ),
        ]
        back[d] = pltpu.make_async_remote_copy(
            bsend.at[slot_of(behind[d])], brecv.at[z], bs.at[d], br.at[d], device_id=zback[d], device_id_type=MESH
        )
    def send_to(j):
        d = (j - z) & (NZ - 1)
        for src, dst, ss, rs in ((csend, crecv, cs, cr), (send, recv, ps, pr)):
            pltpu.make_async_remote_copy(
                src.at[j], dst.at[slot], ss.at[d], rs.at[d], device_id=at(y, j, c), device_id_type=MESH
            ).start()

    for j in range(HALF):
        pl.when(precedes[j])(functools.partial(send_to, j))

    @pl.when(lone)
    def _():
        for j in near_lone:
            send_to(j)


    eye = iota((64, 128), 0) == iota((64, 128), 1)
    hsend[0] = jnp.sum(jnp.where(eye, field[:, 255:256], 0.0), axis=0, keepdims=True)
    hsend[1] = jnp.sum(jnp.where(eye, field[:, 0:1], 0.0), axis=0, keepdims=True)
    to_after = pltpu.make_async_remote_copy(
        hsend.at[0], hrecv.at[0], hs.at[0], hr.at[0], device_id=after, device_id_type=MESH
    )
    to_before = pltpu.make_async_remote_copy(
        hsend.at[1], hrecv.at[1], hs.at[1], hr.at[1], device_id=before, device_id_type=MESH
    )

    pl.semaphore_wait(wready.at[2], 1)
    weights[2].start()
    pl.when(i_last)(to_after.start)
    pl.when(b_first)(to_before.start)

    span = pl.ds(jnp.minimum(z + FAR[0], NZ - len(FAR)), len(FAR))
    via, half_of = GROUP + ((z + 1) >> 1), (z + 1) & 1
    bundle = [
        pltpu.make_async_remote_copy(
            src.at[span], dst.at[half_of], bds.at[i], bdr.at[2 * half_of + i],
            device_id=at(y, via, c), device_id_type=MESH,
        )
        for i, (src, dst) in enumerate([(csend, crbuf), (send, rbuf)])
    ]

    def onward(b, i):
        source = jnp.clip(2 * (z - GROUP) - 1 + b, 0, GROUP - 1)
        to = source + FAR[0] + i
        return [
            pltpu.make_async_remote_copy(
                src.at[b, i], dst.at[source], ss.at[b * len(FAR) + i], rs.at[to - source],
                device_id=at(y, to, c), device_id_type=MESH,
            )
            for src, dst, ss, rs in ((crbuf, crecv, cfs, cr), (rbuf, recv, fs, pr))
        ]

    def send_onward(d):
        for b in range(2):
            i = d - b - (z - GROUP)

            @pl.when(jnp.logical_and(present[b], jnp.logical_and(i >= 0, i < len(FAR))))
            def _(b=b, i=i):
                for copy in onward(b, jnp.clip(i, 0, len(FAR) - 1)):
                    copy.start()

    def send_on(d):
        @pl.when(jnp.logical_and(z + d < NZ, jnp.logical_not(relayed)) if d in FAR else z + d < NZ)
        def _():
            pl.semaphore_wait(ready.at[d], 1)
            if d in (3, 4):
                @pl.when(jnp.logical_and(relayed, via - z == d))
                def _():
                    for copy in bundle:
                        copy.start()

            if GROUP <= d <= GROUP + 3:
                pl.when(relays)(functools.partial(send_onward, d))
            for copy in out[d]:
                copy.start()

    @pl.when(early)
    def _():
        for d in range(1, GROUP):
            send_on(d)
        for b in range(2):
            @pl.when(present[b])
            def _(b=b):
                for i, buffer in enumerate((crbuf, rbuf)):
                    pltpu.make_async_remote_copy(
                        buffer.at[b], buffer.at[b], bds.at[i], bdr.at[2 * b + i],
                        device_id=zpeer[1], device_id_type=MESH,
                    ).wait_recv()

        @pl.when(relays)
        def _():
            for d in range(GROUP - 1, 0, -1):
                send_onward(d)

        for d in (*range(GROUP, HALF), *range(NZ - 1, HALF - 1, -1)):
            send_on(d)

    @pl.when(relayed)
    def _():
        for d in FAR:
            pl.semaphore_wait(ready.at[d], 1)

    def tell(when, at_offset, told):
        @pl.when(when)
        def _():
            @pl.when(special)
            def _():
                pl.semaphore_wait(ready.at[at_offset], 1)
                for copy in out[at_offset]:
                    copy.start()

            if told[0] != 1:
                @pl.when(special)
                def _():
                    pl.semaphore_signal(allhere, inc=1, device_id=zpeer[at_offset], device_id_type=MESH)

            for d in told:
                pl.semaphore_signal(allhere, inc=1, device_id=zpeer[d], device_id_type=MESH)

    tell(z == HALF - 1, HALF + 1, range(1, GROUP + 1))
    tell(z == 1, NZ - 1, range(NZ - 2, NZ - 2 - GROUP, -1))

    @pl.when(lone)
    def _():
        pl.semaphore_wait(allhere, 1)
        for j in range(HALF, HALF + GROUP):
            send_to(j)


    @pl.when(later[4])
    def _():
        pl.semaphore_wait(wready.at[4], 1)
        weights[4].start()

    empty = jnp.where(special, 0, HALF)
    recv[empty] = jnp.zeros((16, 128), BF16)
    crecv[empty] = jnp.zeros((1, 128), F32)
    recv[slot] = send[z]
    crecv[slot] = csend[z]

    @pl.when(i_first)
    def _():
        pl.semaphore_wait(hready.at[0], 1)
        to_after.start()

    @pl.when(jnp.logical_and(b_last, z > 0))
    def _():
        pl.semaphore_wait(hready.at[1], 1)
        to_before.start()

    @pl.when(tells_after)
    def _():
        pl.semaphore_signal(rowhere, inc=1, device_id=after, device_id_type=MESH)

    @pl.when(tells_before)
    def _():
        pl.semaphore_signal(rowhere, inc=1, device_id=before, device_id_type=MESH)

    table[...] = coefficients(skin)
    total = skin[0]
    for k in range(1, 8):
        total = total + skin[k]

    gbuf[0] = product(wbuf[0, 0:128, :], wbuf[0, 128:192, :])
    for k in (1, 3, 2):
        weights[k].wait_recv()
        weights[k + 4].start()
    for ks in ((1, 3, 2), (4, 5, 7, 6)):
        for k in ks:
            if k >= 4:
                weights[k].wait_recv()
        for k in ks:
            gbuf[k] = product(wbuf[k, 0:128, :], wbuf[k, 128:192, :])

    spreads = table[...]
    for start, stop in ((0, GROUP), (GROUP, HALF + 1), (HALF + 1, NZ + 1)):
        sources = [j for j in range(NZ) if start <= j + (j >= HALF) < stop] + ([0] if start == GROUP else [])
        apply = {j: (special if start == GROUP else jnp.logical_not(special)) if j == 0 else True for j in sources}
        for j in reversed(sources):
            @pl.when(jnp.logical_and(z != j, apply[j]))
            def _(j=j):
                d = (z - j) & (NZ - 1)
                for src, dst, ss, rs in ((csend, crecv, cs, cr), (send, recv, ps, pr)):
                    pltpu.make_async_remote_copy(
                        src.at[j], dst.at[j], ss.at[d], rs.at[d], device_id=at(y, j, c), device_id_type=MESH
                    ).wait_recv()

        n = stop - start
        answer = solve(
            recv[start:stop].reshape(n * 16, 128), crecv[start:stop].reshape(n, 128), wbuf, gbuf, spreads, total
        )
        bsend[start:stop] = answer.reshape(n, 16, 128)
        for j in sources:
            @pl.when(jnp.logical_and(z != j, apply[j]))
            def _(j=j):
                d = (z - j) & (NZ - 1)
                pltpu.make_async_remote_copy(
                    bsend.at[slot_of(j)], brecv.at[z], bs.at[d], br.at[d], device_id=at(y, j, c), device_id_type=MESH
                ).start()

        if start == 0:
            @pl.when(late)
            def _():
                pl.semaphore_wait(allhere, 1)
                for j in range(HALF, NZ):
                    pl.when(z != j)(functools.partial(send_to, j))

                @pl.when(jnp.logical_and(special, middle))
                def _():
                    send_to(0)

            @pl.when(jnp.logical_or(tells_after, tells_before))
            def _():
                pl.semaphore_wait(rowhere, 1)
                for d in range(1, NZ - 1):
                    pl.semaphore_signal(rowhere, inc=1, device_id=zpeer[d], device_id_type=MESH)

            others = jnp.logical_and(jnp.logical_and(z > 1, z != HALF - 1), jnp.logical_not(middle))

            @pl.when(jnp.logical_and(special, others))
            def _():
                pl.semaphore_wait(ready.at[(NZ - z) & (NZ - 1)], 1)
                send_to(0)

    brecv[z] = bsend[slot]

    @pl.when(jnp.logical_and(b_last, z == 0))
    def _():
        pl.semaphore_wait(hready.at[1], 1)
        to_before.start()

    @pl.when(part_after)
    def _():
        pl.semaphore_wait(rowhere, 1)
        to_after.start()

    @pl.when(part_before)
    def _():
        pl.semaphore_wait(rowhere, 1)
        to_before.start()

    pl.when(has_before)(to_after.wait_recv)
    pl.when(has_after)(to_before.wait_recv)
    lane = iota((64, 256), 1)
    left = jnp.sum(jnp.where(jnp.logical_and(eye, has_before), hrecv[0], 0.0), axis=1, keepdims=True)
    right = jnp.sum(jnp.where(jnp.logical_and(eye, has_after), hrecv[1], 0.0), axis=1, keepdims=True)
    left = jnp.where(lane == 0, left, pltpu.roll(field, 1, 1))
    right = jnp.where(lane == 255, right, pltpu.roll(field, 255, 1))
    pot[...] = field + 0.25 * (left - 2.0 * field + right)

    for k in weights:
        weights[k].wait_send()
    for d in OFFSETS:
        if d in FAR:
            @pl.when(jnp.logical_not(relayed))
            def _(d=d):
                for copy in out[d]:
                    copy.wait_send()
        else:
            for copy in out[d]:
                copy.wait_send()
        back[d].wait_send()

    @pl.when(relayed)
    def _():
        for copy in bundle:
            copy.wait_send()

    for b in range(2):
        @pl.when(present[b])
        def _(b=b):
            for i in range(len(FAR)):
                for copy in onward(b, i):
                    copy.wait_send()

    pl.when(has_after)(to_after.wait_send)
    pl.when(has_before)(to_before.wait_send)

    for d in OFFSETS:
        back[d].wait_recv()
    got = mm(brecv[...].reshape(256, 128), place[...], TN)
    out_ref[...] = pot[...] - (got[0:64, 0:256] + got[64:128, 256:512])


def body(potential, types, saturation, pattern, inverses, coupling, skin):
    dma = pltpu.SemaphoreType.DMA
    return pl.pallas_call(
        kernel,
        out_shape=jax.ShapeDtypeStruct((64, 256), F32),
        in_specs=[pl.BlockSpec(memory_space=pl.ANY)] * 7,
        out_specs=pl.BlockSpec(memory_space=pltpu.VMEM),
        scratch_shapes=[
            pltpu.VMEM((64, 256), F32),
            pltpu.VMEM((1, 256), jnp.int32),
            pltpu.VMEM((1, 256), jnp.int32),
            pltpu.VMEM((1, 256), jnp.int32),
            pltpu.VMEM((256, 64), BF16),
            pltpu.VMEM((64, 64), BF16),
            pltpu.SMEM((8,), F32),
            pltpu.VMEM((256, 512), BF16),
            pltpu.VMEM((128, 768), BF16),
            pltpu.VMEM((8, 192, 128), BF16),
            pltpu.VMEM((8, 256, 128), BF16),
            pltpu.VMEM((NZ, 16, 128), BF16),
            pltpu.VMEM((NZ + 1, 16, 128), BF16),
            pltpu.VMEM((NZ + 1, 16, 128), BF16),
            pltpu.VMEM((NZ, 16, 128), BF16),
            pltpu.VMEM((NZ, 1, 128), F32),
            pltpu.VMEM((NZ + 1, 1, 128), F32),
            pltpu.VMEM((2, 1, 128), F32),
            pltpu.VMEM((2, 1, 128), F32),
            pltpu.VMEM((2, len(FAR), 16, 128), BF16),
            pltpu.VMEM((2, len(FAR), 1, 128), F32),
            dma((7,)),
            pltpu.SemaphoreType.REGULAR((NZ,)),
            pltpu.SemaphoreType.REGULAR((8,)),
            pltpu.SemaphoreType.REGULAR((2,)),
            pltpu.SemaphoreType.REGULAR,
            pltpu.SemaphoreType.REGULAR,
            *[dma((NZ,)) for _ in range(6)],
            *[dma((8,)) for _ in range(2)],
            *[dma((2,)) for _ in range(3)],
            dma((4,)),
            *[dma((2 * len(FAR),)) for _ in range(2)],
        ],
        compiler_params=pltpu.CompilerParams(
            collective_id=0, has_side_effects=True, vmem_limit_bytes=32 * 1024 * 1024
        ),
        name="regroup_solve",
    )(
        *[
            pltpu.with_memory_space_constraint(array, pltpu.HBM)
            for array in (
                potential,
                types.reshape(1, 256),
                saturation.reshape(1, 256),
                pattern.reshape(1, 256),
                inverses.reshape(256, 64),
                coupling.reshape(64, 64),
                skin,
            )
        ]
    )


def solution(mesh):
    placed = (
        P(None, ("dom", "cell")),
        P(("dom", "cell"), None),
        P(("dom", "cell")),
        P(("dom", "cell")),
        P("dom", None, None, None),
        P("dom", None, None),
        P(),
    )
    return jax.shard_map(
        body, mesh=mesh, in_specs=placed, out_specs=P(None, ("dom", "cell")), check_vma=False
    )
```

```python
import functools

import jax
import jax.numpy as jnp
from jax import lax
from jax.experimental import pallas as pl
from jax.experimental.pallas import tpu as pltpu
from jax.sharding import PartitionSpec as P

MESH = pl.DeviceIdType.MESH
F32 = jnp.float32
BF16 = jnp.bfloat16
NY, NZ, NX = 4, 16, 4
NT = (((1,), (1,)), ((), ()))
TN = (((0,), (0,)), ((), ()))
NN = (((1,), (0,)), ((), ()))
GROUP, HALF = 4, NZ // 2
FAR = range(GROUP + 1, 2 * GROUP + 2)
OFFSETS = sorted(range(1, NZ), key=lambda d: min(d, NZ - d))


def mm(a, b, dims=NN):
    return lax.dot_general(a, b, dims, preferred_element_type=F32)


def iota(shape, axis):
    return lax.broadcasted_iota(jnp.int32, shape, axis)


def turn(x):
    return pltpu.roll(x, 64, 1)


def coefficients(skin):
    row, lane = iota((128, 128), 0), iota((128, 128), 1)
    place_in = row % 64
    bit, part, first = place_in % 13, place_in // 13, lane < 64

    def chosen(lower, upper):
        value = jnp.zeros((128, 128), F32)
        for i in range(13):
            a = skin[lower[i]] if i in lower else 0.0
            b = skin[upper[i]] if i in upper else 0.0
            value = jnp.where(bit == i, jnp.where(first, a, b), value)
        return value

    above, here = {i: i + 1 for i in range(7)}, {i: i for i in range(7)}
    above2, here2 = {7 + i: i + 2 for i in range(6)}, {7 + i: i for i in range(6)}
    value = jnp.concatenate([chosen(above, here), chosen(above2, above), chosen(here, here2)], axis=1)
    row, part = iota((128, 384), 0), (iota((128, 384), 0) % 64) // 13
    high = value.astype(BF16).astype(F32)
    rest = value - high
    middle = rest.astype(BF16).astype(F32)
    value = jnp.where(part == 0, high, jnp.where(part == 1, middle, jnp.where(part == 2, rest - middle, 0.0)))
    return jnp.concatenate([jnp.where(row // 64 == h, value, 0.0) for h in range(2)], axis=1).astype(BF16)


def product(a, c):
    low = iota((128, 128), 1) < 64
    a = a.astype(F32)
    levels = jnp.concatenate([jnp.where(low, a, 0.0), jnp.where(low, 0.0, a)], axis=0).astype(BF16)
    return mm(levels, jnp.concatenate([c, c], axis=0)).astype(BF16)


def natural(a, b):
    low = iota((128, 128), 1) < 64
    a, b = a.astype(F32), b.astype(F32)
    return jnp.concatenate([jnp.where(low, a, turn(b)), jnp.where(low, turn(a), b)], axis=0).astype(BF16)


def solve(points, codes, abuf, gbuf, table, total):
    n = codes.shape[0]
    rows = 16 * n
    row, lane = iota((rows, 128), 0), iota((rows, 128), 1)
    first = lane < 64
    pair = (row // 4) % 4
    spread = jnp.broadcast_to(codes.reshape(n, 1, 128), (n, 16, 128)).reshape(rows, 128)
    spread = jnp.where(lane % 64 == row % 16, spread, 0.0).astype(BF16)
    from_half, to = iota((128, 384), 0) // 64, iota((128, 384), 1)
    pick = (from_half == jnp.where(to < 256, to // 128, (to // 64) % 2)).astype(BF16)
    code = mm(spread, pick)
    bits = jnp.abs(code[:, 256:384]).astype(jnp.int32) - 1
    bit = (lane % 64) % 13
    mask = jnp.where(bit < 7, jnp.left_shift(1, bit), jnp.left_shift(3, jnp.maximum(bit - 7, 0)))
    held = jnp.logical_and(jnp.bitwise_and(bits, mask) == mask, lane % 64 < 39)
    factors = mm(held.astype(F32).astype(BF16), table)
    x = points.astype(F32)
    xr = turn(x)

    def by_pair(v):
        return jnp.concatenate([jnp.where(pair == p, v, 0.0).astype(BF16) for p in range(4)], axis=1)

    def doubled(v, lo):
        v = jnp.where(lo, v, 0.0)
        return v + turn(v)

    sides, ys, pqs, answers = [], [], [], []
    for h in range(2):
        c = code[:, h * 128 : (h + 1) * 128]
        sides.append((c < 0.0, (jnp.abs(c) > 128.0) != first))
        upper = sides[h][0]
        d2 = jnp.where(first, x, xr) if h == 0 else jnp.where(first, xr, x)
        own = jnp.concatenate(
            [jnp.where(pair == 2 * q + lane // 64, d2, 0.0).astype(BF16) for q in range(2)], axis=1
        )
        got = mm(own, jnp.concatenate([abuf[2 * h], abuf[2 * h + 1]], axis=1), NT)
        ys.append(doubled(jnp.where(upper, got[:, 128:256], got[:, 0:128]), sides[h][1]))

    def coupled(v, h):
        return mm(v, jnp.concatenate([gbuf[h * 4 + p] for p in range(4)], axis=1), NT)

    for h in range(2):
        upper, lo = sides[h]
        y = ys[h]
        both = jnp.concatenate([by_pair(jnp.where(first, y, 0.0)), by_pair(jnp.where(first, 0.0, y))], axis=0)
        got = coupled(both, h)
        pqs.append([doubled(jnp.where(upper, g[:, 128:256], g[:, 0:128]), lo) for g in (got[:rows], got[rows:])])
    for h in range(2):
        upper, lo = sides[h]
        f = [factors[:, h * 384 + i * 128 : h * 384 + (i + 1) * 128] for i in range(3)]
        mixed = f[0] * ys[h] - f[1] * pqs[h][0] - f[2] * pqs[h][1]
        got = coupled(by_pair(mixed), h)
        rest = doubled(jnp.where(upper, got[:, 128:256], got[:, 0:128]), lo)
        answers.append((total * ys[h] - rest) * 0.125)
    return jnp.where(first, answers[0], answers[1]).astype(BF16)


def kernel(
    pot_hbm, types_hbm, sat_hbm, pat_hbm, inv_hbm, cpl_hbm, skin_hbm, out_ref,
    pot, typ, sat, pat, inv, cpl, skin, place, table, wbuf, gbuf, abuf, send, recv, bsend, brecv, csend, crecv, hsend, hrecv, rbuf, crbuf,
    load_sem, ready, wready, hready, allhere, rowhere, ps, pr, cs, cr, bs, br, ws, wr, hs, hr, bds, bdr, fs, cfs,
):
    dom, x = lax.axis_index("dom"), lax.axis_index("cell")
    c, z, y = dom & 1, (dom >> 1) & (NZ - 1), dom >> 5

    def at(yy, zz, cc):
        return ((yy * NZ + zz) * 2 + cc, x)

    ahead = {d: (z + d) & (NZ - 1) for d in OFFSETS}
    behind = {d: (z - d) & (NZ - 1) for d in OFFSETS}
    zpeer = {d: at(y, ahead[d], c) for d in OFFSETS}
    special = jnp.logical_and(x == 0, jnp.logical_and(y == 0, c == 0))
    shift = special.astype(jnp.int32)

    def turn_of(zz):
        return jnp.where(jnp.logical_and(special, zz == 0), NZ, jnp.minimum(zz, HALF))

    def slot_of(zz):
        return jnp.where(jnp.logical_and(special, zz == 0), HALF, zz + (zz >= HALF) * 1)

    zback = {d: at(y, behind[d], c) for d in OFFSETS}
    mine, slot = turn_of(z), slot_of(z)
    n_behind = jnp.where(mine == NZ, NZ - 1 - GROUP, mine - shift)
    middle = jnp.logical_and(z >= HALF, z < HALF + GROUP)
    early, late, lone = mine < HALF, mine == HALF, mine == NZ
    wpeer, later = {}, {}
    for k in range(1, 4):
        yy = (y - k) & (NY - 1)
        wpeer[k] = at(yy, z, c)
        later[k] = yy > y
    wpeer[4] = at(y, z, 1 - c)
    later[4] = c == 1
    index = dom * NX + x
    after = ((index + 1) >> 2, (index + 1) & (NX - 1))
    before = ((index - 1) >> 2, (index - 1) & (NX - 1))
    has_after, has_before = index < 2 * NY * NZ * NX - 1, index > 0

    ahead_next = jnp.logical_or(x < NX - 1, jnp.logical_and(c == 1, z < NZ - 1))
    behind_next = jnp.logical_or(x > 0, jnp.logical_and(c == 0, z > 0))
    part_after = jnp.logical_and(jnp.logical_and(x == NX - 1, c == 1), jnp.logical_and(z > 0, z < NZ - 1))
    part_before = jnp.logical_and(jnp.logical_and(x == 0, c == 0), z > 1)
    tells_after = jnp.logical_and(jnp.logical_and(x == NX - 1, c == 1), z == 0)
    tells_before = jnp.logical_and(jnp.logical_and(x == 0, c == 0), z == 1)
    i_first = jnp.logical_and(has_after, jnp.logical_and(ahead_next, jnp.logical_not(part_after)))
    i_last = jnp.logical_and(has_after, jnp.logical_not(ahead_next))
    b_first = jnp.logical_and(has_before, jnp.logical_and(behind_next, jnp.logical_not(part_before)))
    b_last = jnp.logical_and(has_before, jnp.logical_not(behind_next))
    relayed = mine < GROUP
    relays = jnp.logical_and(jnp.logical_and(z >= GROUP, z < 2 * GROUP), turn_of(z - GROUP) < GROUP)

    barrier = pltpu.get_barrier_semaphore()
    @pl.when(early)
    def _():
        for j in range(1, NZ):
            @pl.when(z < j)
            def _(j=j):
                pl.semaphore_signal(barrier, inc=1, device_id=at(y, j, c), device_id_type=MESH)

    @pl.when(jnp.logical_and(jnp.logical_and(special, z > 0), jnp.logical_not(middle)))
    def _():
        pl.semaphore_signal(barrier, inc=1, device_id=at(y, 0, c), device_id_type=MESH)

    for k in (1, 3, 4):
        @pl.when(later[k])
        def _(k=k):
            pl.semaphore_signal(barrier, inc=1, device_id=wpeer[k], device_id_type=MESH)

    @pl.when(i_first)
    def _():
        pl.semaphore_signal(barrier, inc=1, device_id=after, device_id_type=MESH)

    @pl.when(b_last)
    def _():
        pl.semaphore_signal(barrier, inc=1, device_id=before, device_id_type=MESH)

    loads = [
        pltpu.make_async_copy(src, dst, load_sem.at[i])
        for i, (src, dst) in enumerate([
            (types_hbm, typ), (sat_hbm, sat), (pat_hbm, pat), (pot_hbm, pot), (inv_hbm, inv), (cpl_hbm, cpl),
            (skin_hbm, skin),
        ])
    ]
    for load in loads:
        load.start()
    n_earlier = jnp.minimum(y, 1) + y // 3 + 1 - c + n_behind + b_first.astype(jnp.int32) + i_last.astype(jnp.int32)

    @pl.when(n_earlier > 0)
    def _():
        pl.semaphore_wait(barrier, n_earlier)

    near_lone = (*range(1, HALF), *range(HALF + GROUP, NZ))
    precedes = {j: jnp.logical_and(z > 0, jnp.logical_not(special)) if j == 0 else z > j for j in range(HALF)}
    for j in range(HALF):
        @pl.when(precedes[j])
        def _(j=j):
            pl.semaphore_signal(ready.at[(z - j) & (NZ - 1)], inc=1, device_id=at(y, j, c), device_id_type=MESH)

    @pl.when(lone)
    def _():
        for j in near_lone:
            pl.semaphore_signal(ready.at[NZ - j], inc=1, device_id=at(y, j, c), device_id_type=MESH)

    for k in (1, 3, 4):
        @pl.when(jnp.logical_not(later[k]))
        def _(k=k):
            at_peer = k if k == 4 else 4 - k
            pl.semaphore_signal(wready.at[at_peer], inc=1, device_id=wpeer[k], device_id_type=MESH)

    @pl.when(i_last)
    def _():
        pl.semaphore_signal(hready.at[1], inc=1, device_id=after, device_id_type=MESH)

    @pl.when(b_first)
    def _():
        pl.semaphore_signal(hready.at[0], inc=1, device_id=before, device_id_type=MESH)

    loads[4].wait()
    loads[5].wait()
    w = inv[...]
    wbuf[0, 0:128, :] = jnp.concatenate([w[0:128].astype(F32), w[128:256].astype(F32)], axis=1).astype(BF16)
    block = cpl[...].astype(F32)
    wbuf[0, 128:192, :] = jnp.concatenate([block, block.T], axis=1).astype(BF16)
    weights = {
        k: pltpu.make_async_remote_copy(
            wbuf.at[max(k - 4, 0)], wbuf.at[k], ws.at[k], wr.at[k], device_id=wpeer[min(k, 4)], device_id_type=MESH
        )
        for k in range(1, 8)
    }
    for want in (False, True):
        for k in (3, 1, 4):
            if want and k == 4:
                continue

            @pl.when(later[k] == want)
            def _(k=k, want=want):
                if want:
                    pl.semaphore_wait(wready.at[k], 1)
                weights[k].start()

    @pl.when(jnp.logical_and(y > 0, later[3]))
    def _():
        for k in (3, 1):
            pl.semaphore_signal(wready.at[2], inc=1, device_id=wpeer[k], device_id_type=MESH)

    for i in (0, 1, 2, 3, 6):
        loads[i].wait()

    field = pot[...]
    t = typ[...]
    onehot = (iota((128, 256), 0) == t).astype(BF16)
    earlier = (iota((256, 256), 0) < iota((256, 256), 1)).astype(BF16)
    rank = jnp.sum(onehot.astype(F32) * mm(onehot, earlier), axis=0, keepdims=True).astype(jnp.int32)
    t_y, t_z, t_c = t // (2 * NZ), (t // 2) % NZ, t % 2
    row = t_z * 16 + ((t_y - y + NY) % NY) * 4 + rank
    side = (t_c - c + 2) % 2
    both = jnp.concatenate([jnp.where(side == 0, row, -1), jnp.where(side == 1, row, -1)], axis=1)
    place[...] = (iota((256, 512), 0) == both).astype(BF16)
    level, bits = sat[...], pat[...]
    code = (1 + (level % 2) * 128 + bits) * jnp.where(level >= 2, -1, 1)
    code = jnp.broadcast_to(code.astype(F32), (64, 256)).astype(BF16)
    drive = field.astype(BF16)
    none = jnp.zeros((64, 256), BF16)
    spread = jnp.concatenate(
        [jnp.concatenate([a, none], axis=1) if i == 0 else jnp.concatenate([none, a], axis=1)
         for a in (drive, code) for i in range(2)], axis=0
    )
    placed = mm(place[...], spread, NT)
    keep = iota((NZ, 16, 128), 2) % 64 == iota((NZ, 16, 128), 1)
    send[...] = placed[:, 0:128].astype(BF16).reshape(NZ, 16, 128)
    csend[...] = jnp.sum(jnp.where(keep, placed[:, 128:256].reshape(NZ, 16, 128), 0.0), axis=1, keepdims=True)

    out, back, backin = {}, {}, {}
    for d in OFFSETS:
        out[d] = [
            pltpu.make_async_remote_copy(
                csend.at[ahead[d]], crecv.at[slot], cs.at[d], cr.at[d], device_id=zpeer[d], device_id_type=MESH
            ),
            pltpu.make_async_remote_copy(
                send.at[ahead[d]], recv.at[slot], ps.at[d], pr.at[d], device_id=zpeer[d], device_id_type=MESH
            ),
        ]
        back[d] = pltpu.make_async_remote_copy(
            bsend.at[slot_of(behind[d])], brecv.at[z], bs.at[d], br.at[d], device_id=zback[d], device_id_type=MESH
        )
    def send_to(j):
        d = (j - z) & (NZ - 1)
        for src, dst, ss, rs in ((csend, crecv, cs, cr), (send, recv, ps, pr)):
            pltpu.make_async_remote_copy(
                src.at[j], dst.at[slot], ss.at[d], rs.at[d], device_id=at(y, j, c), device_id_type=MESH
            ).start()

    for j in range(HALF):
        pl.when(precedes[j])(functools.partial(send_to, j))

    @pl.when(lone)
    def _():
        for j in near_lone:
            send_to(j)


    eye = iota((64, 128), 0) == iota((64, 128), 1)
    hsend[0] = jnp.sum(jnp.where(eye, field[:, 255:256], 0.0), axis=0, keepdims=True)
    hsend[1] = jnp.sum(jnp.where(eye, field[:, 0:1], 0.0), axis=0, keepdims=True)
    to_after = pltpu.make_async_remote_copy(
        hsend.at[0], hrecv.at[0], hs.at[0], hr.at[0], device_id=after, device_id_type=MESH
    )
    to_before = pltpu.make_async_remote_copy(
        hsend.at[1], hrecv.at[1], hs.at[1], hr.at[1], device_id=before, device_id_type=MESH
    )

    pl.semaphore_wait(wready.at[2], 1)
    weights[2].start()
    pl.when(i_last)(to_after.start)
    pl.when(b_first)(to_before.start)

    span = pl.ds(lax.rem(z + FAR[0], NZ - len(FAR) + 1), len(FAR))
    bundle = [
        pltpu.make_async_remote_copy(
            src.at[span], dst, bds.at[i], bdr.at[i], device_id=zpeer[GROUP], device_id_type=MESH
        )
        for i, (src, dst) in enumerate([(csend, crbuf), (send, rbuf)])
    ]
    from_slot = slot_of(jnp.maximum(z - GROUP, 0))
    onward = {}
    for j in range(1, len(FAR) + 1):
        onward[j] = [
            pltpu.make_async_remote_copy(
                src.at[j - 1], dst.at[from_slot], ss.at[j - 1], rs.at[j + GROUP],
                device_id=zpeer[j], device_id_type=MESH,
            )
            for src, dst, ss, rs in ((crbuf, crecv, cfs, cr), (rbuf, recv, fs, pr))
        ]

    def send_on(d):
        @pl.when(jnp.logical_and(z + d < NZ, jnp.logical_not(relayed)) if d in FAR else z + d < NZ)
        def _():
            pl.semaphore_wait(ready.at[d], 1)
            for copy in out[d]:
                copy.start()

    @pl.when(early)
    def _():
        for d in (*range(1, GROUP + 2), *range(NZ - 1, FAR[-1], -1), *range(FAR[-1], GROUP + 1, -1)):
            send_on(d)
            if d == GROUP:
                @pl.when(relayed)
                def _():
                    for copy in bundle:
                        copy.start()

            if d in onward:
                @pl.when(relays)
                def _(d=d):
                    if d == 1:
                        for copy in bundle:
                            copy.wait_recv()
                    for copy in onward[d]:
                        copy.start()

    @pl.when(relayed)
    def _():
        for d in FAR:
            pl.semaphore_wait(ready.at[d], 1)

    def tell(when, at_offset, told):
        @pl.when(when)
        def _():
            @pl.when(special)
            def _():
                pl.semaphore_wait(ready.at[at_offset], 1)
                for copy in out[at_offset]:
                    copy.start()

            if told[0] != 1:
                @pl.when(special)
                def _():
                    pl.semaphore_signal(allhere, inc=1, device_id=zpeer[at_offset], device_id_type=MESH)

            for d in told:
                pl.semaphore_signal(allhere, inc=1, device_id=zpeer[d], device_id_type=MESH)

    tell(z == HALF - 1, HALF + 1, range(1, GROUP + 1))
    tell(z == 1, NZ - 1, range(NZ - 2, NZ - 2 - GROUP, -1))

    @pl.when(lone)
    def _():
        pl.semaphore_wait(allhere, 1)
        for j in range(HALF, HALF + GROUP):
            send_to(j)


    @pl.when(later[4])
    def _():
        pl.semaphore_wait(wready.at[4], 1)
        weights[4].start()

    empty = jnp.where(special, 0, HALF)
    recv[empty] = jnp.zeros((16, 128), BF16)
    crecv[empty] = jnp.zeros((1, 128), F32)
    recv[slot] = send[z]
    crecv[slot] = csend[z]

    @pl.when(i_first)
    def _():
        pl.semaphore_wait(hready.at[0], 1)
        to_after.start()

    @pl.when(jnp.logical_and(b_last, z > 0))
    def _():
        pl.semaphore_wait(hready.at[1], 1)
        to_before.start()

    @pl.when(tells_after)
    def _():
        pl.semaphore_signal(rowhere, inc=1, device_id=after, device_id_type=MESH)

    @pl.when(tells_before)
    def _():
        pl.semaphore_signal(rowhere, inc=1, device_id=before, device_id_type=MESH)

    table[...] = coefficients(skin)
    total = skin[0]
    for k in range(1, 8):
        total = total + skin[k]

    gbuf[0] = product(wbuf[0, 0:128, :], wbuf[0, 128:192, :])
    for k in (1, 3, 2):
        weights[k].wait_recv()
        weights[k + 4].start()
    for ks in ((1, 3, 2), (4, 5, 7, 6)):
        for k in ks:
            if k >= 4:
                weights[k].wait_recv()
        for k in ks:
            gbuf[k] = product(wbuf[k, 0:128, :], wbuf[k, 128:192, :])
        for q in range(2):
            k = 0 if 1 in ks else 4
            abuf[k // 2 + q] = natural(wbuf[k + 2 * q, 0:128, :], wbuf[k + 2 * q + 1, 0:128, :])

    spreads = table[...]
    for start, stop in ((0, GROUP), (GROUP, HALF + 1), (HALF + 1, NZ + 1)):
        sources = [j for j in range(NZ) if start <= j + (j >= HALF) < stop] + ([0] if start == GROUP else [])
        apply = {j: (special if start == GROUP else jnp.logical_not(special)) if j == 0 else True for j in sources}
        for j in reversed(sources):
            @pl.when(jnp.logical_and(z != j, apply[j]))
            def _(j=j):
                d = (z - j) & (NZ - 1)
                for src, dst, ss, rs in ((csend, crecv, cs, cr), (send, recv, ps, pr)):
                    pltpu.make_async_remote_copy(
                        src.at[j], dst.at[j], ss.at[d], rs.at[d], device_id=at(y, j, c), device_id_type=MESH
                    ).wait_recv()

        n = stop - start
        answer = solve(
            recv[start:stop].reshape(n * 16, 128), crecv[start:stop].reshape(n, 128), abuf, gbuf, spreads, total
        )
        bsend[start:stop] = answer.reshape(n, 16, 128)
        for j in sources:
            @pl.when(jnp.logical_and(z != j, apply[j]))
            def _(j=j):
                d = (z - j) & (NZ - 1)
                pltpu.make_async_remote_copy(
                    bsend.at[slot_of(j)], brecv.at[z], bs.at[d], br.at[d], device_id=at(y, j, c), device_id_type=MESH
                ).start()

        if start == 0:
            @pl.when(late)
            def _():
                pl.semaphore_wait(allhere, 1)
                for j in range(HALF, NZ):
                    pl.when(z != j)(functools.partial(send_to, j))

                @pl.when(jnp.logical_and(special, middle))
                def _():
                    send_to(0)

            @pl.when(jnp.logical_or(tells_after, tells_before))
            def _():
                pl.semaphore_wait(rowhere, 1)
                for d in range(1, NZ - 1):
                    pl.semaphore_signal(rowhere, inc=1, device_id=zpeer[d], device_id_type=MESH)

            others = jnp.logical_and(jnp.logical_and(z > 1, z != HALF - 1), jnp.logical_not(middle))

            @pl.when(jnp.logical_and(special, others))
            def _():
                pl.semaphore_wait(ready.at[(NZ - z) & (NZ - 1)], 1)
                send_to(0)

    brecv[z] = bsend[slot]

    @pl.when(jnp.logical_and(b_last, z == 0))
    def _():
        pl.semaphore_wait(hready.at[1], 1)
        to_before.start()

    @pl.when(part_after)
    def _():
        pl.semaphore_wait(rowhere, 1)
        to_after.start()

    @pl.when(part_before)
    def _():
        pl.semaphore_wait(rowhere, 1)
        to_before.start()

    pl.when(has_before)(to_after.wait_recv)
    pl.when(has_after)(to_before.wait_recv)
    lane = iota((64, 256), 1)
    left = jnp.sum(jnp.where(jnp.logical_and(eye, has_before), hrecv[0], 0.0), axis=1, keepdims=True)
    right = jnp.sum(jnp.where(jnp.logical_and(eye, has_after), hrecv[1], 0.0), axis=1, keepdims=True)
    left = jnp.where(lane == 0, left, pltpu.roll(field, 1, 1))
    right = jnp.where(lane == 255, right, pltpu.roll(field, 255, 1))
    pot[...] = field + 0.25 * (left - 2.0 * field + right)

    for k in weights:
        weights[k].wait_send()
    for d in OFFSETS:
        if d in FAR:
            @pl.when(jnp.logical_not(relayed))
            def _(d=d):
                for copy in out[d]:
                    copy.wait_send()
        else:
            for copy in out[d]:
                copy.wait_send()
        back[d].wait_send()

    @pl.when(relayed)
    def _():
        for copy in bundle:
            copy.wait_send()

    @pl.when(relays)
    def _():
        for j in onward:
            for copy in onward[j]:
                copy.wait_send()

    pl.when(has_after)(to_after.wait_send)
    pl.when(has_before)(to_before.wait_send)

    for d in OFFSETS:
        back[d].wait_recv()
    got = mm(brecv[...].reshape(256, 128), place[...], TN)
    out_ref[...] = pot[...] - (got[0:64, 0:256] + got[64:128, 256:512])


def body(potential, types, saturation, pattern, inverses, coupling, skin):
    dma = pltpu.SemaphoreType.DMA
    return pl.pallas_call(
        kernel,
        out_shape=jax.ShapeDtypeStruct((64, 256), F32),
        in_specs=[pl.BlockSpec(memory_space=pl.ANY)] * 7,
        out_specs=pl.BlockSpec(memory_space=pltpu.VMEM),
        scratch_shapes=[
            pltpu.VMEM((64, 256), F32),
            pltpu.VMEM((1, 256), jnp.int32),
            pltpu.VMEM((1, 256), jnp.int32),
            pltpu.VMEM((1, 256), jnp.int32),
            pltpu.VMEM((256, 64), BF16),
            pltpu.VMEM((64, 64), BF16),
            pltpu.SMEM((8,), F32),
            pltpu.VMEM((256, 512), BF16),
            pltpu.VMEM((128, 768), BF16),
            pltpu.VMEM((8, 192, 128), BF16),
            pltpu.VMEM((8, 256, 128), BF16),
            pltpu.VMEM((4, 256, 128), BF16),
            pltpu.VMEM((NZ, 16, 128), BF16),
            pltpu.VMEM((NZ + 1, 16, 128), BF16),
            pltpu.VMEM((NZ + 1, 16, 128), BF16),
            pltpu.VMEM((NZ, 16, 128), BF16),
            pltpu.VMEM((NZ, 1, 128), F32),
            pltpu.VMEM((NZ + 1, 1, 128), F32),
            pltpu.VMEM((2, 1, 128), F32),
            pltpu.VMEM((2, 1, 128), F32),
            pltpu.VMEM((len(FAR), 16, 128), BF16),
            pltpu.VMEM((len(FAR), 1, 128), F32),
            dma((7,)),
            pltpu.SemaphoreType.REGULAR((NZ,)),
            pltpu.SemaphoreType.REGULAR((8,)),
            pltpu.SemaphoreType.REGULAR((2,)),
            pltpu.SemaphoreType.REGULAR,
            pltpu.SemaphoreType.REGULAR,
            *[dma((NZ,)) for _ in range(6)],
            *[dma((8,)) for _ in range(2)],
            *[dma((2,)) for _ in range(4)],
            *[dma((len(FAR),)) for _ in range(2)],
        ],
        compiler_params=pltpu.CompilerParams(
            collective_id=0, has_side_effects=True, vmem_limit_bytes=32 * 1024 * 1024
        ),
        name="regroup_solve",
    )(
        *[
            pltpu.with_memory_space_constraint(array, pltpu.HBM)
            for array in (
                potential,
                types.reshape(1, 256),
                saturation.reshape(1, 256),
                pattern.reshape(1, 256),
                inverses.reshape(256, 64),
                coupling.reshape(64, 64),
                skin,
            )
        ]
    )


def solution(mesh):
    placed = (
        P(None, ("dom", "cell")),
        P(("dom", "cell"), None),
        P(("dom", "cell")),
        P(("dom", "cell")),
        P("dom", None, None, None),
        P("dom", None, None),
        P(),
    )
    return jax.shard_map(
        body, mesh=mesh, in_specs=placed, out_specs=P(None, ("dom", "cell")), check_vma=False
    )
```
